256 devices in a mesh: ctx: 64 (over y, z, x_lo), head: 4 (over x_hi, core).
Axes of the slice: x: 4 (x_hi: 2, x_lo: 2; x = x_hi * 2 + x_lo), y: 4, z: 8, core: 2. Of those that a mesh axis runs over, the one named last changes fastest.
Arguments:
- queries: bfloat16 [8192, 64, 576], P('ctx', 'head'), may hold values from -22 to 22
- latent_kv: bfloat16 [8192, 576], P('ctx'), may hold values from -22 to 22
- positions: int32 [8192], P('ctx'), may hold values from 0 to 896, as said below
- value_up: bfloat16 [512, 64, 128], P(None, 'head'), may hold values from -0.25 to 0.25
- cotangent: bfloat16 [8192, 64, 128], P('ctx', 'head'), may hold values from -6 to 6
Outputs:
- attn_out: bfloat16 [8192, 64, 128], P('ctx', 'head')
- grad_queries: bfloat16 [8192, 64, 576], P('ctx', 'head')
- grad_latent: bfloat16 [8192, 576], P('ctx')
- grad_value_up: float32 [512, 64, 128], P('ctx', 'head')
The draws below stay inside these ranges and needn't reach their ends.
Inputs may be any that keep to these rules, and one draw needn't show every extreme that they name: `positions`: positions count up by one inside a document and are 0 where a document begins; no document holds more than 897 tokens, and some document holds exactly 897.
All inputs are finite; a program needn't handle non-finite values.
Results may differ from the reference program's by a relative error of at most 0.02.
The reference program's roundings to bfloat16 on the way count: a program that leaves them out, or rounds other values in their place, can miss the bound.
Values may be sent and summed in bfloat16 or wider, within the bound.
A program may use at most 320 MiB of HBM per device.

```python
import math
import jax
import jax.numpy as jnp
from jax import lax

D_C = 512
D_R = 64
D_V = 128
D_NOPE = 128
HEADS = 64
TOK_DEV = 128
REACH = 8
TOKENS = 8192
DOC_MAX = 897


def draw_queries(key, part):
    key = jax.random.fold_in(key, 11)
    latent_key, rope_key = jax.random.split(key)
    latent_part = 0.5 * jax.random.truncated_normal(latent_key, -6.0, 6.0, (TOKENS, HEADS, D_C), jnp.float32)
    rope_part = jax.random.truncated_normal(rope_key, -6.0, 6.0, (TOKENS, HEADS, D_R), jnp.float32)
    return jnp.concatenate([latent_part, rope_part], axis=-1).astype(jnp.bfloat16)


def draw_latent_kv(key, part):
    key = jax.random.fold_in(key, 23)
    values = jax.random.truncated_normal(key, -6.0, 6.0, (TOKENS, D_C + D_R), jnp.float32)
    return values.astype(jnp.bfloat16)


def draw_positions(key, part):
    key = jax.random.fold_in(key, 7)
    start_key, coin_key = jax.random.split(key)
    row_index = jnp.arange(TOKENS, dtype=jnp.int32)
    long_start = jax.random.randint(start_key, (), 0, TOKENS - DOC_MAX + 1).astype(jnp.int32)
    coin_draw = jax.random.randint(coin_key, (TOKENS,), 0, 2 * TOK_DEV) == 0
    inside = (row_index >= long_start) & (row_index < long_start + DOC_MAX)
    begins = (row_index == 0) | (jnp.mod(row_index - long_start, DOC_MAX) == 0) | coin_draw & jnp.logical_not(inside)
    last_begin = lax.cummax(jnp.where(begins, row_index, 0), axis=0)
    return (row_index - last_begin).astype(jnp.int32)


def block_levels(stream_key, shape, pieces, low, top_value):
    factor_of, own = 1.0, jax.random.fold_in(stream_key, 6)
    for position, parts in pieces:
        steps = jnp.exp(jax.random.uniform(jax.random.fold_in(own, position), (parts,), jnp.float32, low / len(pieces), top_value / len(pieces)))
        factor_of = factor_of * jnp.repeat(steps, shape[position] // parts).reshape([-1 if axis == position else 1 for axis in range(len(shape))])
    return factor_of


def gaussian(own_key, extent, scale, limit, cuts=(), kind=jnp.bfloat16):
    gain = block_levels(own_key, extent, cuts, -0.22, 0.18) if cuts else 1.0
    values = jax.random.normal(own_key, extent, jnp.float32) * scale * gain
    return jnp.minimum(jnp.maximum(values, -limit), limit).astype(kind)


def setup_inputs(seed: int = 0) -> dict:
    streams_of = jax.random.split(jax.random.key(seed), 6)
    queries = draw_queries(jax.random.fold_in(streams_of[5], 71), 0)
    latent_kv = draw_latent_kv(jax.random.fold_in(streams_of[5], 71), 0)
    positions = draw_positions(jax.random.fold_in(streams_of[5], 71), 0)
    value_up = gaussian(streams_of[3], (D_C, HEADS, D_V), D_C ** -0.5, 0.25, ((1, 4),))
    cotangent = gaussian(streams_of[4], (TOKENS, HEADS, D_V), 1.0, 6.0, ((0, 64), (1, 4)))
    return dict(queries=queries, latent_kv=latent_kv, positions=positions, value_up=value_up, cotangent=cotangent)


ROPE_BASE = 10000.0

def rope_tables(positions):
    half_dim = D_R // 2
    frequency = ROPE_BASE ** (-2.0 * jnp.arange(half_dim, dtype=jnp.float32) / D_R)
    angles = positions.astype(jnp.float32)[:, None] * frequency[None, :]
    return (jnp.cos(angles), jnp.sin(angles))

def rotate(vectors, cosine_table, sine_table):
    half_dim = vectors.shape[-1] // 2
    lower_half = vectors[..., :half_dim]
    upper_half = vectors[..., half_dim:]
    return jnp.concatenate([lower_half * cosine_table - upper_half * sine_table, upper_half * cosine_table + lower_half * sine_table], axis=-1)

def unrotate(gradients, cosine_table, sine_table):
    half_dim = gradients.shape[-1] // 2
    lower_half = gradients[..., :half_dim]
    upper_half = gradients[..., half_dim:]
    return jnp.concatenate([lower_half * cosine_table + upper_half * sine_table, upper_half * cosine_table - lower_half * sine_table], axis=-1)

def reference(queries, latent_kv, positions, value_up, cotangent):
    softmax_scale = 1.0 / math.sqrt(D_NOPE + D_R)
    kv_width = D_C + D_R
    cosine_table, sine_table = rope_tables(positions)
    q_rope = rotate(queries[:, :, D_C:].astype(jnp.float32), cosine_table[:, None, :], sine_table[:, None, :]).astype(jnp.bfloat16)
    q_cat = jnp.concatenate([queries[:, :, :D_C], q_rope], axis=-1)
    k_rope = rotate(latent_kv[:, D_C:].astype(jnp.float32), cosine_table, sine_table).astype(jnp.bfloat16)
    k_cat = jnp.concatenate([latent_kv[:, :D_C], k_rope], axis=-1)
    window_rows = REACH * TOK_DEV
    pad_rows = window_rows - TOK_DEV
    token_index = jnp.arange(TOKENS, dtype=jnp.int32)
    begins = token_index - positions
    k_padded = jnp.concatenate([jnp.zeros((pad_rows, kv_width), jnp.bfloat16), k_cat], axis=0)
    begin_padded = jnp.concatenate([jnp.full((pad_rows,), -1, jnp.int32), begins], axis=0)
    up_heads = jnp.swapaxes(value_up, 0, 1)
    block_offsets = jnp.arange(TOK_DEV, dtype=jnp.int32)
    window_offsets = jnp.arange(window_rows, dtype=jnp.int32)

    def one_block(carry, block):
        grad_acc, up_acc = carry
        first_row = (block * TOK_DEV).astype(jnp.int32)
        q_blk = lax.dynamic_slice_in_dim(q_cat, first_row, TOK_DEV, 0)
        cot_blk = lax.dynamic_slice_in_dim(cotangent, first_row, TOK_DEV, 0)
        cos_blk = lax.dynamic_slice_in_dim(cosine_table, first_row, TOK_DEV, 0)
        sin_blk = lax.dynamic_slice_in_dim(sine_table, first_row, TOK_DEV, 0)
        q_begin = lax.dynamic_slice_in_dim(begins, first_row, TOK_DEV, 0)
        k_win = lax.dynamic_slice_in_dim(k_padded, first_row, window_rows, 0)
        b_win = lax.dynamic_slice_in_dim(begin_padded, first_row, window_rows, 0)
        q_index = first_row + block_offsets
        k_index = first_row - pad_rows + window_offsets
        visible = (k_index[None, :] >= 0) & (k_index[None, :] <= q_index[:, None]) & (b_win[None, :] == q_begin[:, None])
        k_latent = k_win[:, :D_C]

        def one_head(summed, head_items):
            q_head, cot_head, up_head = head_items
            scores = jnp.dot(q_head, k_win.T, preferred_element_type=jnp.float32) * softmax_scale
            scores = jnp.where(visible, scores, -jnp.inf)
            row_peak = lax.optimization_barrier(jnp.max(scores, axis=1, keepdims=True))
            log_total = row_peak + jnp.log(lax.optimization_barrier(jnp.sum(jnp.exp(scores - row_peak), axis=1, keepdims=True)))
            prob_tile = jnp.exp(scores - log_total).astype(jnp.bfloat16)
            o_lat = jnp.dot(prob_tile, k_latent, preferred_element_type=jnp.float32).astype(jnp.bfloat16)
            out_head = jnp.dot(o_lat, up_head, preferred_element_type=jnp.float32).astype(jnp.bfloat16)
            do_lat = jnp.dot(cot_head, up_head.T, preferred_element_type=jnp.float32).astype(jnp.bfloat16)
            d_probs = jnp.dot(do_lat, k_latent.T, preferred_element_type=jnp.float32)
            prob_values = prob_tile.astype(jnp.float32)
            row_delta = lax.optimization_barrier(jnp.sum(prob_values * d_probs, axis=1, keepdims=True))
            d_scores = (prob_values * (d_probs - row_delta) * softmax_scale).astype(jnp.bfloat16)
            dq_cat = jnp.dot(d_scores, k_win, preferred_element_type=jnp.float32)
            dk_cat = jnp.dot(d_scores.T, q_head, preferred_element_type=jnp.float32)
            dv_lat = jnp.dot(prob_tile.T, do_lat, preferred_element_type=jnp.float32)
            summed = summed + jnp.concatenate([dk_cat[:, :D_C] + dv_lat, dk_cat[:, D_C:]], axis=1)
            dq_out = jnp.concatenate([dq_cat[:, :D_C], unrotate(dq_cat[:, D_C:], cos_blk, sin_blk)], axis=1).astype(jnp.bfloat16)
            d_up = jnp.dot(o_lat.T, cot_head, preferred_element_type=jnp.float32)
            return (summed, (out_head, dq_out, d_up))
        start_grad = jnp.zeros((window_rows, kv_width), jnp.float32)
        summed, (head_outs, dq_outs, d_ups) = lax.scan(one_head, start_grad, (jnp.swapaxes(q_blk, 0, 1), jnp.swapaxes(cot_blk, 0, 1), up_heads))
        current = lax.dynamic_slice_in_dim(grad_acc, first_row, window_rows, 0)
        grad_acc = lax.dynamic_update_slice_in_dim(grad_acc, current + summed, first_row, 0)
        up_acc = up_acc + d_ups
        return ((grad_acc, up_acc), (head_outs, dq_outs))
    start_acc = jnp.zeros((TOKENS + pad_rows, kv_width), jnp.float32)
    start_up = jnp.zeros((HEADS, D_C, D_V), jnp.float32)
    block_ids = jnp.arange(TOKENS // TOK_DEV, dtype=jnp.int32)
    (grad_acc, up_acc), (head_outs, dq_outs) = lax.scan(one_block, (start_acc, start_up), block_ids)
    summed_all = grad_acc[pad_rows:]
    grad_latent = jnp.concatenate([summed_all[:, :D_C], unrotate(summed_all[:, D_C:], cosine_table, sine_table)], axis=1).astype(jnp.bfloat16)
    attn_out = jnp.swapaxes(head_outs, 1, 2).reshape(TOKENS, HEADS, D_V)
    grad_queries = jnp.swapaxes(dq_outs, 1, 2).reshape(TOKENS, HEADS, kv_width)
    grad_value_up = jnp.swapaxes(up_acc, 0, 1)
    return (attn_out, grad_queries, grad_latent, grad_value_up)
```

```python
import math

import jax
import jax.numpy as jnp
import numpy as np
from jax import lax
from jax.experimental import pallas as pl
from jax.experimental.pallas import tpu as pltpu
from jax.sharding import PartitionSpec as P

F32, BF16 = jnp.float32, jnp.bfloat16
MESH = pl.DeviceIdType.MESH
SCALE = 1.0 / math.sqrt(192.0)
LOG2E = 1.4426950408889634
FREQUENCY = [
    float(f) for f in np.asarray(10000.0 ** (-2.0 * np.arange(32, dtype=np.float32) / 64), np.float32)
]


def dot(a, b):
    return jnp.dot(a, b, preferred_element_type=F32)


def dot_nt(a, b):
    return lax.dot_general(a, b, (((1,), (1,)), ((), ())), preferred_element_type=F32)


def swap_halves(x):
    lane = lax.broadcasted_iota(jnp.int32, x.shape, 1)
    return jnp.where(lane < 32, pltpu.roll(x, 96, 1), pltpu.roll(x, 32, 1))


def widened(x):
    return jnp.concatenate([x, jnp.zeros_like(x)], axis=1)


def kernel(
    q_hbm, lat_hbm, pos_ref, vup_hbm, cot_hbm,
    attn_hbm, gq_hbm, gl_hbm, gv_hbm,
    q_raw, lat_raw, vup_raw, cot_raw, tab, sbuf, dpbuf, q_hm, q_t, do_hm, do_t, vup_h, cot_h,
    p_buf, ds_buf, bias, ao, kw, k_t,
    dup_s, rx, ry, xs, rxy, ys, ryx, zs, rz, gv,
    dks, drow, zsend, zrecv, glt, gl,
    in_sem, out_sem, kz_s, kz_r, kr_s, kr_r,
    rx_s, rx_r, ry_s, ry_r, rxy_s, rxy_r, ryx_s, ryx_r, rz_s, rz_r,
    dr_s, dr_r, dz_s, dz_r, gl_s, gl_r,
):
    ctx, head = lax.axis_index("ctx"), lax.axis_index("head")
    a, row = ctx % 2, ctx // 2
    y, z = ctx // 16, (ctx // 2) % 8
    me = a * 4 + head
    partner = ctx + 1 - 2 * a

    def mate(t):
        m = (me + t) % 8
        return m, m // 4, m % 4

    def rcopy(src, dst, ss, rs, to_ctx, to_head):
        return pltpu.make_async_remote_copy(
            src_ref=src, dst_ref=dst, send_sem=ss, recv_sem=rs,
            device_id=(to_ctx, to_head), device_id_type=MESH,
        )

    in_copies = [
        pltpu.make_async_copy(src, dst, in_sem.at[i])
        for i, (src, dst) in enumerate(
            ((lat_hbm, lat_raw), (vup_hbm, vup_raw), (cot_hbm, cot_raw), (q_hbm, q_raw))
        )
    ]
    for c in in_copies:
        c.start()

    partners = []
    for t in range(1, 8):
        m, a2, h2 = mate(t)
        partners.append((row * 2 + a2, h2))
    for d in (1, 2, 3, 4):
        partners.append(((ctx + 2 * d) % 64, head))
        partners.append(((ctx + 64 - 2 * d) % 64, head))
    partners.append(((ctx + 64 - 7 + 14 * a) % 64, head))
    for t in range(1, 4):
        partners.append((((y + t) % 4) * 16 + ctx % 16, head))
    for t in range(1, 8):
        partners.append((y * 16 + ((z + t) % 8) * 2 + a, head))
    barrier = pltpu.get_barrier_semaphore()
    for c, h in partners:
        pl.semaphore_signal(barrier, inc=1, device_id=(c, h), device_id_type=MESH)

    lane = lax.broadcasted_iota(jnp.int32, (128, 128), 1)
    freq_row = jnp.zeros((8, 128), F32)
    lane8 = lax.broadcasted_iota(jnp.int32, (8, 128), 1) % 32
    for i in range(32):
        freq_row = jnp.where(lane8 == i, FREQUENCY[i], freq_row)
    pos_col = jnp.broadcast_to(pos_ref[...].astype(F32), (128, 128)).T
    angle = pos_col * freq_row[:1]
    sine = jnp.where(lane < 32, -jnp.sin(angle), jnp.sin(angle))
    tab[0] = jnp.where(lane < 64, jnp.cos(angle), 0.0)
    tab[1] = jnp.where(lane < 64, sine, 0.0)

    in_copies[0].wait()
    own = 7 * 128
    kw[own:own + 128, :512] = lat_raw[:, :512]
    k_rope = widened(lat_raw[:, 512:].astype(F32))
    k_rope = k_rope * tab[0] + swap_halves(k_rope) * tab[1]
    kw[own:own + 128, 512:] = k_rope[:, :64].astype(BF16)

    pl.semaphore_wait(barrier, len(partners))

    def krows(slot, h):
        return kw.at[pl.ds(pl.multiple_of(slot * 128 + h * 32, 32), 32)]

    def kz(d):
        to = (ctx + (2 * d if d < 4 else 7)) % 64
        return rcopy(krows(7, head), krows(7 - 2 * d if d < 4 else 0, head), kz_s.at[d], kz_r.at[d], to, head)

    def kfwd(d, t):
        m, a2, h2 = mate(t)
        return rcopy(
            krows(7 - 2 * d, head), krows(7 - (2 * d + a2 - a), head),
            kr_s.at[d, t], kr_r.at[d, me], row * 2 + a2, h2,
        )

    def kgot(d, t):
        m, a2, h2 = mate(t)
        ref = krows(7 - (2 * d + a - a2), h2)
        return rcopy(ref, ref, kr_s.at[d, t], kr_r.at[d, m], row * 2 + a2, h2)

    def kfirst(h2):
        return rcopy(krows(7, head), krows(6, head), kr_s.at[0, h2], kr_r.at[0, head], row * 2 + 1, h2)

    def kfirst_got(h2):
        return rcopy(krows(6, h2), krows(6, h2), kr_s.at[0, h2], kr_r.at[0, h2], row * 2, h2)

    def klast(t):
        return rcopy(krows(0, head), krows(0, head), kr_s.at[4, t], kr_r.at[4, head], row * 2, (head + t) % 4)

    def klast_got(t):
        h2 = (head + t) % 4
        return rcopy(krows(0, h2), krows(0, h2), kr_s.at[4, t], kr_r.at[4, h2], row * 2, h2)

    for d in (1, 2, 3):
        kz(d).start()

    @pl.when(a == 1)
    def _():
        kz(4).start()

    @pl.when(a == 0)
    def _():
        for h2 in range(4):
            kfirst(h2).start()

    def forward(d):
        kz(d).wait_recv()
        for t in range(1, 8):
            kfwd(d, t).start()

    def vup_in(i, c):
        v = vup_raw[pl.ds(i * 8, 8)].astype(F32).reshape(128, 128)
        sbuf[i // 16, pl.ds((i % 16) * 128, 128), :] = v
        return c

    def cot_in(i, c):
        sbuf[4, pl.ds(i * 128, 128), :] = cot_raw[pl.ds(i * 8, 8)].astype(F32).reshape(128, 128)
        return c

    def q_in(i, c):
        for j in range(5):
            w = 128 if j < 4 else 64
            x = q_raw[pl.ds(i * 8, 8), :, j * 128:j * 128 + w].astype(F32).reshape(128, w)
            dpbuf[j, pl.ds(i * 128, 128), :] = x if w == 128 else widened(x)
        return c

    def head_up(h, c):
        rows = pl.ds(h * 128, 128)
        for cc in range(4):
            vup_h[h, cc * 128:(cc + 1) * 128, :] = sbuf[cc, pl.ds(h, 128, stride=16), :].astype(BF16)
        cot = sbuf[4, pl.ds(h, 128, stride=16), :].astype(BF16)
        cot_h[h] = cot
        v = vup_h[h]
        do_hm[rows, :] = dot_nt(cot, v).astype(BF16)
        do_t[:, rows] = dot_nt(v, cot).astype(BF16)
        return c

    def head_q(h, c):
        rows = pl.ds(h * 128, 128)
        for j in range(4):
            x = dpbuf[j, pl.ds(h, 128, stride=16), :].astype(BF16)
            q_hm[rows, j * 128:(j + 1) * 128] = x
            q_t[j * 128:(j + 1) * 128, rows] = x.T
        x = dpbuf[4, pl.ds(h, 128, stride=16), :]
        x = (x * tab[0] + swap_halves(x) * tab[1]).astype(BF16)
        q_hm[rows, 512:576] = x[:, :64]
        q_t[512:576, rows] = x.T[:64]
        return c

    in_copies[1].wait()
    lax.fori_loop(0, 64, vup_in, 0)
    in_copies[2].wait()
    lax.fori_loop(0, 16, cot_in, 0)
    forward(1)
    lax.fori_loop(0, 16, head_up, 0)
    forward(2)
    in_copies[3].wait()
    lax.fori_loop(0, 16, q_in, 0)
    forward(3)
    lax.fori_loop(0, 16, head_q, 0)

    @pl.when(a == 0)
    def _():
        kz(4).wait_recv()
        for t in range(1, 4):
            klast(t).start()

    q_idx = lax.broadcasted_iota(jnp.int32, (128, 128), 0)
    pos_row = pos_col.astype(jnp.int32)
    for w in range(8):
        back = 896 - w * 128 + q_idx - lane
        bias[:, w * 128:(w + 1) * 128] = jnp.where((back >= 0) & (back <= pos_row), 0.0, -jnp.inf)

    def score_group(g):
        cols = slice(g * 256, g * 256 + 256)
        for w in (2 * g, 2 * g + 1):
            k_t[:, w * 128:(w + 1) * 128] = kw[w * 128:(w + 1) * 128, :].T

        def qk(r, c):
            rows = pl.ds(r * 512, 512)
            s = dot(q_hm[rows, :], k_t[:, cols])
            sbuf[2 * g, rows, :] = s[:, :128]
            sbuf[2 * g + 1, rows, :] = s[:, 128:]
            s = dot(do_hm[rows, :], k_t[:512, cols])
            dpbuf[2 * g, rows, :] = s[:, :128]
            dpbuf[2 * g + 1, rows, :] = s[:, 128:]
            return c

        lax.fori_loop(0, 4, qk, 0)

    def arrived(d):
        for t in range(1, 8):
            kgot(d, t).wait_recv()

    @pl.when(a == 1)
    def _():
        for h2 in range(4):
            kfirst_got(h2).wait_recv()

    arrived(1)
    score_group(3)
    arrived(2)
    score_group(2)
    arrived(3)
    score_group(1)

    @pl.when(a == 0)
    def _():
        for t in range(1, 4):
            klast_got(t).wait_recv()

    score_group(0)

    def x_copy(hg):
        return rcopy(dup_s.at[pl.ds(4 * hg, 2), 1 - a], rx.at[hg], rx_s.at[hg], rx_r.at[hg], partner, head)

    def y_to(t):
        return ((y + t) % 4) * 16 + ctx % 16

    def y_copy(hg, t):
        y2 = (y + t) % 4
        return rcopy(
            dup_s.at[pl.ds(4 * hg + 2, 2), :, pl.ds(pl.multiple_of(64 * y2, 64), 64)], ry.at[hg, t - 1],
            ry_s.at[hg, t - 1], ry_r.at[hg, t - 1], y_to(t), head,
        )

    def xy_copy(hg, t):
        y2 = (y + t) % 4
        return rcopy(
            xs.at[hg, :, pl.ds(pl.multiple_of(64 * y2, 64), 64)], rxy.at[hg, t - 1],
            rxy_s.at[hg, t - 1], rxy_r.at[hg, t - 1], y_to(t), head,
        )

    def yx_copy(hg):
        return rcopy(ys.at[hg, :, 1 - a], ryx.at[hg], ryx_s.at[hg], ryx_r.at[hg], partner, head)

    def z_copy(hg, t):
        z2 = (z + t) % 8
        rows = pl.ds(pl.multiple_of(32 * hg, 32), 32)
        return rcopy(
            zs.at[z2, rows], rz.at[t - 1, rows], rz_s.at[hg, t - 1], rz_r.at[hg, t - 1],
            y * 16 + z2 * 2 + a, head,
        )

    own_y = pl.ds(pl.multiple_of(64 * y, 64), 64)

    def up_second(hg):
        x_copy(hg).wait_recv()
        for j in range(2):
            xs[hg, j] = dup_s[4 * hg + j, a].astype(F32) + rx[hg, j].astype(F32)
        for t in range(1, 4):
            xy_copy(hg, t).start()
        for t in range(1, 4):
            y_copy(hg, t).wait_recv()
        for j in range(2):
            for half in range(2):
                total = dup_s[4 * hg + 2 + j, half, own_y, :].astype(F32)
                for t in range(3):
                    total = total + ry[hg, t, j, half].astype(F32)
                ys[hg, j, half] = total
        yx_copy(hg).start()

    def up_third(hg):
        for t in range(1, 4):
            xy_copy(hg, t).wait_recv()
        yx_copy(hg).wait_recv()
        for j in range(2):
            total = xs[hg, j, own_y, :]
            for t in range(3):
                total = total + rxy[hg, t, j]
            zs[:, pl.ds(pl.multiple_of((4 * hg + j) * 8, 8), 8), :] = total.reshape(8, 8, 128)
            total = ys[hg, j, a] + ryx[hg, j]
            zs[:, pl.ds(pl.multiple_of((4 * hg + 2 + j) * 8, 8), 8), :] = total.reshape(8, 8, 128)
        for t in range(1, 8):
            z_copy(hg, t).start()

    def up_last(hg):
        for t in range(1, 8):
            z_copy(hg, t).wait_recv()
        rows = pl.ds(pl.multiple_of(32 * hg, 32), 32)
        total = zs[z, rows, :]
        for t in range(7):
            total = total + rz[t, rows, :]
        for j in range(4):
            gv[pl.ds(4 * hg + j, 8, stride=16), :] = total[8 * j:8 * j + 8]

    def group(hg, c):
        def soft(r, c2):
            q0 = pl.multiple_of((r % 4) * 32, 32)
            rows = pl.ds(pl.multiple_of(hg * 512 + r * 32, 32), 32)
            s = [sbuf[w, rows, :] + bias[pl.ds(q0, 32), w * 128:(w + 1) * 128] for w in range(8)]
            m = s[0]
            for w in range(1, 8):
                m = jnp.maximum(m, s[w])
            m = jnp.max(m, axis=1, keepdims=True)
            e = [jnp.exp2((x - m) * (SCALE * LOG2E)) for x in s]
            mass = e[0]
            for w in range(1, 8):
                mass = mass + e[w]
            inverse = 1.0 / jnp.sum(mass, axis=1, keepdims=True)
            p = [(x * inverse).astype(BF16) for x in e]
            delta = jnp.zeros((32, 128), F32)
            for w in range(8):
                p_buf[rows, w * 128:(w + 1) * 128] = p[w]
                delta = delta + p[w].astype(F32) * dpbuf[w, rows, :]
            delta = jnp.sum(delta, axis=1, keepdims=True)
            for w in range(8):
                ds = p[w].astype(F32) * (dpbuf[w, rows, :] - delta) * SCALE
                ds_buf[rows, w * 128:(w + 1) * 128] = ds.astype(BF16)
            return c2

        lax.fori_loop(0, 16, soft, 0)
        rows = pl.ds(pl.multiple_of(hg * 512, 512), 512)
        o = dot(p_buf[rows, :], kw[:, :512]).astype(BF16)
        for j in range(4):
            h = hg * 4 + j
            oh = o[j * 128:(j + 1) * 128]
            ao[pl.ds(h, 128, stride=16), :] = dot(oh, vup_h[h])
            up = dot(oh.T, cot_h[h]).reshape(32, 2, 8, 128)
            for half in range(2):
                dup_s[h, half] = up[:, half].reshape(256, 128).astype(BF16)
        x_copy(hg).start()
        for t in range(1, 4):
            y_copy(hg, t).start()

        @pl.when(hg >= 1)
        def _():
            up_second(hg - 1)

        @pl.when(hg >= 2)
        def _():
            up_third(hg - 2)

        return c

    lax.fori_loop(0, 4, group, 0)

    def quarter(slot, j):
        return dks.at[slot, pl.ds(pl.multiple_of(144 * j, 16), 144)]

    def dr_copy(d, t):
        m, a2, h2 = mate(t)
        return rcopy(
            quarter(7 - (2 * d + a - a2), h2), drow.at[d, me], dr_s.at[d, t], dr_r.at[d, me], row * 2 + a2, h2
        )

    def dr_got(d, t):
        m, a2, h2 = mate(t)
        return rcopy(drow.at[d, m], drow.at[d, m], dr_s.at[d, t], dr_r.at[d, m], row * 2 + a2, h2)

    def dr_last(h2):
        return rcopy(quarter(0, h2), drow.at[4, head], dr_s.at[4, h2], dr_r.at[4, head], row * 2 + 1, h2)

    def dr_last_got(h2):
        return rcopy(drow.at[4, h2], drow.at[4, h2], dr_s.at[4, h2], dr_r.at[4, h2], row * 2, h2)

    def dz_copy(d):
        return rcopy(zsend.at[d], zrecv.at[d], dz_s.at[d], dz_r.at[d], (ctx + 64 - 2 * d) % 64, head)

    def same_row(t):
        m, a2, h2 = mate(t)
        return a2 <= a

    def same_row_got(t):
        m, a2, h2 = mate(t)
        return a2 >= a

    def key_grads(g):
        cols = slice(g * 256, g * 256 + 256)
        x = dot(q_t[...], ds_buf[:, cols])
        v = dot(do_t[...], p_buf[:, cols])
        for i in range(2):
            part = slice(128 * i, 128 * i + 128)
            dks[2 * g + i, :512, :] = (x[:512, part] + v[:, part]).astype(BF16)
            dks[2 * g + i, 512:, :] = x[512:, part].astype(BF16)

    def row_sum(d):
        for t in range(1, 8):
            dr_got(d, t).wait_recv()
        total = quarter(7 - 2 * d, head)[...].astype(F32)
        for t in range(1, 8):
            total = total + drow[d, (me + t) % 8].astype(F32)
        zsend[d] = total.astype(BF16)
        dz_copy(d).start()

    @pl.when(a == 1)
    def _():
        drow[0, 0:4] = jnp.zeros((4, 144, 128), BF16)

    @pl.when(a == 0)
    def _():
        zrecv[4] = jnp.zeros((144, 128), BF16)

    key_grads(0)

    @pl.when(a == 0)
    def _():
        for h2 in range(4):
            dr_last(h2).start()

    up_second(3)
    up_third(2)
    key_grads(1)
    for t in range(1, 8):
        dr_copy(3, t).start()
    up_third(3)
    key_grads(2)
    for t in range(1, 8):
        dr_copy(2, t).start()
    row_sum(3)

    @pl.when(a == 1)
    def _():
        for h2 in range(4):
            dr_last_got(h2).wait_recv()
        total = drow[4, 0].astype(F32)
        for h2 in range(1, 4):
            total = total + drow[4, h2].astype(F32)
        zsend[4] = total.astype(BF16)
        dz_copy(4).start()

    key_grads(3)
    for t in range(1, 8):
        dr_copy(1, t).start()
    for t in range(1, 8):
        @pl.when(same_row(t))
        def _():
            dr_copy(0, t).start()
    row_sum(2)

    def dq(r, c):
        x = dot(ds_buf[pl.ds(pl.multiple_of(r * 512, 512), 512), :], kw[...])
        for j in range(4):
            h = r * 4 + j
            part = x[j * 128:(j + 1) * 128]
            for t in range(4):
                dpbuf[t, pl.ds(h, 128, stride=16), :] = part[:, t * 128:(t + 1) * 128]
            rope = widened(part[:, 512:])
            dpbuf[4, pl.ds(h, 128, stride=16), :] = rope * tab[0] - swap_halves(rope) * tab[1]
        return c

    lax.fori_loop(0, 2, dq, 0)
    row_sum(1)

    def last(hg, c):
        up_last(hg)
        return c

    lax.fori_loop(0, 4, last, 0)
    lax.fori_loop(2, 4, dq, 0)

    for t in range(1, 8):
        @pl.when(same_row_got(t))
        def _():
            dr_got(0, t).wait_recv()
    total = quarter(7, head)[...].astype(F32)
    for t in range(1, 8):
        total = total + drow[0, (me + t) % 8].astype(F32)
    for d in (1, 2, 3):
        dz_copy(d).wait_recv()

    @pl.when(a == 1)
    def _():
        dz_copy(4).wait_recv()

    for d in (1, 2, 3, 4):
        total = total + zrecv[d].astype(F32)
    roped = head == 3
    cosine = jnp.where(roped, tab[0].T[:32], 1.0)
    sine = jnp.where(roped, tab[1].T[32:64], 0.0)
    lower, upper = total[80:112], total[112:144]
    own_quarter = glt.at[pl.ds(pl.multiple_of(144 * head, 16), 144)]
    own_quarter[...] = jnp.concatenate(
        [total[:80], lower * cosine + upper * sine, upper * cosine - lower * sine], axis=0
    ).astype(BF16)

    def gl_copy(t):
        return rcopy(own_quarter, own_quarter, gl_s.at[t], gl_r.at[head], ctx, (head + t) % 4)

    def gl_got(t):
        h2 = (head + t) % 4
        ref = glt.at[pl.ds(pl.multiple_of(144 * h2, 16), 144)]
        return rcopy(ref, ref, gl_s.at[t], gl_r.at[h2], ctx, h2)

    for t in range(1, 4):
        gl_copy(t).start()

    def out16(i, c):
        toks = pl.ds(i * 8, 8)
        cot_raw[toks] = ao[pl.ds(i * 128, 128), :].reshape(8, 16, 128).astype(BF16)
        for j in range(5):
            w = 128 if j < 4 else 64
            part = dpbuf[j, pl.ds(i * 128, 128), :]
            q_raw[toks, :, j * 128:j * 128 + w] = part[:, :w].reshape(8, 16, w).astype(BF16)
        return c

    outs = [pltpu.make_async_copy(gv, gv_hbm, out_sem.at[0])]
    outs[0].start()
    for i in range(4):
        lax.fori_loop(4 * i, 4 * i + 4, out16, 0)
        toks = pl.ds(32 * i, 32)
        outs.append(pltpu.make_async_copy(q_raw.at[toks], gq_hbm.at[toks], out_sem.at[1 + i]))
        outs[-1].start()
    outs.append(pltpu.make_async_copy(cot_raw, attn_hbm, out_sem.at[5]))
    outs[-1].start()
    for t in range(1, 4):
        gl_got(t).wait_recv()
    gl[...] = glt[...].T
    outs.append(pltpu.make_async_copy(gl, gl_hbm, out_sem.at[6]))
    outs[-1].start()

    for d in (1, 2, 3):
        kz(d).wait_send()
        for t in range(1, 8):
            kfwd(d, t).wait_send()
            dr_copy(d, t).wait_send()
        dz_copy(d).wait_send()

    @pl.when(a == 1)
    def _():
        kz(4).wait_send()
        dz_copy(4).wait_send()

    @pl.when(a == 0)
    def _():
        for h2 in range(4):
            kfirst(h2).wait_send()
            dr_last(h2).wait_send()
        for t in range(1, 4):
            klast(t).wait_send()

    for t in range(1, 8):
        @pl.when(same_row(t))
        def _():
            dr_copy(0, t).wait_send()

    for t in range(1, 4):
        gl_copy(t).wait_send()

    def drained(hg, c):
        x_copy(hg).wait_send()
        yx_copy(hg).wait_send()
        for t in range(1, 4):
            y_copy(hg, t).wait_send()
            xy_copy(hg, t).wait_send()
        for t in range(1, 8):
            z_copy(hg, t).wait_send()
        return c

    lax.fori_loop(0, 4, drained, 0)
    for c in outs:
        c.wait()


def body(queries, latent_kv, positions, value_up, cotangent):
    anywhere = pl.BlockSpec(memory_space=pl.ANY)
    vmem, dma = pltpu.VMEM, pltpu.SemaphoreType.DMA
    attn, gq, gl, gv = pl.pallas_call(
        kernel,
        out_shape=(
            jax.ShapeDtypeStruct((128, 16, 128), BF16),
            jax.ShapeDtypeStruct((128, 16, 576), BF16),
            jax.ShapeDtypeStruct((128, 576), BF16),
            jax.ShapeDtypeStruct((128, 128), F32),
        ),
        in_specs=[anywhere, anywhere, pl.BlockSpec(memory_space=pltpu.VMEM), anywhere, anywhere],
        out_specs=(anywhere,) * 4,
        scratch_shapes=[
            vmem((128, 16, 576), BF16), vmem((128, 576), BF16), vmem((512, 16, 128), BF16),
            vmem((128, 16, 128), BF16), vmem((2, 128, 128), F32),
            vmem((8, 2048, 128), F32), vmem((8, 2048, 128), F32),
            vmem((2048, 576), BF16), vmem((576, 2048), BF16), vmem((2048, 512), BF16), vmem((512, 2048), BF16),
            vmem((16, 512, 128), BF16), vmem((16, 128, 128), BF16),
            vmem((2048, 1024), BF16), vmem((2048, 1024), BF16), vmem((128, 1024), F32), vmem((2048, 128), F32),
            vmem((1024, 576), BF16), vmem((576, 1024), BF16),
            vmem((16, 2, 256, 128), BF16), vmem((4, 2, 256, 128), BF16), vmem((4, 3, 2, 2, 64, 128), BF16),
            vmem((4, 2, 256, 128), F32), vmem((4, 3, 2, 64, 128), F32), vmem((4, 2, 2, 64, 128), F32),
            vmem((4, 2, 64, 128), F32), vmem((8, 128, 128), F32), vmem((7, 128, 128), F32), vmem((128, 128), F32),
            vmem((8, 576, 128), BF16), vmem((5, 8, 144, 128), BF16), vmem((5, 144, 128), BF16),
            vmem((5, 144, 128), BF16), vmem((576, 128), BF16), vmem((128, 576), BF16),
            dma((4,)), dma((7,)), dma((5,)), dma((5,)), dma((5, 8)), dma((5, 8)),
            dma((4,)), dma((4,)), dma((4, 3)), dma((4, 3)), dma((4, 3)), dma((4, 3)), dma((4,)), dma((4,)),
            dma((4, 7)), dma((4, 7)),
            dma((5, 8)), dma((5, 8)), dma((5,)), dma((5,)), dma((4,)), dma((4,)),
        ],
        compiler_params=pltpu.CompilerParams(
            collective_id=0, has_side_effects=True, vmem_limit_bytes=64 * 2**20 - 2**16
        ),
    )(queries, latent_kv, positions.reshape(1, 128), value_up, cotangent)
    return attn, gq, gl, gv.reshape(8, 16, 128)


def solution(mesh):
    in_specs = (
        P("ctx", "head", None),
        P("ctx", None),
        P("ctx"),
        P(None, "head", None),
        P("ctx", "head", None),
    )
    out_specs = (
        P("ctx", "head", None),
        P("ctx", "head", None),
        P("ctx", None),
        P("ctx", "head", None),
    )
    return jax.shard_map(body, mesh=mesh, in_specs=in_specs, out_specs=out_specs, check_vma=False)
```

```python
import math

import jax
import jax.numpy as jnp
import numpy as np
from jax import lax
from jax.experimental import pallas as pl
from jax.experimental.pallas import tpu as pltpu
from jax.sharding import PartitionSpec as P

F32, BF16 = jnp.float32, jnp.bfloat16
MESH = pl.DeviceIdType.MESH
SCALE = 1.0 / math.sqrt(192.0)
LOG2E = 1.4426950408889634
FREQUENCY = [
    float(f) for f in np.asarray(10000.0 ** (-2.0 * np.arange(32, dtype=np.float32) / 64), np.float32)
]


def dot(a, b):
    return jnp.dot(a, b, preferred_element_type=F32)


def dot_nt(a, b):
    return lax.dot_general(a, b, (((1,), (1,)), ((), ())), preferred_element_type=F32)


def kernel(
    q_hbm, lat_hbm, pos_ref, vup_hbm, cot_hbm,
    attn_hbm, gq_hbm, gl_hbm, gv_hbm,
    lat_raw, vup_raw, cot_raw, gq, tab, s_buf, dp_buf, q_t, do_t, vup_h, vup_t, cot_h,
    p_buf, ds_buf, bias, peak, ao, kw, k_t,
    dup_s, rx, ry, xs, rxy, ys, ryx, zs, rz, gv,
    dks, drow, zsend, zrecv, glt,
    in_sem, q_sem, out_sem, gq_sem, kz_s, kz_r, kr_s, kr_r,
    rx_s, rx_r, ry_s, ry_r, rxy_s, rxy_r, ryx_s, ryx_r, rz_s, rz_r,
    dr_s, dr_r, dz_s, dz_r, gl_s, gl_r,
):
    ctx, head = lax.axis_index("ctx"), lax.axis_index("head")
    a, row = ctx % 2, ctx // 2
    y, z = ctx // 16, (ctx // 2) % 8
    me = a * 4 + head
    partner = ctx + 1 - 2 * a

    def mate(t):
        m = (me + t) % 8
        return m, m // 4, m % 4

    def rcopy(src, dst, ss, rs, to_ctx, to_head):
        return pltpu.make_async_remote_copy(
            src_ref=src, dst_ref=dst, send_sem=ss, recv_sem=rs,
            device_id=(to_ctx, to_head), device_id_type=MESH,
        )

    in_copies = [
        pltpu.make_async_copy(src, dst, in_sem.at[i])
        for i, (src, dst) in enumerate(((lat_hbm, lat_raw), (vup_hbm, vup_raw), (cot_hbm, cot_raw)))
    ]
    for c in in_copies:
        c.start()

    def q_copy(h):
        cols = pl.ds(pl.multiple_of(h * 128, 128), 128)
        return pltpu.make_async_copy(q_hbm.at[h], q_t.at[:, cols], q_sem.at[h])

    for h in range(16):
        q_copy(h).start()

    partners = []
    for t in range(1, 8):
        m, a2, h2 = mate(t)
        partners.append((row * 2 + a2, h2))
    for d in (1, 2, 3, 4):
        partners.append(((ctx + 2 * d) % 64, head))
        partners.append(((ctx + 64 - 2 * d) % 64, head))
    partners.append(((ctx + 64 - 7 + 14 * a) % 64, head))
    for t in range(1, 4):
        partners.append((((y + t) % 4) * 16 + ctx % 16, head))
    for t in range(1, 8):
        partners.append((y * 16 + ((z + t) % 8) * 2 + a, head))
    barrier = pltpu.get_barrier_semaphore()
    for c, h in partners:
        pl.semaphore_signal(barrier, inc=1, device_id=(c, h), device_id_type=MESH)

    lane = lax.broadcasted_iota(jnp.int32, (128, 128), 1)
    sub = lax.broadcasted_iota(jnp.int32, (128, 128), 0)
    frequency = jnp.zeros((32, 128), F32)
    for i in range(32):
        frequency = jnp.where(sub[:32] == i, FREQUENCY[i], frequency)
    angle = pos_ref[...].astype(F32) * frequency
    tab[0] = jnp.cos(angle)
    tab[1] = jnp.sin(angle)

    in_copies[0].wait()
    own = 7 * 128
    k_t[:512, own:own + 128] = lat_raw[:512, :]
    lower, upper = lat_raw[512:544, :].astype(F32), lat_raw[544:576, :].astype(F32)
    k_t[512:544, own:own + 128] = (lower * tab[0] - upper * tab[1]).astype(BF16)
    k_t[544:576, own:own + 128] = (upper * tab[0] + lower * tab[1]).astype(BF16)
    kw[own:own + 128, :] = k_t[:, own:own + 128].T

    pl.semaphore_wait(barrier, len(partners))

    def krows(slot, h):
        return kw.at[pl.ds(pl.multiple_of(slot * 128 + h * 32, 32), 32)]

    def kz(d):
        to = (ctx + (2 * d if d < 4 else 7)) % 64
        return rcopy(krows(7, head), krows(7 - 2 * d if d < 4 else 0, head), kz_s.at[d], kz_r.at[d], to, head)

    def kfwd(d, t):
        m, a2, h2 = mate(t)
        return rcopy(
            krows(7 - 2 * d, head), krows(7 - (2 * d + a2 - a), head),
            kr_s.at[d, t], kr_r.at[d, me], row * 2 + a2, h2,
        )

    def kgot(d, t):
        m, a2, h2 = mate(t)
        ref = krows(7 - (2 * d + a - a2), h2)
        return rcopy(ref, ref, kr_s.at[d, t], kr_r.at[d, m], row * 2 + a2, h2)

    def kfirst(h2):
        return rcopy(krows(7, head), krows(6, head), kr_s.at[0, h2], kr_r.at[0, head], row * 2 + 1, h2)

    def kfirst_got(h2):
        return rcopy(krows(6, h2), krows(6, h2), kr_s.at[0, h2], kr_r.at[0, h2], row * 2, h2)

    def klast(t):
        return rcopy(krows(0, head), krows(0, head), kr_s.at[4, t], kr_r.at[4, head], row * 2, (head + t) % 4)

    def klast_got(t):
        h2 = (head + t) % 4
        return rcopy(krows(0, h2), krows(0, h2), kr_s.at[4, t], kr_r.at[4, h2], row * 2, h2)

    for d in (1, 2, 3):
        kz(d).start()

    @pl.when(a == 1)
    def _():
        kz(4).start()

    @pl.when(a == 0)
    def _():
        for h2 in range(4):
            kfirst(h2).start()

    def forward(d):
        kz(d).wait_recv()
        for t in range(1, 8):
            kfwd(d, t).start()

    def vup_in(i, c):
        v = vup_raw[pl.ds(i * 8, 8)].astype(F32).reshape(128, 128)
        s_buf[i // 8, pl.ds((i % 8) * 128, 128), :] = v
        return c

    def cot_in(i, c):
        s_buf[8 + i // 8, pl.ds((i % 8) * 128, 128), :] = cot_raw[pl.ds(i * 8, 8)].astype(F32).reshape(128, 128)
        return c

    def head_up(h, c):
        for cc in range(8):
            vup_h[h, cc * 64:(cc + 1) * 64, :] = s_buf[cc, pl.ds(h, 64, stride=16), :].astype(BF16)
        cot = jnp.concatenate(
            [s_buf[8, pl.ds(h, 64, stride=16), :], s_buf[9, pl.ds(h, 64, stride=16), :]], axis=0
        ).astype(BF16)
        cot_h[h] = cot
        v = vup_h[h]
        vup_t[h] = v.T
        do_t[:, pl.ds(pl.multiple_of(h * 128, 128), 128)] = dot(v, cot.T).astype(BF16)
        return c

    def head_q(h, c):
        q_copy(h).wait()
        cols = pl.ds(pl.multiple_of(h * 128, 128), 128)
        lower, upper = q_t[512:544, cols].astype(F32), q_t[544:576, cols].astype(F32)
        q_t[512:544, cols] = (lower * tab[0] - upper * tab[1]).astype(BF16)
        q_t[544:576, cols] = (upper * tab[0] + lower * tab[1]).astype(BF16)
        return c

    in_copies[1].wait()
    lax.fori_loop(0, 64, vup_in, 0)
    in_copies[2].wait()
    lax.fori_loop(0, 16, cot_in, 0)
    forward(1)
    lax.fori_loop(0, 8, head_up, 0)
    forward(2)
    lax.fori_loop(8, 16, head_up, 0)
    forward(3)
    lax.fori_loop(0, 16, head_q, 0)

    @pl.when(a == 0)
    def _():
        kz(4).wait_recv()
        for t in range(1, 4):
            klast(t).start()

    for w in range(8):
        back = 896 - w * 128 + lane - sub
        bias[w * 128:(w + 1) * 128, :] = jnp.where((back >= 0) & (back <= pos_ref[...]), 0.0, -jnp.inf)

    def score_group(g):
        rows = slice(g * 256, g * 256 + 256)

        def qk(r, c):
            cols = pl.ds(pl.multiple_of(r * 512, 512), 512)
            s = dot(kw[rows, :], q_t[:, cols])
            d = dot(kw[rows, :512], do_t[:, cols])
            for j in range(4):
                h = r * 4 + j
                x = s[:, j * 128:(j + 1) * 128] * (SCALE * LOG2E) + bias[rows, :]
                s_buf[h, rows, :] = x
                dp_buf[h, rows, :] = d[:, j * 128:(j + 1) * 128] * SCALE
                top = jnp.max(x.reshape(32, 8, 128), axis=0)
                peak[h] = top if g == 3 else jnp.maximum(peak[h], top)
            return c

        lax.fori_loop(0, 4, qk, 0)
        for w in (2 * g, 2 * g + 1):
            if w < 7:
                k_t[:, w * 128:(w + 1) * 128] = kw[w * 128:(w + 1) * 128, :].T

    def arrived(d):
        for t in range(1, 8):
            kgot(d, t).wait_recv()

    @pl.when(a == 1)
    def _():
        for h2 in range(4):
            kfirst_got(h2).wait_recv()

    arrived(1)
    score_group(3)
    arrived(2)
    score_group(2)
    arrived(3)
    score_group(1)

    @pl.when(a == 0)
    def _():
        for t in range(1, 4):
            klast_got(t).wait_recv()

    score_group(0)

    def x_copy(hg):
        return rcopy(dup_s.at[pl.ds(4 * hg, 2), 1 - a], rx.at[hg], rx_s.at[hg], rx_r.at[hg], partner, head)

    def y_to(t):
        return ((y + t) % 4) * 16 + ctx % 16

    def y_copy(hg, t):
        y2 = (y + t) % 4
        return rcopy(
            dup_s.at[pl.ds(4 * hg + 2, 2), :, pl.ds(pl.multiple_of(64 * y2, 64), 64)], ry.at[hg, t - 1],
            ry_s.at[hg, t - 1], ry_r.at[hg, t - 1], y_to(t), head,
        )

    def xy_copy(hg, t):
        y2 = (y + t) % 4
        return rcopy(
            xs.at[hg, :, pl.ds(pl.multiple_of(64 * y2, 64), 64)], rxy.at[hg, t - 1],
            rxy_s.at[hg, t - 1], rxy_r.at[hg, t - 1], y_to(t), head,
        )

    def yx_copy(hg):
        return rcopy(ys.at[hg, :, 1 - a], ryx.at[hg], ryx_s.at[hg], ryx_r.at[hg], partner, head)

    def z_copy(hg, t):
        z2 = (z + t) % 8
        rows = pl.ds(pl.multiple_of(32 * hg, 32), 32)
        return rcopy(
            zs.at[z2, rows], rz.at[t - 1, rows], rz_s.at[hg, t - 1], rz_r.at[hg, t - 1],
            y * 16 + z2 * 2 + a, head,
        )

    own_y = pl.ds(pl.multiple_of(64 * y, 64), 64)

    def up_second(hg):
        x_copy(hg).wait_recv()
        for j in range(2):
            xs[hg, j] = dup_s[4 * hg + j, a].astype(F32) + rx[hg, j].astype(F32)
        for t in range(1, 4):
            xy_copy(hg, t).start()
        for t in range(1, 4):
            y_copy(hg, t).wait_recv()
        for j in range(2):
            for half in range(2):
                total = dup_s[4 * hg + 2 + j, half, own_y, :].astype(F32)
                for t in range(3):
                    total = total + ry[hg, t, j, half].astype(F32)
                ys[hg, j, half] = total
        yx_copy(hg).start()

    def up_third(hg):
        for t in range(1, 4):
            xy_copy(hg, t).wait_recv()
        yx_copy(hg).wait_recv()
        for j in range(2):
            total = xs[hg, j, own_y, :]
            for t in range(3):
                total = total + rxy[hg, t, j]
            zs[:, pl.ds(pl.multiple_of((4 * hg + j) * 8, 8), 8), :] = total.reshape(8, 8, 128)
            total = ys[hg, j, a] + ryx[hg, j]
            zs[:, pl.ds(pl.multiple_of((4 * hg + 2 + j) * 8, 8), 8), :] = total.reshape(8, 8, 128)
        for t in range(1, 8):
            z_copy(hg, t).start()

    def up_last(hg):
        for t in range(1, 8):
            z_copy(hg, t).wait_recv()
        rows = pl.ds(pl.multiple_of(32 * hg, 32), 32)
        total = zs[z, rows, :]
        for t in range(7):
            total = total + rz[t, rows, :]
        for j in range(4):
            gv[pl.ds(4 * hg + j, 8, stride=16), :] = total[8 * j:8 * j + 8]

    def softmax(h, c):
        cols = pl.ds(pl.multiple_of(h * 128, 128), 128)
        top = jnp.max(peak[h], axis=0, keepdims=True)

        def folded(x):
            return jnp.sum(x.reshape(16, 8, 128), axis=0)

        def block(i):
            return pl.ds(pl.multiple_of(i * 128, 128), 128)

        def exps(i, mass):
            e = jnp.exp2(s_buf[h, block(i), :] - top)
            s_buf[h, block(i), :] = e
            return mass + folded(e)

        mass = lax.fori_loop(0, 8, exps, jnp.zeros((8, 128), F32), unroll=2)
        inverse = 1.0 / jnp.sum(mass, axis=0, keepdims=True)

        def probs(i, delta):
            p = (s_buf[h, block(i), :] * inverse).astype(BF16)
            p_buf[block(i), cols] = p
            return delta + folded(p.astype(F32) * dp_buf[h, block(i), :])

        delta = lax.fori_loop(0, 8, probs, jnp.zeros((8, 128), F32), unroll=2)
        delta = jnp.sum(delta, axis=0, keepdims=True)

        def score_grads(i, c2):
            p = p_buf[block(i), cols].astype(F32)
            ds_buf[block(i), cols] = (p * (dp_buf[h, block(i), :] - delta)).astype(BF16)
            return c2

        lax.fori_loop(0, 8, score_grads, 0, unroll=2)
        return c

    def group(hg, c):
        lax.fori_loop(4 * hg, 4 * hg + 4, softmax, 0)
        o = dot(k_t[:512, :], p_buf[:, pl.ds(pl.multiple_of(hg * 512, 512), 512)]).astype(BF16)
        for j in range(4):
            h = hg * 4 + j
            oh = o[:, j * 128:(j + 1) * 128]
            ao[pl.ds(h, 128, stride=16), :] = dot(vup_t[h], oh).T
            up = dot(oh, cot_h[h]).reshape(32, 2, 8, 128)
            for half in range(2):
                dup_s[h, half] = up[:, half].reshape(256, 128).astype(BF16)
        x_copy(hg).start()
        for t in range(1, 4):
            y_copy(hg, t).start()

        @pl.when(hg >= 1)
        def _():
            up_second(hg - 1)

        @pl.when(hg >= 2)
        def _():
            up_third(hg - 2)

        return c

    lax.fori_loop(0, 4, group, 0)

    def quarter(slot, j):
        return dks.at[slot, pl.ds(pl.multiple_of(144 * j, 16), 144)]

    def dr_copy(d, t):
        m, a2, h2 = mate(t)
        return rcopy(
            quarter(7 - (2 * d + a - a2), h2), drow.at[d, me], dr_s.at[d, t], dr_r.at[d, me], row * 2 + a2, h2
        )

    def dr_got(d, t):
        m, a2, h2 = mate(t)
        return rcopy(drow.at[d, m], drow.at[d, m], dr_s.at[d, t], dr_r.at[d, m], row * 2 + a2, h2)

    def dr_last(h2):
        return rcopy(quarter(0, h2), drow.at[4, head], dr_s.at[4, h2], dr_r.at[4, head], row * 2 + 1, h2)

    def dr_last_got(h2):
        return rcopy(drow.at[4, h2], drow.at[4, h2], dr_s.at[4, h2], dr_r.at[4, h2], row * 2, h2)

    def dz_copy(d):
        return rcopy(zsend.at[d], zrecv.at[d], dz_s.at[d], dz_r.at[d], (ctx + 64 - 2 * d) % 64, head)

    def same_row(t):
        m, a2, h2 = mate(t)
        return a2 <= a

    def same_row_got(t):
        m, a2, h2 = mate(t)
        return a2 >= a

    def key_grads(g):
        rows = slice(g * 256, g * 256 + 256)
        x = dot_nt(q_t[...], ds_buf[rows, :])
        v = dot_nt(do_t[...], p_buf[rows, :])
        for i in range(2):
            part = slice(128 * i, 128 * i + 128)
            dks[2 * g + i, :512, :] = (x[:512, part] + v[:, part]).astype(BF16)
            dks[2 * g + i, 512:, :] = x[512:, part].astype(BF16)

    def row_sum(d):
        for t in range(1, 8):
            dr_got(d, t).wait_recv()
        total = quarter(7 - 2 * d, head)[...].astype(F32)
        for t in range(1, 8):
            total = total + drow[d, (me + t) % 8].astype(F32)
        zsend[d] = total
        dz_copy(d).start()

    @pl.when(a == 1)
    def _():
        drow[0, 0:4] = jnp.zeros((4, 144, 128), BF16)

    @pl.when(a == 0)
    def _():
        zrecv[4] = jnp.zeros((144, 128), F32)

    key_grads(0)

    @pl.when(a == 0)
    def _():
        for h2 in range(4):
            dr_last(h2).start()

    up_second(3)
    up_third(2)
    key_grads(1)
    for t in range(1, 8):
        dr_copy(3, t).start()
    up_third(3)
    key_grads(2)
    for t in range(1, 8):
        dr_copy(2, t).start()
    row_sum(3)

    @pl.when(a == 1)
    def _():
        for h2 in range(4):
            dr_last_got(h2).wait_recv()
        total = drow[4, 0].astype(F32)
        for h2 in range(1, 4):
            total = total + drow[4, h2].astype(F32)
        zsend[4] = total
        dz_copy(4).start()

    key_grads(3)
    for t in range(1, 8):
        dr_copy(1, t).start()
    for t in range(1, 8):
        @pl.when(same_row(t))
        def _():
            dr_copy(0, t).start()
    row_sum(2)

    def gq_copy(h):
        return pltpu.make_async_copy(gq.at[h], gq_hbm.at[h], gq_sem.at[h])

    def dq(r, c):
        x = dot(k_t[...], ds_buf[:, pl.ds(pl.multiple_of(r * 512, 512), 512)])
        for j in range(4):
            h = r * 4 + j
            part = x[:, j * 128:(j + 1) * 128]
            lower, upper = part[512:544], part[544:576]
            gq[h, :512, :] = part[:512].astype(BF16)
            gq[h, 512:544, :] = (lower * tab[0] + upper * tab[1]).astype(BF16)
            gq[h, 544:576, :] = (upper * tab[0] - lower * tab[1]).astype(BF16)
            gq_copy(h).start()
        return c

    def attn16(i, c):
        cot_raw[pl.ds(i * 8, 8)] = ao[pl.ds(i * 128, 128), :].reshape(8, 16, 128).astype(BF16)
        return c

    lax.fori_loop(0, 16, attn16, 0)
    outs = [pltpu.make_async_copy(cot_raw, attn_hbm, out_sem.at[0])]
    outs[0].start()
    lax.fori_loop(0, 2, dq, 0)
    row_sum(1)

    def last(hg, c):
        up_last(hg)
        return c

    lax.fori_loop(0, 4, last, 0)
    outs.append(pltpu.make_async_copy(gv, gv_hbm, out_sem.at[1]))
    outs[-1].start()
    lax.fori_loop(2, 4, dq, 0)

    for t in range(1, 8):
        @pl.when(same_row_got(t))
        def _():
            dr_got(0, t).wait_recv()
    total = quarter(7, head)[...].astype(F32)
    for t in range(1, 8):
        total = total + drow[0, (me + t) % 8].astype(F32)
    for d in (1, 2, 3):
        dz_copy(d).wait_recv()

    @pl.when(a == 1)
    def _():
        dz_copy(4).wait_recv()

    for d in (1, 2, 3, 4):
        total = total + zrecv[d]
    roped = head == 3
    cosine = jnp.where(roped, tab[0], 1.0)
    sine = jnp.where(roped, tab[1], 0.0)
    lower, upper = total[80:112], total[112:144]
    own_quarter = glt.at[pl.ds(pl.multiple_of(144 * head, 16), 144)]
    own_quarter[...] = jnp.concatenate(
        [total[:80], lower * cosine + upper * sine, upper * cosine - lower * sine], axis=0
    ).astype(BF16)

    def gl_copy(t):
        return rcopy(own_quarter, own_quarter, gl_s.at[t], gl_r.at[head], ctx, (head + t) % 4)

    def gl_got(t):
        h2 = (head + t) % 4
        ref = glt.at[pl.ds(pl.multiple_of(144 * h2, 16), 144)]
        return rcopy(ref, ref, gl_s.at[t], gl_r.at[h2], ctx, h2)

    for t in range(1, 4):
        gl_copy(t).start()

    for t in range(1, 4):
        gl_got(t).wait_recv()
    outs.append(pltpu.make_async_copy(glt, gl_hbm, out_sem.at[2]))
    outs[-1].start()

    for d in (1, 2, 3):
        kz(d).wait_send()
        for t in range(1, 8):
            kfwd(d, t).wait_send()
            dr_copy(d, t).wait_send()
        dz_copy(d).wait_send()

    @pl.when(a == 1)
    def _():
        kz(4).wait_send()
        dz_copy(4).wait_send()

    @pl.when(a == 0)
    def _():
        for h2 in range(4):
            kfirst(h2).wait_send()
            dr_last(h2).wait_send()
        for t in range(1, 4):
            klast(t).wait_send()

    for t in range(1, 8):
        @pl.when(same_row(t))
        def _():
            dr_copy(0, t).wait_send()

    for t in range(1, 4):
        gl_copy(t).wait_send()

    def drained(hg, c):
        x_copy(hg).wait_send()
        yx_copy(hg).wait_send()
        for t in range(1, 4):
            y_copy(hg, t).wait_send()
            xy_copy(hg, t).wait_send()
        for t in range(1, 8):
            z_copy(hg, t).wait_send()
        return c

    lax.fori_loop(0, 4, drained, 0)
    for c in outs:
        c.wait()
    for h in range(16):
        gq_copy(h).wait()


def body(queries, latent_kv, positions, value_up, cotangent):
    anywhere = pl.BlockSpec(memory_space=pl.ANY)
    vmem, dma = pltpu.VMEM, pltpu.SemaphoreType.DMA
    attn, gq, gl, gv = pl.pallas_call(
        kernel,
        out_shape=(
            jax.ShapeDtypeStruct((128, 16, 128), BF16),
            jax.ShapeDtypeStruct((16, 576, 128), BF16),
            jax.ShapeDtypeStruct((576, 128), BF16),
            jax.ShapeDtypeStruct((128, 128), F32),
        ),
        in_specs=[anywhere, anywhere, pl.BlockSpec(memory_space=pltpu.VMEM), anywhere, anywhere],
        out_specs=(anywhere,) * 4,
        scratch_shapes=[
            vmem((576, 128), BF16), vmem((512, 16, 128), BF16), vmem((128, 16, 128), BF16),
            vmem((16, 576, 128), BF16), vmem((2, 32, 128), F32),
            vmem((16, 1024, 128), F32), vmem((16, 1024, 128), F32),
            vmem((576, 2048), BF16), vmem((512, 2048), BF16),
            vmem((16, 512, 128), BF16), vmem((16, 128, 512), BF16), vmem((16, 128, 128), BF16),
            vmem((1024, 2048), BF16), vmem((1024, 2048), BF16), vmem((1024, 128), F32), vmem((16, 8, 128), F32),
            vmem((2048, 128), F32), vmem((1024, 576), BF16), vmem((576, 1024), BF16),
            vmem((16, 2, 256, 128), BF16), vmem((4, 2, 256, 128), BF16), vmem((4, 3, 2, 2, 64, 128), BF16),
            vmem((4, 2, 256, 128), F32), vmem((4, 3, 2, 64, 128), F32), vmem((4, 2, 2, 64, 128), F32),
            vmem((4, 2, 64, 128), F32), vmem((8, 128, 128), F32), vmem((7, 128, 128), F32), vmem((128, 128), F32),
            vmem((8, 576, 128), BF16), vmem((5, 8, 144, 128), BF16), vmem((5, 144, 128), F32),
            vmem((5, 144, 128), F32), vmem((576, 128), BF16),
            dma((3,)), dma((16,)), dma((3,)), dma((16,)), dma((5,)), dma((5,)), dma((5, 8)), dma((5, 8)),
            dma((4,)), dma((4,)), dma((4, 3)), dma((4, 3)), dma((4, 3)), dma((4, 3)), dma((4,)), dma((4,)),
            dma((4, 7)), dma((4, 7)),
            dma((5, 8)), dma((5, 8)), dma((5,)), dma((5,)), dma((4,)), dma((4,)),
        ],
        compiler_params=pltpu.CompilerParams(
            collective_id=0, has_side_effects=True, vmem_limit_bytes=64 * 2**20 - 2**16
        ),
    )(
        jnp.transpose(queries, (1, 2, 0)), latent_kv.T, positions.reshape(1, 128), value_up, cotangent
    )
    return attn, jnp.transpose(gq, (2, 0, 1)), gl.T, gv.reshape(8, 16, 128)


def solution(mesh):
    in_specs = (
        P("ctx", "head", None),
        P("ctx", None),
        P("ctx"),
        P(None, "head", None),
        P("ctx", "head", None),
    )
    out_specs = (
        P("ctx", "head", None),
        P("ctx", "head", None),
        P("ctx", None),
        P("ctx", "head", None),
    )
    return jax.shard_map(body, mesh=mesh, in_specs=in_specs, out_specs=out_specs, check_vma=False)
```

```python
import math

import jax
import jax.numpy as jnp
import numpy as np
from jax import lax
from jax.experimental import pallas as pl
from jax.experimental.pallas import tpu as pltpu
from jax.sharding import PartitionSpec as P

F32, BF16 = jnp.float32, jnp.bfloat16
MESH = pl.DeviceIdType.MESH
SCALE = 1.0 / math.sqrt(192.0)
LOG2E = 1.4426950408889634
FREQUENCY = [
    float(f) for f in np.asarray(10000.0 ** (-2.0 * np.arange(32, dtype=np.float32) / 64), np.float32)
]


def dot(a, b):
    return jnp.dot(a, b, preferred_element_type=F32)


def dot_nt(a, b):
    return lax.dot_general(a, b, (((1,), (1,)), ((), ())), preferred_element_type=F32)


def kernel(
    q_hbm, lat_hbm, pos_ref, vup_hbm, cot_hbm,
    attn_hbm, gq_hbm, gl_hbm, gv_hbm,
    lat_raw, vup_raw, cot_raw, gq, tab, s_buf, dp_buf, q_t, do_t, vup_h, vup_t, cot_h,
    p_buf, ds_buf, bias, peak, ao, kw, k_t,
    o_buf, ox, oy, cotx, coty, dxf, xs, rxy, ysf, ysb, ryx, zs, rz, fxs, fxr, fys, fyr, gv,
    dks, drow, zsend, zrecv, glt,
    in_sem, q_sem, out_sem, gq_sem, kz_s, kz_r, kr_s, kr_r,
    cx_s, cx_r, cy_s, cy_r, ox_s, ox_r, oy_s, oy_r, xy_s, xy_r, yx_s, yx_r, rz_s, rz_r, fx_s, fx_r, fy_s, fy_r,
    dr_s, dr_r, dz_s, dz_r, gl_s, gl_r,
):
    ctx, head = lax.axis_index("ctx"), lax.axis_index("head")
    a, row = ctx % 2, ctx // 2
    y, z = ctx // 16, (ctx // 2) % 8
    me = a * 4 + head
    partner = ctx + 1 - 2 * a

    def mate(t):
        m = (me + t) % 8
        return m, m // 4, m % 4

    def rcopy(src, dst, ss, rs, to_ctx, to_head):
        return pltpu.make_async_remote_copy(
            src_ref=src, dst_ref=dst, send_sem=ss, recv_sem=rs,
            device_id=(to_ctx, to_head), device_id_type=MESH,
        )

    in_copies = [
        pltpu.make_async_copy(src, dst, in_sem.at[i])
        for i, (src, dst) in enumerate(((lat_hbm, lat_raw), (vup_hbm, vup_raw), (cot_hbm, cot_raw)))
    ]
    for c in in_copies:
        c.start()

    def q_copy(h):
        cols = pl.ds(pl.multiple_of(h * 128, 128), 128)
        return pltpu.make_async_copy(q_hbm.at[h], q_t.at[:, cols], q_sem.at[h])

    for h in range(16):
        q_copy(h).start()

    partners = []
    for t in range(1, 8):
        m, a2, h2 = mate(t)
        partners.append((row * 2 + a2, h2))
    for d in (1, 2, 3, 4):
        partners.append(((ctx + 2 * d) % 64, head))
        partners.append(((ctx + 64 - 2 * d) % 64, head))
    partners.append(((ctx + 64 - 7 + 14 * a) % 64, head))
    for t in range(1, 4):
        partners.append((((y + t) % 4) * 16 + ctx % 16, head))
    for t in range(1, 8):
        partners.append((y * 16 + ((z + t) % 8) * 2 + a, head))
    barrier = pltpu.get_barrier_semaphore()
    for c, h in partners:
        pl.semaphore_signal(barrier, inc=1, device_id=(c, h), device_id_type=MESH)

    lane = lax.broadcasted_iota(jnp.int32, (128, 128), 1)
    sub = lax.broadcasted_iota(jnp.int32, (128, 128), 0)
    frequency = jnp.zeros((32, 128), F32)
    for i in range(32):
        frequency = jnp.where(sub[:32] == i, FREQUENCY[i], frequency)
    angle = pos_ref[...].astype(F32) * frequency
    tab[0] = jnp.cos(angle)
    tab[1] = jnp.sin(angle)

    in_copies[0].wait()
    own = 7 * 128
    k_t[:512, own:own + 128] = lat_raw[:512, :]
    lower, upper = lat_raw[512:544, :].astype(F32), lat_raw[544:576, :].astype(F32)
    k_t[512:544, own:own + 128] = (lower * tab[0] - upper * tab[1]).astype(BF16)
    k_t[544:576, own:own + 128] = (upper * tab[0] + lower * tab[1]).astype(BF16)
    kw[own:own + 128, :] = k_t[:, own:own + 128].T

    pl.semaphore_wait(barrier, len(partners))

    def krows(slot, h):
        return kw.at[pl.ds(pl.multiple_of(slot * 128 + h * 32, 32), 32)]

    def kz(d):
        to = (ctx + (2 * d if d < 4 else 7)) % 64
        return rcopy(krows(7, head), krows(7 - 2 * d if d < 4 else 0, head), kz_s.at[d], kz_r.at[d], to, head)

    def kfwd(d, t):
        m, a2, h2 = mate(t)
        return rcopy(
            krows(7 - 2 * d, head), krows(7 - (2 * d + a2 - a), head),
            kr_s.at[d, t], kr_r.at[d, me], row * 2 + a2, h2,
        )

    def kgot(d, t):
        m, a2, h2 = mate(t)
        ref = krows(7 - (2 * d + a - a2), h2)
        return rcopy(ref, ref, kr_s.at[d, t], kr_r.at[d, m], row * 2 + a2, h2)

    def kfirst(h2):
        return rcopy(krows(7, head), krows(6, head), kr_s.at[0, h2], kr_r.at[0, head], row * 2 + 1, h2)

    def kfirst_got(h2):
        return rcopy(krows(6, h2), krows(6, h2), kr_s.at[0, h2], kr_r.at[0, h2], row * 2, h2)

    def klast(t):
        return rcopy(krows(0, head), krows(0, head), kr_s.at[4, t], kr_r.at[4, head], row * 2, (head + t) % 4)

    def klast_got(t):
        h2 = (head + t) % 4
        return rcopy(krows(0, h2), krows(0, h2), kr_s.at[4, t], kr_r.at[4, h2], row * 2, h2)

    for d in (1, 2, 3):
        kz(d).start()

    @pl.when(a == 1)
    def _():
        kz(4).start()

    @pl.when(a == 0)
    def _():
        for h2 in range(4):
            kfirst(h2).start()

    def forward(d):
        kz(d).wait_recv()
        for t in range(1, 8):
            kfwd(d, t).start()

    def vup_in(i, c):
        v = vup_raw[pl.ds(i * 8, 8)].astype(F32).reshape(128, 128)
        s_buf[i // 8, pl.ds((i % 8) * 128, 128), :] = v
        return c

    def cot_in(i, c):
        s_buf[8 + i // 8, pl.ds((i % 8) * 128, 128), :] = cot_raw[pl.ds(i * 8, 8)].astype(F32).reshape(128, 128)
        return c

    def head_up(h, c):
        for cc in range(8):
            vup_h[h, cc * 64:(cc + 1) * 64, :] = s_buf[cc, pl.ds(h, 64, stride=16), :].astype(BF16)
        cot = jnp.concatenate(
            [s_buf[8, pl.ds(h, 64, stride=16), :], s_buf[9, pl.ds(h, 64, stride=16), :]], axis=0
        ).astype(BF16)
        cot_h[h] = cot
        v = vup_h[h]
        vup_t[h] = v.T
        do_t[:, pl.ds(pl.multiple_of(h * 128, 128), 128)] = dot(v, cot.T).astype(BF16)
        return c

    def head_q(h, c):
        q_copy(h).wait()
        cols = pl.ds(pl.multiple_of(h * 128, 128), 128)
        lower, upper = q_t[512:544, cols].astype(F32), q_t[544:576, cols].astype(F32)
        q_t[512:544, cols] = (lower * tab[0] - upper * tab[1]).astype(BF16)
        q_t[544:576, cols] = (upper * tab[0] + lower * tab[1]).astype(BF16)
        return c

    in_copies[1].wait()
    lax.fori_loop(0, 64, vup_in, 0)
    in_copies[2].wait()
    lax.fori_loop(0, 16, cot_in, 0)
    forward(1)
    lax.fori_loop(0, 8, head_up, 0)
    forward(2)
    lax.fori_loop(8, 16, head_up, 0)
    forward(3)

    def cx_copy(hg):
        return rcopy(
            cot_h.at[4 * hg + 1 - a], cotx.at[hg, pl.ds(pl.multiple_of(128 * a, 128), 128)],
            cx_s.at[hg], cx_r.at[hg], partner, head,
        )

    def cx_got(hg):
        ref = cotx.at[hg, pl.ds(pl.multiple_of(128 - 128 * a, 128), 128)]
        return rcopy(ref, ref, cx_s.at[hg], cx_r.at[hg], partner, head)

    def y_head(r, y2):
        return 4 * (2 * r + y2 // 2) + 2 + y2 % 2

    def cy_copy(r, t):
        y2 = (y + t) % 4
        return rcopy(
            cot_h.at[y_head(r, y2)], coty.at[r, pl.ds(pl.multiple_of(128 * y, 128), 128)],
            cy_s.at[r, t], cy_r.at[r, y], y2 * 16 + ctx % 16, head,
        )

    def cy_got(r, t):
        y2 = (y + t) % 4
        ref = coty.at[r, pl.ds(pl.multiple_of(128 * y2, 128), 128)]
        return rcopy(ref, ref, cy_s.at[r, t], cy_r.at[r, y2], y2 * 16 + ctx % 16, head)

    for hg in range(4):
        cx_copy(hg).start()
        cotx[hg, pl.ds(pl.multiple_of(128 * a, 128), 128), :] = cot_h[4 * hg + a]
    for r in range(2):
        for t in range(1, 4):
            cy_copy(r, t).start()
        coty[r, pl.ds(pl.multiple_of(128 * y, 128), 128), :] = cot_h[y_head(r, y)]

    lax.fori_loop(0, 16, head_q, 0)

    @pl.when(a == 0)
    def _():
        kz(4).wait_recv()
        for t in range(1, 4):
            klast(t).start()

    for w in range(8):
        back = 896 - w * 128 + lane - sub
        bias[w * 128:(w + 1) * 128, :] = jnp.where((back >= 0) & (back <= pos_ref[...]), 0.0, -jnp.inf)

    def score_group(g):
        rows = slice(g * 256, g * 256 + 256)

        def qk(r, c):
            s = dot(kw[rows, :], q_t[:, pl.ds(pl.multiple_of(r * 512, 512), 512)])
            for j in range(4):
                h = r * 4 + j
                x = s[:, j * 128:(j + 1) * 128] * (SCALE * LOG2E) + bias[rows, :]
                s_buf[h, rows, :] = x
                top = jnp.max(x.reshape(32, 8, 128), axis=0)
                peak[h] = top if g == 3 else jnp.maximum(peak[h], top)
            return c

        lax.fori_loop(0, 4, qk, 0)
        for w in (2 * g, 2 * g + 1):
            if w < 7:
                k_t[:, w * 128:(w + 1) * 128] = kw[w * 128:(w + 1) * 128, :].T

    def arrived(d):
        for t in range(1, 8):
            kgot(d, t).wait_recv()

    @pl.when(a == 1)
    def _():
        for h2 in range(4):
            kfirst_got(h2).wait_recv()

    arrived(1)
    score_group(3)
    arrived(2)
    score_group(2)
    arrived(3)
    score_group(1)

    @pl.when(a == 0)
    def _():
        for t in range(1, 4):
            klast_got(t).wait_recv()

    score_group(0)

    def y_index(y2):
        return y2 * 16 + ctx % 16

    def ox_copy(hg):
        cols = pl.ds(pl.multiple_of(128 * a, 128), 128)
        return rcopy(o_buf.at[4 * hg + 1 - a], ox.at[hg, :, cols], ox_s.at[hg], ox_r.at[hg], partner, head)

    def ox_got(hg):
        ref = ox.at[hg, :, pl.ds(pl.multiple_of(128 - 128 * a, 128), 128)]
        return rcopy(ref, ref, ox_s.at[hg], ox_r.at[hg], partner, head)

    def oy_copy(hg, j):
        y2 = 2 * (hg % 2) + j
        cols = pl.ds(pl.multiple_of(128 * y, 128), 128)
        return rcopy(
            o_buf.at[4 * hg + 2 + j], oy.at[hg // 2, :, cols], oy_s.at[hg, j], oy_r.at[hg // 2, y],
            y_index(y2), head,
        )

    def oy_got(r, t):
        y2 = (y + t) % 4
        ref = oy.at[r, :, pl.ds(pl.multiple_of(128 * y2, 128), 128)]
        return rcopy(ref, ref, oy_s.at[2 * r, 0], oy_r.at[r, y2], y_index(y2), head)

    def xy_copy(hg, t):
        y2 = (y + t) % 4
        rows = pl.ds(pl.multiple_of(128 * y2, 128), 128)
        return rcopy(
            xs.at[hg, rows], rxy.at[hg, t - 1], xy_s.at[hg, t - 1], xy_r.at[hg, t - 1], y_index(y2), head
        )

    def yx_copy(r):
        return rcopy(ysb.at[r, 1 - a], ryx.at[r], yx_s.at[r], yx_r.at[r], partner, head)

    def z_copy(r, t):
        z2 = (z + t) % 8
        return rcopy(
            zs.at[r, z2], rz.at[r, t - 1], rz_s.at[r, t - 1], rz_r.at[r, t - 1], y * 16 + z2 * 2 + a, head
        )

    def fx_copy(r):
        return rcopy(fxs.at[r], fxr.at[r], fx_s.at[r], fx_r.at[r], partner, head)

    def fy_copy(r, t):
        y2 = (y + t) % 4
        rows = pl.ds(pl.multiple_of(8 * y2, 8), 8)
        return rcopy(fys.at[r, rows], fyr.at[r, t - 1], fy_s.at[r, t - 1], fy_r.at[r, t - 1], y_index(y2), head)

    def x_second(hg):
        ox_got(hg).wait_recv()
        cx_got(hg).wait_recv()
        total = dot(ox[hg], cotx[hg])
        dxf[hg] = total
        xs[hg] = total.astype(BF16)
        for t in range(1, 4):
            xy_copy(hg, t).start()

    def y_second(r):
        for t in range(1, 4):
            oy_got(r, t).wait_recv()
            cy_got(r, t).wait_recv()
        total = dot(oy[r], coty[r]).reshape(32, 2, 8, 128)
        for half in range(2):
            part = total[:, half].reshape(256, 128)
            ysf[r, half] = part
            ysb[r, half] = part.astype(BF16)
        yx_copy(r).start()

    def third(r):
        for j in range(2):
            hg = 2 * r + j
            for t in range(1, 4):
                xy_copy(hg, t).wait_recv()
            total = dxf[hg, pl.ds(pl.multiple_of(128 * y, 128), 128), :]
            for t in range(3):
                total = total + rxy[hg, t].astype(F32)
            zs[r, :, 16 * j:16 * j + 16, :] = total.reshape(8, 16, 128)
        yx_copy(r).wait_recv()
        total = (ysf[r, a] + ryx[r].astype(F32)).reshape(4, 8, 8, 128)
        for y2 in range(4):
            zs[r, :, 32 + 8 * y2:40 + 8 * y2, :] = total[y2]
        for t in range(1, 8):
            z_copy(r, t).start()

    def fourth(r):
        for t in range(1, 8):
            z_copy(r, t).wait_recv()
        total = zs[r, z]
        for t in range(7):
            total = total + rz[r, t]
        for j in range(2):
            low, high = total[16 * j:16 * j + 8], total[16 * j + 8:16 * j + 16]
            fxs[r, 8 * j:8 * j + 8, :] = jnp.where(a == 0, high, low)
            gv[pl.ds(4 * (2 * r + j) + a, 8, stride=16), :] = jnp.where(a == 0, low, high)
        fys[r] = total[32:]
        fx_copy(r).start()
        for t in range(1, 4):
            fy_copy(r, t).start()

    def fifth(r):
        fx_copy(r).wait_recv()
        for j in range(2):
            gv[pl.ds(4 * (2 * r + j) + 1 - a, 8, stride=16), :] = fxr[r, 8 * j:8 * j + 8, :]
        for t in range(1, 4):
            fy_copy(r, t).wait_recv()
        for t in range(4):
            y2 = (y + 4 - t) % 4
            rows = fys[r, pl.ds(pl.multiple_of(8 * y, 8), 8), :] if t == 0 else fyr[r, t - 1]
            gv[pl.ds(4 * (2 * r + y2 // 2) + 2 + y2 % 2, 8, stride=16), :] = rows

    def folded(x):
        return jnp.sum(x.reshape(16, 8, 128), axis=0)

    def block(i):
        return pl.ds(pl.multiple_of(i * 128, 128), 128)

    def softmax(h, c):
        cols = pl.ds(pl.multiple_of(h * 128, 128), 128)
        top = jnp.max(peak[h], axis=0, keepdims=True)

        def exps(i, mass):
            e = jnp.exp2(s_buf[h, block(i), :] - top)
            s_buf[h, block(i), :] = e
            return mass + folded(e)

        mass = lax.fori_loop(0, 8, exps, jnp.zeros((8, 128), F32), unroll=2)
        inverse = 1.0 / jnp.sum(mass, axis=0, keepdims=True)

        def probs(i, c2):
            p_buf[block(i), cols] = (s_buf[h, block(i), :] * inverse).astype(BF16)
            return c2

        lax.fori_loop(0, 8, probs, 0, unroll=2)
        return c

    for hg in range(4):
        lax.fori_loop(4 * hg, 4 * hg + 4, softmax, 0)
        o = dot(k_t[:512, :], p_buf[:, hg * 512:hg * 512 + 512]).astype(BF16)
        for j in range(4):
            o_buf[4 * hg + j] = o[:, j * 128:(j + 1) * 128]
        ox_copy(hg).start()
        ox[hg, :, pl.ds(pl.multiple_of(128 * a, 128), 128)] = o_buf[4 * hg + a]
        for j in range(2):
            @pl.when(y != 2 * (hg % 2) + j)
            def _():
                oy_copy(hg, j).start()

            @pl.when(y == 2 * (hg % 2) + j)
            def _():
                oy[hg // 2, :, pl.ds(pl.multiple_of(128 * y, 128), 128)] = o_buf[4 * hg + 2 + j]
        for j in range(4):
            h = hg * 4 + j
            ao[pl.ds(h, 128, stride=16), :] = dot(vup_t[h], o[:, j * 128:(j + 1) * 128]).T
        if hg >= 1:
            x_second(hg - 1)
        if hg == 2:
            y_second(0)

    def attn16(i, c):
        cot_raw[pl.ds(i * 8, 8)] = ao[pl.ds(i * 128, 128), :].reshape(8, 16, 128).astype(BF16)
        return c

    lax.fori_loop(0, 16, attn16, 0)
    outs = [pltpu.make_async_copy(cot_raw, attn_hbm, out_sem.at[0])]
    outs[0].start()

    def score_grads(hg):
        dp_buf[...] = dot(kw[:, :512], do_t[:, hg * 512:hg * 512 + 512]) * SCALE

        def one_head(j, c):
            h = hg * 4 + j
            cols = pl.ds(pl.multiple_of(h * 128, 128), 128)
            dp_cols = pl.ds(pl.multiple_of(j * 128, 128), 128)

            def deltas(i, delta):
                return delta + folded(p_buf[block(i), cols].astype(F32) * dp_buf[block(i), dp_cols])

            delta = lax.fori_loop(0, 8, deltas, jnp.zeros((8, 128), F32), unroll=2)
            delta = jnp.sum(delta, axis=0, keepdims=True)

            def grads(i, c2):
                p = p_buf[block(i), cols].astype(F32)
                ds_buf[block(i), cols] = (p * (dp_buf[block(i), dp_cols] - delta)).astype(BF16)
                return c2

            lax.fori_loop(0, 8, grads, 0, unroll=2)
            return c

        lax.fori_loop(0, 4, one_head, 0)

    score_grads(0)
    x_second(3)
    y_second(1)
    third(0)
    score_grads(1)
    score_grads(2)
    third(1)
    score_grads(3)
    fourth(0)

    def quarter(slot, j):
        return dks.at[slot, pl.ds(pl.multiple_of(144 * j, 16), 144)]

    def dr_copy(d, t):
        m, a2, h2 = mate(t)
        return rcopy(
            quarter(7 - (2 * d + a - a2), h2), drow.at[d, me], dr_s.at[d, t], dr_r.at[d, me], row * 2 + a2, h2
        )

    def dr_got(d, t):
        m, a2, h2 = mate(t)
        return rcopy(drow.at[d, m], drow.at[d, m], dr_s.at[d, t], dr_r.at[d, m], row * 2 + a2, h2)

    def dr_last(h2):
        return rcopy(quarter(0, h2), drow.at[4, head], dr_s.at[4, h2], dr_r.at[4, head], row * 2 + 1, h2)

    def dr_last_got(h2):
        return rcopy(drow.at[4, h2], drow.at[4, h2], dr_s.at[4, h2], dr_r.at[4, h2], row * 2, h2)

    def dz_copy(d):
        return rcopy(zsend.at[d], zrecv.at[d], dz_s.at[d], dz_r.at[d], (ctx + 64 - 2 * d) % 64, head)

    def same_row(t):
        m, a2, h2 = mate(t)
        return a2 <= a

    def same_row_got(t):
        m, a2, h2 = mate(t)
        return a2 >= a

    def key_grads(g):
        rows = slice(g * 256, g * 256 + 256)
        x = dot_nt(q_t[...], ds_buf[rows, :])
        v = dot_nt(do_t[...], p_buf[rows, :])
        for i in range(2):
            part = slice(128 * i, 128 * i + 128)
            dks[2 * g + i, :512, :] = (x[:512, part] + v[:, part]).astype(BF16)
            dks[2 * g + i, 512:, :] = x[512:, part].astype(BF16)

    def row_sum(d):
        for t in range(1, 8):
            dr_got(d, t).wait_recv()
        total = quarter(7 - 2 * d, head)[...].astype(F32)
        for t in range(1, 8):
            total = total + drow[d, (me + t) % 8].astype(F32)
        zsend[d] = total
        dz_copy(d).start()

    @pl.when(a == 1)
    def _():
        drow[0, 0:4] = jnp.zeros((4, 144, 128), BF16)

    @pl.when(a == 0)
    def _():
        zrecv[4] = jnp.zeros((144, 128), F32)

    key_grads(0)

    @pl.when(a == 0)
    def _():
        for h2 in range(4):
            dr_last(h2).start()

    key_grads(1)
    for t in range(1, 8):
        dr_copy(3, t).start()
    key_grads(2)
    for t in range(1, 8):
        dr_copy(2, t).start()
    row_sum(3)

    @pl.when(a == 1)
    def _():
        for h2 in range(4):
            dr_last_got(h2).wait_recv()
        total = drow[4, 0].astype(F32)
        for h2 in range(1, 4):
            total = total + drow[4, h2].astype(F32)
        zsend[4] = total
        dz_copy(4).start()

    key_grads(3)
    for t in range(1, 8):
        dr_copy(1, t).start()
    for t in range(1, 8):
        @pl.when(same_row(t))
        def _():
            dr_copy(0, t).start()
    row_sum(2)

    def gq_copy(h):
        return pltpu.make_async_copy(gq.at[h], gq_hbm.at[h], gq_sem.at[h])

    def dq(r, c):
        x = dot(k_t[...], ds_buf[:, pl.ds(pl.multiple_of(r * 512, 512), 512)])
        for j in range(4):
            h = r * 4 + j
            part = x[:, j * 128:(j + 1) * 128]
            lower, upper = part[512:544], part[544:576]
            gq[h, :512, :] = part[:512].astype(BF16)
            gq[h, 512:544, :] = (lower * tab[0] + upper * tab[1]).astype(BF16)
            gq[h, 544:576, :] = (upper * tab[0] - lower * tab[1]).astype(BF16)
            gq_copy(h).start()
        return c

    lax.fori_loop(0, 2, dq, 0)
    row_sum(1)

    fourth(1)
    fifth(0)
    lax.fori_loop(2, 4, dq, 0)

    for t in range(1, 8):
        @pl.when(same_row_got(t))
        def _():
            dr_got(0, t).wait_recv()
    total = quarter(7, head)[...].astype(F32)
    for t in range(1, 8):
        total = total + drow[0, (me + t) % 8].astype(F32)
    for d in (1, 2, 3):
        dz_copy(d).wait_recv()

    @pl.when(a == 1)
    def _():
        dz_copy(4).wait_recv()

    for d in (1, 2, 3, 4):
        total = total + zrecv[d]
    roped = head == 3
    cosine = jnp.where(roped, tab[0], 1.0)
    sine = jnp.where(roped, tab[1], 0.0)
    lower, upper = total[80:112], total[112:144]
    own_quarter = glt.at[pl.ds(pl.multiple_of(144 * head, 16), 144)]
    own_quarter[...] = jnp.concatenate(
        [total[:80], lower * cosine + upper * sine, upper * cosine - lower * sine], axis=0
    ).astype(BF16)

    def gl_copy(t):
        return rcopy(own_quarter, own_quarter, gl_s.at[t], gl_r.at[head], ctx, (head + t) % 4)

    def gl_got(t):
        h2 = (head + t) % 4
        ref = glt.at[pl.ds(pl.multiple_of(144 * h2, 16), 144)]
        return rcopy(ref, ref, gl_s.at[t], gl_r.at[h2], ctx, h2)

    for t in range(1, 4):
        gl_copy(t).start()
    fifth(1)
    outs.append(pltpu.make_async_copy(gv, gv_hbm, out_sem.at[1]))
    outs[-1].start()

    for t in range(1, 4):
        gl_got(t).wait_recv()
    outs.append(pltpu.make_async_copy(glt, gl_hbm, out_sem.at[2]))
    outs[-1].start()

    for d in (1, 2, 3):
        kz(d).wait_send()
        for t in range(1, 8):
            kfwd(d, t).wait_send()
            dr_copy(d, t).wait_send()
        dz_copy(d).wait_send()

    @pl.when(a == 1)
    def _():
        kz(4).wait_send()
        dz_copy(4).wait_send()

    @pl.when(a == 0)
    def _():
        for h2 in range(4):
            kfirst(h2).wait_send()
            dr_last(h2).wait_send()
        for t in range(1, 4):
            klast(t).wait_send()

    for t in range(1, 8):
        @pl.when(same_row(t))
        def _():
            dr_copy(0, t).wait_send()

    for t in range(1, 4):
        gl_copy(t).wait_send()

    for hg in range(4):
        cx_copy(hg).wait_send()
        ox_copy(hg).wait_send()
        for t in range(1, 4):
            xy_copy(hg, t).wait_send()
        for j in range(2):
            @pl.when(y != 2 * (hg % 2) + j)
            def _():
                oy_copy(hg, j).wait_send()
    for r in range(2):
        yx_copy(r).wait_send()
        fx_copy(r).wait_send()
        for t in range(1, 4):
            cy_copy(r, t).wait_send()
            fy_copy(r, t).wait_send()
        for t in range(1, 8):
            z_copy(r, t).wait_send()
    for c in outs:
        c.wait()
    for h in range(16):
        gq_copy(h).wait()


def body(queries, latent_kv, positions, value_up, cotangent):
    anywhere = pl.BlockSpec(memory_space=pl.ANY)
    vmem, dma = pltpu.VMEM, pltpu.SemaphoreType.DMA
    attn, gq, gl, gv = pl.pallas_call(
        kernel,
        out_shape=(
            jax.ShapeDtypeStruct((128, 16, 128), BF16),
            jax.ShapeDtypeStruct((16, 576, 128), BF16),
            jax.ShapeDtypeStruct((576, 128), BF16),
            jax.ShapeDtypeStruct((128, 128), F32),
        ),
        in_specs=[anywhere, anywhere, pl.BlockSpec(memory_space=pltpu.VMEM), anywhere, anywhere],
        out_specs=(anywhere,) * 4,
        scratch_shapes=[
            vmem((576, 128), BF16), vmem((512, 16, 128), BF16), vmem((128, 16, 128), BF16),
            vmem((16, 576, 128), BF16), vmem((2, 32, 128), F32),
            vmem((16, 1024, 128), F32), vmem((1024, 512), F32),
            vmem((576, 2048), BF16), vmem((512, 2048), BF16),
            vmem((16, 512, 128), BF16), vmem((16, 128, 512), BF16), vmem((16, 128, 128), BF16),
            vmem((1024, 2048), BF16), vmem((1024, 2048), BF16), vmem((1024, 128), F32), vmem((16, 8, 128), F32),
            vmem((2048, 128), F32), vmem((1024, 576), BF16), vmem((576, 1024), BF16),
            vmem((16, 512, 128), BF16), vmem((4, 512, 256), BF16), vmem((2, 512, 512), BF16),
            vmem((4, 256, 128), BF16), vmem((2, 512, 128), BF16), vmem((4, 512, 128), F32), vmem((4, 512, 128), BF16),
            vmem((4, 3, 128, 128), BF16), vmem((2, 2, 256, 128), F32), vmem((2, 2, 256, 128), BF16),
            vmem((2, 256, 128), BF16), vmem((2, 8, 64, 128), F32), vmem((2, 7, 64, 128), F32),
            vmem((2, 16, 128), F32), vmem((2, 16, 128), F32), vmem((2, 32, 128), F32), vmem((2, 3, 8, 128), F32),
            vmem((128, 128), F32),
            vmem((8, 576, 128), BF16), vmem((5, 8, 144, 128), BF16), vmem((5, 144, 128), F32),
            vmem((5, 144, 128), F32), vmem((576, 128), BF16),
            dma((3,)), dma((16,)), dma((3,)), dma((16,)), dma((5,)), dma((5,)), dma((5, 8)), dma((5, 8)),
            dma((4,)), dma((4,)), dma((2, 4)), dma((2, 4)), dma((4,)), dma((4,)), dma((4, 2)), dma((2, 4)),
            dma((4, 3)), dma((4, 3)), dma((2,)), dma((2,)), dma((2, 7)), dma((2, 7)), dma((2,)), dma((2,)),
            dma((2, 3)), dma((2, 3)),
            dma((5, 8)), dma((5, 8)), dma((5,)), dma((5,)), dma((4,)), dma((4,)),
        ],
        compiler_params=pltpu.CompilerParams(
            collective_id=0, has_side_effects=True, vmem_limit_bytes=64 * 2**20 - 2**16
        ),
    )(
        jnp.transpose(queries, (1, 2, 0)), latent_kv.T, positions.reshape(1, 128), value_up, cotangent
    )
    return attn, jnp.transpose(gq, (2, 0, 1)), gl.T, gv.reshape(8, 16, 128)


def solution(mesh):
    in_specs = (
        P("ctx", "head", None),
        P("ctx", None),
        P("ctx"),
        P(None, "head", None),
        P("ctx", "head", None),
    )
    out_specs = (
        P("ctx", "head", None),
        P("ctx", "head", None),
        P("ctx", None),
        P("ctx", "head", None),
    )
    return jax.shard_map(body, mesh=mesh, in_specs=in_specs, out_specs=out_specs, check_vma=False)
```

```python
import math

import jax
import jax.numpy as jnp
import numpy as np
from jax import lax
from jax.experimental import pallas as pl
from jax.experimental.pallas import tpu as pltpu
from jax.sharding import PartitionSpec as P

F32, BF16 = jnp.float32, jnp.bfloat16
MESH = pl.DeviceIdType.MESH
SCALE = 1.0 / math.sqrt(192.0)
LOG2E = 1.4426950408889634
FREQUENCY = [
    float(f) for f in np.asarray(10000.0 ** (-2.0 * np.arange(32, dtype=np.float32) / 64), np.float32)
]


def dot(a, b):
    return jnp.dot(a, b, preferred_element_type=F32)


def dot_nt(a, b):
    return lax.dot_general(a, b, (((1,), (1,)), ((), ())), preferred_element_type=F32)


def kernel(
    q_hbm, lat_hbm, pos_ref, vup_hbm, cot_hbm,
    attn_hbm, gq_hbm, gl_hbm, gv_hbm,
    lat_raw, vup_raw, cot_raw, gq, tab, s_buf, dp_buf, q_t, do_t, vup_h, vup_t, cot_h,
    p_buf, ds_buf, bias, peak, ao, kw, k_t, k4,
    o_buf, ox, oy, cotx, coty, dxf, xs, rxy, ysf, ysb, ryx, zs, rz, fxs, fxr, fys, fyr, gv,
    dks, dcore, csf, csb, drow, zsend, zrecv, glt,
    in_sem, q_sem, out_sem, gq_sem, ring_sem, kz_s, kz_r, kx_s, kx_r, kc_s, kc_r,
    cx_s, cx_r, cy_s, cy_r, ox_s, ox_r, oy_s, oy_r, xy_s, xy_r, yx_s, yx_r, rz_s, rz_r, fx_s, fx_r, fy_s, fy_r,
    dc_s, dc_r, dx_s, dx_r, dz_s, dz_r, gl_s, gl_r,
):
    ctx, head = lax.axis_index("ctx"), lax.axis_index("head")
    a, row = ctx % 2, ctx // 2
    y, z = ctx // 16, (ctx // 2) % 8
    partner = ctx + 1 - 2 * a

    def rcopy(src, dst, ss, rs, to_ctx, to_head):
        return pltpu.make_async_remote_copy(
            src_ref=src, dst_ref=dst, send_sem=ss, recv_sem=rs,
            device_id=(to_ctx, to_head), device_id_type=MESH,
        )

    in_copies = [
        pltpu.make_async_copy(src, dst, in_sem.at[i])
        for i, (src, dst) in enumerate(((lat_hbm, lat_raw), (vup_hbm, vup_raw), (cot_hbm, cot_raw)))
    ]
    for c in in_copies:
        c.start()

    def q_copy(h):
        cols = pl.ds(pl.multiple_of(h * 128, 128), 128)
        return pltpu.make_async_copy(q_hbm.at[h], q_t.at[:, cols], q_sem.at[h])

    for h in range(16):
        q_copy(h).start()

    core, chip = head % 2, (head // 2) * 2 + a

    def chip_at(t):
        x2 = (chip + t) % 4
        return x2, x2 % 2, x2 // 2

    def on_chip(t):
        x2, a2, hi2 = chip_at(t)
        return row * 2 + a2, hi2 * 2 + core

    def y_index(y2):
        return (y2 % 4) * 16 + ctx % 16

    def z_index(z2):
        return y * 16 + (z2 % 8) * 2 + a

    sibling = head + 1 - 2 * core
    up_row, down_row = (ctx + 2) % 64, (ctx + 62) % 64
    rings = [(y_index(y + 1), head), (y_index(y + 3), head), (z_index(z + 1), head), (z_index(z + 7), head)]
    partners = [on_chip(t) for t in range(1, 4)] + [(ctx, sibling), (up_row, head), (down_row, head)] + rings
    barrier = pltpu.get_barrier_semaphore()
    for c, h in partners:
        pl.semaphore_signal(barrier, inc=1, device_id=(c, h), device_id_type=MESH)

    lane = lax.broadcasted_iota(jnp.int32, (128, 128), 1)
    sub = lax.broadcasted_iota(jnp.int32, (128, 128), 0)
    frequency = jnp.zeros((32, 128), F32)
    for i in range(32):
        frequency = jnp.where(sub[:32] == i, FREQUENCY[i], frequency)
    angle = pos_ref[...].astype(F32) * frequency
    tab[0] = jnp.cos(angle)
    tab[1] = jnp.sin(angle)

    in_copies[0].wait()
    own = 7 * 128
    k_t[:512, own:own + 128] = lat_raw[:512, :]
    lower, upper = lat_raw[512:544, :].astype(F32), lat_raw[544:576, :].astype(F32)
    k_t[512:544, own:own + 128] = (lower * tab[0] - upper * tab[1]).astype(BF16)
    k_t[544:576, own:own + 128] = (upper * tab[0] + lower * tab[1]).astype(BF16)
    kw[own:own + 128, :] = k_t[:, own:own + 128].T

    pl.semaphore_wait(barrier, len(partners))

    def krows(slot, h):
        return kw.at[pl.ds(pl.multiple_of(slot * 128 + h * 32, 32), 32)]

    def kz(d):
        src = krows(9 - 2 * d, head)
        dst = krows(7 - 2 * d, head) if d < 4 else k4
        return rcopy(src, dst, kz_s.at[d], kz_r.at[d], up_row, head)

    def kz_got(d):
        ref = krows(7 - 2 * d, head) if d < 4 else k4
        return rcopy(ref, ref, kz_s.at[d], kz_r.at[d], down_row, head)

    def kx(d, t):
        x2, a2, hi2 = chip_at(t)
        src = krows(7 - 2 * d, head) if d < 4 else k4
        dst = krows(7 - (2 * d + a2 - a), head) if d < 4 else krows(0, head)
        return rcopy(src, dst, kx_s.at[d, t], kx_r.at[d, chip], row * 2 + a2, hi2 * 2 + core)

    def kpiece(d, x2, cc):
        slot = 7 - (2 * d + a - x2 % 2) if d < 4 else 0
        return krows(slot, (x2 // 2) * 2 + cc)

    def kx_got(d, t):
        x2, a2, hi2 = chip_at(t)
        ref = kpiece(d, x2, core)
        return rcopy(ref, ref, kx_s.at[d, t], kx_r.at[d, x2], row * 2 + a2, hi2 * 2 + core)

    def kc(d, t):
        x2, a2, hi2 = chip_at(t)
        ref = kpiece(d, x2, core)
        return rcopy(ref, ref, kc_s.at[d, x2], kc_r.at[d, x2], ctx, sibling)

    def kc_got(d, t):
        x2, a2, hi2 = chip_at(t)
        ref = kpiece(d, x2, 1 - core)
        return rcopy(ref, ref, kc_s.at[d, x2], kc_r.at[d, x2], ctx, sibling)

    def arrive(d):
        if d < 4:
            kz_got(d).wait_recv()
            if d < 3:
                kz(d + 1).start()
            else:
                @pl.when(a == 1)
                def _():
                    kz(4).start()
            for t in (1, 3, 2):
                kx(d, t).start()
            kc(d, 0).start()
        else:
            @pl.when(a == 1)
            def _():
                kz_got(4).wait_recv()
                for t in (1, 3):
                    kx(4, t).start()

    def pass_on(d):
        if d in (1, 2, 3):
            for t in (1, 3, 2):
                kx_got(d, t).wait_recv()
                kc(d, t).start()
        else:
            @pl.when(a == (1 if d == 0 else 0))
            def _():
                for t in (1, 3):
                    kx_got(d, t).wait_recv()
                    kc(d, t).start()

    def complete(d):
        if d in (1, 2, 3):
            for t in range(4):
                kc_got(d, t).wait_recv()
        else:
            @pl.when(a == (1 if d == 0 else 0))
            def _():
                for t in (1, 3):
                    kc_got(d, t).wait_recv()

    kz(1).start()

    @pl.when(a == 0)
    def _():
        for t in (1, 3):
            kx(0, t).start()

    for c, h in rings:
        pl.semaphore_signal(ring_sem.at[0], inc=1, device_id=(c, h), device_id_type=MESH)

    def vup_in(i, c):
        v = vup_raw[pl.ds(i * 8, 8)].astype(F32).reshape(128, 128)
        s_buf[i // 8, pl.ds((i % 8) * 128, 128), :] = v
        return c

    def cot_in(i, c):
        s_buf[8 + i // 8, pl.ds((i % 8) * 128, 128), :] = cot_raw[pl.ds(i * 8, 8)].astype(F32).reshape(128, 128)
        return c

    def head_up(h, c):
        for cc in range(8):
            vup_h[h, cc * 64:(cc + 1) * 64, :] = s_buf[cc, pl.ds(h, 64, stride=16), :].astype(BF16)
        cot = jnp.concatenate(
            [s_buf[8, pl.ds(h, 64, stride=16), :], s_buf[9, pl.ds(h, 64, stride=16), :]], axis=0
        ).astype(BF16)
        cot_h[h] = cot
        v = vup_h[h]
        vup_t[h] = v.T
        do_t[:, pl.ds(pl.multiple_of(h * 128, 128), 128)] = dot(v, cot.T).astype(BF16)
        return c

    def head_q(h, c):
        q_copy(h).wait()
        cols = pl.ds(pl.multiple_of(h * 128, 128), 128)
        lower, upper = q_t[512:544, cols].astype(F32), q_t[544:576, cols].astype(F32)
        q_t[512:544, cols] = (lower * tab[0] - upper * tab[1]).astype(BF16)
        q_t[544:576, cols] = (upper * tab[0] + lower * tab[1]).astype(BF16)
        return c

    in_copies[1].wait()
    lax.fori_loop(0, 32, vup_in, 0)
    arrive(1)
    lax.fori_loop(32, 64, vup_in, 0)
    pass_on(0)
    in_copies[2].wait()
    lax.fori_loop(0, 16, cot_in, 0)
    arrive(2)
    pass_on(1)
    lax.fori_loop(0, 4, head_up, 0)
    arrive(3)
    pass_on(2)
    lax.fori_loop(4, 8, head_up, 0)
    arrive(4)
    pass_on(3)
    lax.fori_loop(8, 12, head_up, 0)
    pass_on(4)
    lax.fori_loop(12, 16, head_up, 0)

    def cx_copy(hg):
        return rcopy(
            cot_h.at[4 * hg + 1 - a], cotx.at[hg, pl.ds(pl.multiple_of(128 * a, 128), 128)],
            cx_s.at[hg], cx_r.at[hg], partner, head,
        )

    def cx_got(hg):
        ref = cotx.at[hg, pl.ds(pl.multiple_of(128 - 128 * a, 128), 128)]
        return rcopy(ref, ref, cx_s.at[hg], cx_r.at[hg], partner, head)

    def y_head(r, y2):
        return 4 * (2 * r + y2 // 2) + 2 + y2 % 2

    def cy_copy(r, t):
        y2 = (y + t) % 4
        return rcopy(
            cot_h.at[y_head(r, y2)], coty.at[r, pl.ds(pl.multiple_of(128 * y, 128), 128)],
            cy_s.at[r, t], cy_r.at[r, y], y2 * 16 + ctx % 16, head,
        )

    def cy_got(r, t):
        y2 = (y + t) % 4
        ref = coty.at[r, pl.ds(pl.multiple_of(128 * y2, 128), 128)]
        return rcopy(ref, ref, cy_s.at[r, t], cy_r.at[r, y2], y2 * 16 + ctx % 16, head)

    lax.fori_loop(0, 16, head_q, 0)

    for w in range(8):
        back = 896 - w * 128 + lane - sub
        bias[w * 128:(w + 1) * 128, :] = jnp.where((back >= 0) & (back <= pos_ref[...]), 0.0, -jnp.inf)

    def score_group(g):
        rows = slice(g * 256, g * 256 + 256)

        def qk(r, c):
            s = dot(kw[rows, :], q_t[:, pl.ds(pl.multiple_of(r * 512, 512), 512)])
            for j in range(4):
                h = r * 4 + j
                x = s[:, j * 128:(j + 1) * 128] * (SCALE * LOG2E) + bias[rows, :]
                s_buf[h, rows, :] = x
                top = jnp.max(x.reshape(32, 8, 128), axis=0)
                peak[h] = top if g == 3 else jnp.maximum(peak[h], top)
            return c

        lax.fori_loop(0, 4, qk, 0)
        for w in (2 * g, 2 * g + 1):
            if w < 7:
                k_t[:, w * 128:(w + 1) * 128] = kw[w * 128:(w + 1) * 128, :].T

    complete(0)
    complete(1)
    score_group(3)
    complete(2)
    pl.semaphore_wait(ring_sem.at[0], 4)
    for c, h in rings[2:]:
        pl.semaphore_signal(ring_sem.at[1], inc=1, device_id=(c, h), device_id_type=MESH)
    score_group(2)
    complete(3)
    pl.semaphore_wait(ring_sem.at[1], 2)
    for c, h in rings[2:]:
        pl.semaphore_signal(ring_sem.at[2], inc=1, device_id=(c, h), device_id_type=MESH)
    score_group(1)
    complete(4)
    score_group(0)
    pl.semaphore_wait(ring_sem.at[2], 2)

    for hg in range(4):
        cx_copy(hg).start()
        cotx[hg, pl.ds(pl.multiple_of(128 * a, 128), 128), :] = cot_h[4 * hg + a]
    for r in range(2):
        for t in range(1, 4):
            cy_copy(r, t).start()
        coty[r, pl.ds(pl.multiple_of(128 * y, 128), 128), :] = cot_h[y_head(r, y)]

    def ox_copy(hg):
        cols = pl.ds(pl.multiple_of(128 * a, 128), 128)
        return rcopy(o_buf.at[4 * hg + 1 - a], ox.at[hg, :, cols], ox_s.at[hg], ox_r.at[hg], partner, head)

    def ox_got(hg):
        ref = ox.at[hg, :, pl.ds(pl.multiple_of(128 - 128 * a, 128), 128)]
        return rcopy(ref, ref, ox_s.at[hg], ox_r.at[hg], partner, head)

    def oy_copy(hg, j):
        y2 = 2 * (hg % 2) + j
        cols = pl.ds(pl.multiple_of(128 * y, 128), 128)
        return rcopy(
            o_buf.at[4 * hg + 2 + j], oy.at[hg // 2, :, cols], oy_s.at[hg, j], oy_r.at[hg // 2, y],
            y_index(y2), head,
        )

    def oy_got(r, t):
        y2 = (y + t) % 4
        ref = oy.at[r, :, pl.ds(pl.multiple_of(128 * y2, 128), 128)]
        return rcopy(ref, ref, oy_s.at[2 * r, 0], oy_r.at[r, y2], y_index(y2), head)

    def xy_copy(hg, t):
        y2 = (y + t) % 4
        rows = pl.ds(pl.multiple_of(128 * y2, 128), 128)
        return rcopy(
            xs.at[hg, rows], rxy.at[hg, t - 1], xy_s.at[hg, t - 1], xy_r.at[hg, t - 1], y_index(y2), head
        )

    def yx_copy(r):
        return rcopy(ysb.at[r, 1 - a], ryx.at[r], yx_s.at[r], yx_r.at[r], partner, head)

    def z_copy(r, t):
        z2 = (z + t) % 8
        return rcopy(
            zs.at[r, z2], rz.at[r, t - 1], rz_s.at[r, t - 1], rz_r.at[r, t - 1], y * 16 + z2 * 2 + a, head
        )

    def fx_copy(r):
        return rcopy(fxs.at[r], fxr.at[r], fx_s.at[r], fx_r.at[r], partner, head)

    def fy_copy(r, t):
        y2 = (y + t) % 4
        rows = pl.ds(pl.multiple_of(8 * y2, 8), 8)
        return rcopy(fys.at[r, rows], fyr.at[r, t - 1], fy_s.at[r, t - 1], fy_r.at[r, t - 1], y_index(y2), head)

    def x_second(hg):
        ox_got(hg).wait_recv()
        cx_got(hg).wait_recv()
        total = dot(ox[hg], cotx[hg])
        dxf[hg] = total
        xs[hg] = total.astype(BF16)
        for t in range(1, 4):
            xy_copy(hg, t).start()

    def y_second(r):
        for t in range(1, 4):
            oy_got(r, t).wait_recv()
            cy_got(r, t).wait_recv()
        total = dot(oy[r], coty[r]).reshape(32, 2, 8, 128)
        for half in range(2):
            part = total[:, half].reshape(256, 128)
            ysf[r, half] = part
            ysb[r, half] = part.astype(BF16)
        yx_copy(r).start()

    def third(r):
        for j in range(2):
            hg = 2 * r + j
            for t in range(1, 4):
                xy_copy(hg, t).wait_recv()
            total = dxf[hg, pl.ds(pl.multiple_of(128 * y, 128), 128), :]
            for t in range(3):
                total = total + rxy[hg, t].astype(F32)
            zs[r, :, 16 * j:16 * j + 16, :] = total.reshape(8, 16, 128)
        yx_copy(r).wait_recv()
        total = (ysf[r, a] + ryx[r].astype(F32)).reshape(4, 8, 8, 128)
        for y2 in range(4):
            zs[r, :, 32 + 8 * y2:40 + 8 * y2, :] = total[y2]
        for t in range(1, 8):
            z_copy(r, t).start()

    def fourth(r):
        for t in range(1, 8):
            z_copy(r, t).wait_recv()
        total = zs[r, z]
        for t in range(7):
            total = total + rz[r, t]
        for j in range(2):
            low, high = total[16 * j:16 * j + 8], total[16 * j + 8:16 * j + 16]
            fxs[r, 8 * j:8 * j + 8, :] = jnp.where(a == 0, high, low)
            gv[pl.ds(4 * (2 * r + j) + a, 8, stride=16), :] = jnp.where(a == 0, low, high)
        fys[r] = total[32:]
        fx_copy(r).start()
        for t in range(1, 4):
            fy_copy(r, t).start()

    def fifth(r):
        fx_copy(r).wait_recv()
        for j in range(2):
            gv[pl.ds(4 * (2 * r + j) + 1 - a, 8, stride=16), :] = fxr[r, 8 * j:8 * j + 8, :]
        for t in range(1, 4):
            fy_copy(r, t).wait_recv()
        for t in range(4):
            y2 = (y + 4 - t) % 4
            rows = fys[r, pl.ds(pl.multiple_of(8 * y, 8), 8), :] if t == 0 else fyr[r, t - 1]
            gv[pl.ds(4 * (2 * r + y2 // 2) + 2 + y2 % 2, 8, stride=16), :] = rows

    def folded(x):
        return jnp.sum(x.reshape(16, 8, 128), axis=0)

    def block(i):
        return pl.ds(pl.multiple_of(i * 128, 128), 128)

    def softmax(h, c):
        cols = pl.ds(pl.multiple_of(h * 128, 128), 128)
        top = jnp.max(peak[h], axis=0, keepdims=True)

        def exps(i, mass):
            e = jnp.exp2(s_buf[h, block(i), :] - top)
            s_buf[h, block(i), :] = e
            return mass + folded(e)

        mass = lax.fori_loop(0, 8, exps, jnp.zeros((8, 128), F32), unroll=2)
        inverse = 1.0 / jnp.sum(mass, axis=0, keepdims=True)

        def probs(i, c2):
            p_buf[block(i), cols] = (s_buf[h, block(i), :] * inverse).astype(BF16)
            return c2

        lax.fori_loop(0, 8, probs, 0, unroll=2)
        return c

    for hg in range(4):
        lax.fori_loop(4 * hg, 4 * hg + 4, softmax, 0)
        o = dot(k_t[:512, :], p_buf[:, hg * 512:hg * 512 + 512]).astype(BF16)
        for j in range(4):
            o_buf[4 * hg + j] = o[:, j * 128:(j + 1) * 128]
        ox_copy(hg).start()
        ox[hg, :, pl.ds(pl.multiple_of(128 * a, 128), 128)] = o_buf[4 * hg + a]
        for j in range(2):
            @pl.when(y != 2 * (hg % 2) + j)
            def _():
                oy_copy(hg, j).start()

            @pl.when(y == 2 * (hg % 2) + j)
            def _():
                oy[hg // 2, :, pl.ds(pl.multiple_of(128 * y, 128), 128)] = o_buf[4 * hg + 2 + j]
        for j in range(4):
            h = hg * 4 + j
            ao[pl.ds(h, 128, stride=16), :] = dot(vup_t[h], o[:, j * 128:(j + 1) * 128]).T
        if hg >= 1:
            x_second(hg - 1)
        if hg == 2:
            y_second(0)

    def attn16(i, c):
        cot_raw[pl.ds(i * 8, 8)] = ao[pl.ds(i * 128, 128), :].reshape(8, 16, 128).astype(BF16)
        return c

    lax.fori_loop(0, 16, attn16, 0)
    outs = [pltpu.make_async_copy(cot_raw, attn_hbm, out_sem.at[0])]
    outs[0].start()

    def score_grads(hg):
        dp_buf[...] = dot(kw[:, :512], do_t[:, hg * 512:hg * 512 + 512]) * SCALE

        def one_head(j, c):
            h = hg * 4 + j
            cols = pl.ds(pl.multiple_of(h * 128, 128), 128)
            dp_cols = pl.ds(pl.multiple_of(j * 128, 128), 128)

            def deltas(i, delta):
                return delta + folded(p_buf[block(i), cols].astype(F32) * dp_buf[block(i), dp_cols])

            delta = lax.fori_loop(0, 8, deltas, jnp.zeros((8, 128), F32), unroll=2)
            delta = jnp.sum(delta, axis=0, keepdims=True)

            def grads(i, c2):
                p = p_buf[block(i), cols].astype(F32)
                ds_buf[block(i), cols] = (p * (dp_buf[block(i), dp_cols] - delta)).astype(BF16)
                return c2

            lax.fori_loop(0, 8, grads, 0, unroll=2)
            return c

        lax.fori_loop(0, 4, one_head, 0)

    score_grads(0)
    x_second(3)
    y_second(1)
    third(0)
    score_grads(1)
    score_grads(2)
    third(1)
    score_grads(3)
    fourth(0)

    def half_rows(cc):
        return pl.ds(pl.multiple_of(288 * cc, 16), 288)

    def quarter_rows(hi2):
        return pl.ds(pl.multiple_of(144 * hi2, 16), 144)

    def dc_copy(g):
        return rcopy(dks.at[pl.ds(2 * g, 2), half_rows(1 - core)], dcore.at[g], dc_s.at[g], dc_r.at[g], ctx, sibling)

    def dx_copy(d, t):
        x2, a2, hi2 = chip_at(t)
        slot = 7 - (2 * d + a - a2) if d < 4 else 0
        return rcopy(
            csb.at[slot, quarter_rows(hi2)], drow.at[d, chip], dx_s.at[d, t], dx_r.at[d, chip],
            row * 2 + a2, hi2 * 2 + core,
        )

    def dx_got(d, t):
        x2, a2, hi2 = chip_at(t)
        return rcopy(
            drow.at[d, x2], drow.at[d, x2], dx_s.at[d, t], dx_r.at[d, x2], row * 2 + a2, hi2 * 2 + core
        )

    def dz_copy(d):
        return rcopy(zsend.at[d], zrecv.at[d], dz_s.at[d], dz_r.at[d], down_row, head)

    def key_grads(g):
        rows = slice(g * 256, g * 256 + 256)
        x = dot_nt(q_t[...], ds_buf[rows, :])
        v = dot_nt(do_t[...], p_buf[rows, :])
        for i in range(2):
            part = slice(128 * i, 128 * i + 128)
            dks[2 * g + i, :512, :] = x[:512, part] + v[:, part]
            dks[2 * g + i, 512:, :] = x[512:, part]
        dc_copy(g).start()

    def chip_sum(g):
        dc_copy(g).wait_recv()
        for i in range(2):
            total = dks[2 * g + i, half_rows(core), :] + dcore[g, i]
            csf[2 * g + i] = total
            csb[2 * g + i] = total.astype(BF16)

        @pl.when(a == 1)
        def _():
            for t in (1, 3, 2):
                dx_copy(3 - g, t).start()

        @pl.when(a == 0)
        def _():
            for t in (1, 3, 2) if g > 0 else (1, 3):
                dx_copy(4 - g, t).start()
            if g == 3:
                dx_copy(0, 2).start()

    def own_part(d):
        return csf[7 - 2 * d, quarter_rows(head // 2), :]

    def row_sum(d):
        total = own_part(d)
        for t in range(1, 4):
            dx_got(d, t).wait_recv()
        for t in range(1, 4):
            total = total + drow[d, (chip + t) % 4].astype(F32)
        if d < 3:
            dz_copy(d + 1).wait_recv()
            total = total + zrecv[d + 1]
        else:
            @pl.when(a == 1)
            def _():
                dz_copy(4).wait_recv()
            total = total + zrecv[4]
        zsend[d] = total
        dz_copy(d).start()

    @pl.when(a == 0)
    def _():
        zrecv[4] = jnp.zeros((144, 128), F32)

    @pl.when(a == 1)
    def _():
        drow[0, 0] = jnp.zeros((144, 128), BF16)
        drow[0, 2] = jnp.zeros((144, 128), BF16)

    key_grads(0)
    key_grads(1)
    chip_sum(0)
    key_grads(2)
    chip_sum(1)

    @pl.when(a == 1)
    def _():
        for t in (1, 3):
            dx_got(4, t).wait_recv()
        zsend[4] = drow[4, 0].astype(F32) + drow[4, 2].astype(F32)
        dz_copy(4).start()

    key_grads(3)
    chip_sum(2)
    row_sum(3)

    def gq_copy(h):
        return pltpu.make_async_copy(gq.at[h], gq_hbm.at[h], gq_sem.at[h])

    def dq(r, c):
        x = dot(k_t[...], ds_buf[:, pl.ds(pl.multiple_of(r * 512, 512), 512)])
        for j in range(4):
            h = r * 4 + j
            part = x[:, j * 128:(j + 1) * 128]
            lower, upper = part[512:544], part[544:576]
            gq[h, :512, :] = part[:512].astype(BF16)
            gq[h, 512:544, :] = (lower * tab[0] + upper * tab[1]).astype(BF16)
            gq[h, 544:576, :] = (upper * tab[0] - lower * tab[1]).astype(BF16)
            gq_copy(h).start()
        return c

    lax.fori_loop(0, 1, dq, 0)
    chip_sum(3)
    row_sum(2)
    lax.fori_loop(1, 2, dq, 0)
    fourth(1)
    row_sum(1)
    lax.fori_loop(2, 3, dq, 0)
    fifth(0)

    total = own_part(0)
    for t in range(1, 4):
        x2, a2, hi2 = chip_at(t)

        @pl.when(a2 >= a)
        def _():
            dx_got(0, t).wait_recv()
    for t in range(1, 4):
        total = total + drow[0, (chip + t) % 4].astype(F32)
    dz_copy(1).wait_recv()
    total = total + zrecv[1]
    quarter = 2 * core + head // 2
    roped = quarter == 3
    cosine = jnp.where(roped, tab[0], 1.0)
    sine = jnp.where(roped, tab[1], 0.0)
    lower, upper = total[80:112], total[112:144]
    own_quarter = glt.at[pl.ds(pl.multiple_of(144 * quarter, 16), 144)]
    own_quarter[...] = jnp.concatenate(
        [total[:80], lower * cosine + upper * sine, upper * cosine - lower * sine], axis=0
    ).astype(BF16)

    def gl_copy(t):
        return rcopy(own_quarter, own_quarter, gl_s.at[t], gl_r.at[head], ctx, (head + t) % 4)

    def gl_got(t):
        h2 = (head + t) % 4
        ref = glt.at[pl.ds(pl.multiple_of(144 * (2 * (h2 % 2) + h2 // 2), 16), 144)]
        return rcopy(ref, ref, gl_s.at[t], gl_r.at[h2], ctx, h2)

    for t in range(1, 4):
        gl_copy(t).start()
    lax.fori_loop(3, 4, dq, 0)
    fifth(1)
    outs.append(pltpu.make_async_copy(gv, gv_hbm, out_sem.at[1]))
    outs[-1].start()

    for t in range(1, 4):
        gl_got(t).wait_recv()
    outs.append(pltpu.make_async_copy(glt, gl_hbm, out_sem.at[2]))
    outs[-1].start()

    for d in (1, 2, 3):
        kz(d).wait_send()
        for t in range(4):
            kc(d, t).wait_send()
        for t in range(1, 4):
            kx(d, t).wait_send()
            dx_copy(d, t).wait_send()
        dz_copy(d).wait_send()
    dx_copy(0, 2).wait_send()
    for g in range(4):
        dc_copy(g).wait_send()

    @pl.when(a == 1)
    def _():
        kz(4).wait_send()
        dz_copy(4).wait_send()
        for t in (1, 3):
            kx(4, t).wait_send()
            kc(0, t).wait_send()
            dx_copy(0, t).wait_send()

    @pl.when(a == 0)
    def _():
        for t in (1, 3):
            kx(0, t).wait_send()
            kc(4, t).wait_send()
            dx_copy(4, t).wait_send()

    for t in range(1, 4):
        gl_copy(t).wait_send()

    for hg in range(4):
        cx_copy(hg).wait_send()
        ox_copy(hg).wait_send()
        for t in range(1, 4):
            xy_copy(hg, t).wait_send()
        for j in range(2):
            @pl.when(y != 2 * (hg % 2) + j)
            def _():
                oy_copy(hg, j).wait_send()
    for r in range(2):
        yx_copy(r).wait_send()
        fx_copy(r).wait_send()
        for t in range(1, 4):
            cy_copy(r, t).wait_send()
            fy_copy(r, t).wait_send()
        for t in range(1, 8):
            z_copy(r, t).wait_send()
    for c in outs:
        c.wait()
    for h in range(16):
        gq_copy(h).wait()


def handed_on(attn, gq, gl, gv, attn_out, gq_out, gl_out, gv_out, sem):
    pairs = [(gq.at[h], gq_out.at[h]) for h in range(16)] + [(attn, attn_out), (gl, gl_out), (gv, gv_out)]
    copies = [pltpu.make_async_copy(src, dst, sem.at[i]) for i, (src, dst) in enumerate(pairs)]
    for c in copies:
        c.start()
    for c in copies:
        c.wait()


def body(queries, latent_kv, positions, value_up, cotangent):
    anywhere = pl.BlockSpec(memory_space=pl.ANY)
    vmem, dma = pltpu.VMEM, pltpu.SemaphoreType.DMA
    attn, gq, gl, gv = pl.pallas_call(
        kernel,
        out_shape=(
            jax.ShapeDtypeStruct((128, 16, 128), BF16),
            jax.ShapeDtypeStruct((16, 576, 128), BF16),
            jax.ShapeDtypeStruct((576, 128), BF16),
            jax.ShapeDtypeStruct((128, 128), F32),
        ),
        in_specs=[anywhere, anywhere, pl.BlockSpec(memory_space=pltpu.VMEM), anywhere, anywhere],
        out_specs=(anywhere,) * 4,
        scratch_shapes=[
            vmem((576, 128), BF16), vmem((512, 16, 128), BF16), vmem((128, 16, 128), BF16),
            vmem((16, 576, 128), BF16), vmem((2, 32, 128), F32),
            vmem((16, 1024, 128), F32), vmem((1024, 512), F32),
            vmem((576, 2048), BF16), vmem((512, 2048), BF16),
            vmem((16, 512, 128), BF16), vmem((16, 128, 512), BF16), vmem((16, 128, 128), BF16),
            vmem((1024, 2048), BF16), vmem((1024, 2048), BF16), vmem((1024, 128), F32), vmem((16, 8, 128), F32),
            vmem((2048, 128), F32), vmem((1024, 576), BF16), vmem((576, 1024), BF16), vmem((32, 576), BF16),
            vmem((16, 512, 128), BF16), vmem((4, 512, 256), BF16), vmem((2, 512, 512), BF16),
            vmem((4, 256, 128), BF16), vmem((2, 512, 128), BF16), vmem((4, 512, 128), F32), vmem((4, 512, 128), BF16),
            vmem((4, 3, 128, 128), BF16), vmem((2, 2, 256, 128), F32), vmem((2, 2, 256, 128), BF16),
            vmem((2, 256, 128), BF16), vmem((2, 8, 64, 128), F32), vmem((2, 7, 64, 128), F32),
            vmem((2, 16, 128), F32), vmem((2, 16, 128), F32), vmem((2, 32, 128), F32), vmem((2, 3, 8, 128), F32),
            vmem((128, 128), F32),
            vmem((8, 576, 128), F32), vmem((4, 2, 288, 128), F32), vmem((8, 288, 128), F32), vmem((8, 288, 128), BF16),
            vmem((5, 4, 144, 128), BF16), vmem((5, 144, 128), F32),
            vmem((5, 144, 128), F32), vmem((576, 128), BF16),
            dma((3,)), dma((16,)), dma((3,)), dma((16,)), pltpu.SemaphoreType.REGULAR((3,)),
            dma((5,)), dma((5,)), dma((5, 4)), dma((5, 4)), dma((5, 4)), dma((5, 4)),
            dma((4,)), dma((4,)), dma((2, 4)), dma((2, 4)), dma((4,)), dma((4,)), dma((4, 2)), dma((2, 4)),
            dma((4, 3)), dma((4, 3)), dma((2,)), dma((2,)), dma((2, 7)), dma((2, 7)), dma((2,)), dma((2,)),
            dma((2, 3)), dma((2, 3)),
            dma((4,)), dma((4,)), dma((5, 4)), dma((5, 4)), dma((5,)), dma((5,)), dma((4,)), dma((4,)),
        ],
        compiler_params=pltpu.CompilerParams(
            collective_id=0, has_side_effects=True, vmem_limit_bytes=64 * 2**20 - 2**16
        ),
    )(
        jnp.transpose(queries, (1, 2, 0)), latent_kv.T, positions.reshape(1, 128), value_up, cotangent
    )
    attn, gq, gl, gv = pl.pallas_call(
        handed_on,
        out_shape=tuple(jax.ShapeDtypeStruct(x.shape, x.dtype) for x in (attn, gq, gl, gv)),
        in_specs=[anywhere] * 4,
        out_specs=(anywhere,) * 4,
        scratch_shapes=[dma((19,))],
    )(attn, gq, gl, gv)
    return attn, jnp.transpose(gq, (2, 0, 1)), gl.T, gv.reshape(8, 16, 128)


def solution(mesh):
    in_specs = (
        P("ctx", "head", None),
        P("ctx", None),
        P("ctx"),
        P(None, "head", None),
        P("ctx", "head", None),
    )
    out_specs = (
        P("ctx", "head", None),
        P("ctx", "head", None),
        P("ctx", None),
        P("ctx", "head", None),
    )
    return jax.shard_map(body, mesh=mesh, in_specs=in_specs, out_specs=out_specs, check_vma=False)
```

```python
import math

import jax
import jax.numpy as jnp
import numpy as np
from jax import lax
from jax.experimental import pallas as pl
from jax.experimental.pallas import tpu as pltpu
from jax.sharding import PartitionSpec as P

F32, BF16 = jnp.float32, jnp.bfloat16
MESH = pl.DeviceIdType.MESH
SCALE = 1.0 / math.sqrt(192.0)
LOG2E = 1.4426950408889634
FREQUENCY = [
    float(f) for f in np.asarray(10000.0 ** (-2.0 * np.arange(32, dtype=np.float32) / 64), np.float32)
]


def dot(a, b):
    return jnp.dot(a, b, preferred_element_type=F32)


def dot_nt(a, b):
    return lax.dot_general(a, b, (((1,), (1,)), ((), ())), preferred_element_type=F32)


def kernel(
    q_hbm, lat_hbm, pos_ref, vup_hbm, cot_hbm,
    attn_hbm, gq_hbm, gl_hbm, gv_hbm,
    lat_raw, vup_raw, cot_raw, gq, tab, s_buf, dp_buf, q_t, do_t, vup_h, vup_t, cot_h,
    p_buf, ds_buf, bias, peak, ao, kw, k_t, k4,
    o_buf, ox, oy, cotx, coty, dxf, xs, rxy, ysf, ysb, ryx, zs, rz, fxs, fxr, fys, fyr, gv,
    dks, dcore, csf, csb, drow, zsend, zrecv, glt,
    in_sem, q_sem, out_sem, gq_sem, ring_sem, kz_s, kz_r, kx_s, kx_r, kc_s, kc_r,
    cx_s, cx_r, cy_s, cy_r, ox_s, ox_r, oy_s, oy_r, xy_s, xy_r, yx_s, yx_r, rz_s, rz_r, fx_s, fx_r, fy_s, fy_r,
    dc_s, dc_r, dx_s, dx_r, dz_s, dz_r, gl_s, gl_r,
):
    ctx, head = lax.axis_index("ctx"), lax.axis_index("head")
    a, row = ctx % 2, ctx // 2
    y, z = ctx // 16, (ctx // 2) % 8
    partner = ctx + 1 - 2 * a

    def rcopy(src, dst, ss, rs, to_ctx, to_head):
        return pltpu.make_async_remote_copy(
            src_ref=src, dst_ref=dst, send_sem=ss, recv_sem=rs,
            device_id=(to_ctx, to_head), device_id_type=MESH,
        )

    in_copies = [
        pltpu.make_async_copy(src, dst, in_sem.at[i])
        for i, (src, dst) in enumerate(((lat_hbm, lat_raw), (vup_hbm, vup_raw), (cot_hbm, cot_raw)))
    ]
    for c in in_copies:
        c.start()

    def q_copy(h):
        cols = pl.ds(pl.multiple_of(h * 128, 128), 128)
        return pltpu.make_async_copy(q_hbm.at[h], q_t.at[:, cols], q_sem.at[h])

    for h in range(16):
        q_copy(h).start()

    core, chip = head % 2, (head // 2) * 2 + a

    def chip_at(t):
        x2 = (chip + t) % 4
        return x2, x2 % 2, x2 // 2

    def on_chip(t):
        x2, a2, hi2 = chip_at(t)
        return row * 2 + a2, hi2 * 2 + core

    def y_index(y2):
        return (y2 % 4) * 16 + ctx % 16

    def z_index(z2):
        return y * 16 + (z2 % 8) * 2 + a

    sibling = head + 1 - 2 * core
    up_row, down_row = (ctx + 2) % 64, (ctx + 62) % 64
    rings = [(y_index(y + 1), head), (y_index(y + 3), head), (z_index(z + 1), head), (z_index(z + 7), head)]
    partners = [on_chip(t) for t in range(1, 4)] + [(ctx, sibling), (up_row, head), (down_row, head)] + rings
    barrier = pltpu.get_barrier_semaphore()
    for c, h in partners:
        pl.semaphore_signal(barrier, inc=1, device_id=(c, h), device_id_type=MESH)

    lane = lax.broadcasted_iota(jnp.int32, (128, 128), 1)
    sub = lax.broadcasted_iota(jnp.int32, (128, 128), 0)
    frequency = jnp.zeros((32, 128), F32)
    for i in range(32):
        frequency = jnp.where(sub[:32] == i, FREQUENCY[i], frequency)
    angle = pos_ref[...].astype(F32) * frequency
    tab[0] = jnp.cos(angle)
    tab[1] = jnp.sin(angle)

    in_copies[0].wait()
    own = 7 * 128
    k_t[:512, own:own + 128] = lat_raw[:512, :]
    lower, upper = lat_raw[512:544, :].astype(F32), lat_raw[544:576, :].astype(F32)
    k_t[512:544, own:own + 128] = (lower * tab[0] - upper * tab[1]).astype(BF16)
    k_t[544:576, own:own + 128] = (upper * tab[0] + lower * tab[1]).astype(BF16)
    kw[own:own + 128, :] = k_t[:, own:own + 128].T

    pl.semaphore_wait(barrier, len(partners))

    def krows(slot, h):
        return kw.at[pl.ds(pl.multiple_of(slot * 128 + h * 32, 32), 32)]

    def kz(d):
        src = krows(9 - 2 * d, head)
        dst = krows(7 - 2 * d, head) if d < 4 else k4
        return rcopy(src, dst, kz_s.at[d], kz_r.at[d], up_row, head)

    def kz_got(d):
        ref = krows(7 - 2 * d, head) if d < 4 else k4
        return rcopy(ref, ref, kz_s.at[d], kz_r.at[d], down_row, head)

    def kx(d, t):
        x2, a2, hi2 = chip_at(t)
        src = krows(7 - 2 * d, head) if d < 4 else k4
        dst = krows(7 - (2 * d + a2 - a), head) if d < 4 else krows(0, head)
        return rcopy(src, dst, kx_s.at[d, t], kx_r.at[d, chip], row * 2 + a2, hi2 * 2 + core)

    def kpiece(d, x2, cc):
        slot = 7 - (2 * d + a - x2 % 2) if d < 4 else 0
        return krows(slot, (x2 // 2) * 2 + cc)

    def kx_got(d, t):
        x2, a2, hi2 = chip_at(t)
        ref = kpiece(d, x2, core)
        return rcopy(ref, ref, kx_s.at[d, t], kx_r.at[d, x2], row * 2 + a2, hi2 * 2 + core)

    def kc(d, t):
        x2, a2, hi2 = chip_at(t)
        ref = kpiece(d, x2, core)
        return rcopy(ref, ref, kc_s.at[d, x2], kc_r.at[d, x2], ctx, sibling)

    def kc_got(d, t):
        x2, a2, hi2 = chip_at(t)
        ref = kpiece(d, x2, 1 - core)
        return rcopy(ref, ref, kc_s.at[d, x2], kc_r.at[d, x2], ctx, sibling)

    def arrive(d):
        if d < 4:
            kz_got(d).wait_recv()
            if d < 3:
                kz(d + 1).start()
            else:
                @pl.when(a == 1)
                def _():
                    kz(4).start()
            for t in (1, 3, 2):
                kx(d, t).start()
            kc(d, 0).start()
        else:
            @pl.when(a == 1)
            def _():
                kz_got(4).wait_recv()
                for t in (1, 3):
                    kx(4, t).start()

    def pass_on(d):
        if d in (1, 2, 3):
            for t in (1, 3, 2):
                kx_got(d, t).wait_recv()
                kc(d, t).start()
        else:
            @pl.when(a == (1 if d == 0 else 0))
            def _():
                for t in (1, 3):
                    kx_got(d, t).wait_recv()
                    kc(d, t).start()

    def complete(d):
        if d in (1, 2, 3):
            for t in range(4):
                kc_got(d, t).wait_recv()
        else:
            @pl.when(a == (1 if d == 0 else 0))
            def _():
                for t in (1, 3):
                    kc_got(d, t).wait_recv()

    kz(1).start()

    @pl.when(a == 0)
    def _():
        for t in (1, 3):
            kx(0, t).start()

    for c, h in rings:
        pl.semaphore_signal(ring_sem.at[0], inc=1, device_id=(c, h), device_id_type=MESH)

    def vup_in(i, c):
        v = vup_raw[pl.ds(i * 8, 8)].astype(F32).reshape(128, 128)
        s_buf[i // 8, pl.ds((i % 8) * 128, 128), :] = v
        return c

    def cot_in(i, c):
        s_buf[8 + i // 8, pl.ds((i % 8) * 128, 128), :] = cot_raw[pl.ds(i * 8, 8)].astype(F32).reshape(128, 128)
        return c

    def head_up(h, c):
        for cc in range(8):
            vup_h[h, cc * 64:(cc + 1) * 64, :] = s_buf[cc, pl.ds(h, 64, stride=16), :].astype(BF16)
        cot = jnp.concatenate(
            [s_buf[8, pl.ds(h, 64, stride=16), :], s_buf[9, pl.ds(h, 64, stride=16), :]], axis=0
        ).astype(BF16)
        cot_h[h] = cot
        v = vup_h[h]
        vup_t[h] = v.T
        do_t[:, pl.ds(pl.multiple_of(h * 128, 128), 128)] = dot(v, cot.T).astype(BF16)
        return c

    def head_q(h, c):
        q_copy(h).wait()
        cols = pl.ds(pl.multiple_of(h * 128, 128), 128)
        lower, upper = q_t[512:544, cols].astype(F32), q_t[544:576, cols].astype(F32)
        q_t[512:544, cols] = (lower * tab[0] - upper * tab[1]).astype(BF16)
        q_t[544:576, cols] = (upper * tab[0] + lower * tab[1]).astype(BF16)
        return c

    def cx_copy(hg):
        return rcopy(
            cot_h.at[4 * hg + 1 - a], cotx.at[hg, pl.ds(pl.multiple_of(128 * a, 128), 128)],
            cx_s.at[hg], cx_r.at[hg], partner, head,
        )

    def cx_got(hg):
        ref = cotx.at[hg, pl.ds(pl.multiple_of(128 - 128 * a, 128), 128)]
        return rcopy(ref, ref, cx_s.at[hg], cx_r.at[hg], partner, head)

    def y_head(r, y2):
        return 4 * (2 * r + y2 // 2) + 2 + y2 % 2

    def cy_copy(r, t):
        y2 = (y + t) % 4
        return rcopy(
            cot_h.at[y_head(r, y2)], coty.at[r, pl.ds(pl.multiple_of(128 * y, 128), 128)],
            cy_s.at[r, t], cy_r.at[r, y], y2 * 16 + ctx % 16, head,
        )

    def cy_got(r, t):
        y2 = (y + t) % 4
        ref = coty.at[r, pl.ds(pl.multiple_of(128 * y2, 128), 128)]
        return rcopy(ref, ref, cy_s.at[r, t], cy_r.at[r, y2], y2 * 16 + ctx % 16, head)

    def score_group(g):
        rows = slice(g * 256, g * 256 + 256)

        def qk(r, c):
            s = dot(kw[rows, :], q_t[:, r * 512:r * 512 + 512])
            for j in range(4):
                h = r * 4 + j
                x = s[:, j * 128:(j + 1) * 128] * (SCALE * LOG2E) + bias[rows, :]
                s_buf[h, rows, :] = x
                top = jnp.max(x.reshape(32, 8, 128), axis=0)
                peak[h] = top if g == 3 else jnp.maximum(peak[h], top)
            return c

        for r in range(4):
            qk(r, 0)
        for w in (2 * g, 2 * g + 1):
            if w < 7:
                k_t[:, w * 128:(w + 1) * 128] = kw[w * 128:(w + 1) * 128, :].T

    in_copies[1].wait()
    lax.fori_loop(0, 64, vup_in, 0)
    arrive(1)
    pass_on(0)
    in_copies[2].wait()
    lax.fori_loop(0, 16, cot_in, 0)
    lax.fori_loop(0, 6, head_up, 0)
    arrive(2)
    pass_on(1)
    lax.fori_loop(6, 12, head_up, 0)
    arrive(3)
    pass_on(2)
    lax.fori_loop(0, 16, head_q, 0)
    for w in range(8):
        back = 896 - w * 128 + lane - sub
        bias[w * 128:(w + 1) * 128, :] = jnp.where((back >= 0) & (back <= pos_ref[...]), 0.0, -jnp.inf)
    arrive(4)
    lax.fori_loop(12, 16, head_up, 0)
    complete(0)
    complete(1)
    score_group(3)
    pass_on(3)
    complete(2)
    pl.semaphore_wait(ring_sem.at[0], 4)
    for c, h in rings[2:]:
        pl.semaphore_signal(ring_sem.at[1], inc=1, device_id=(c, h), device_id_type=MESH)
    score_group(2)
    pass_on(4)
    complete(3)
    pl.semaphore_wait(ring_sem.at[1], 2)
    for c, h in rings[2:]:
        pl.semaphore_signal(ring_sem.at[2], inc=1, device_id=(c, h), device_id_type=MESH)
    score_group(1)
    complete(4)
    score_group(0)
    pl.semaphore_wait(ring_sem.at[2], 2)

    for hg in range(4):
        cx_copy(hg).start()
        cotx[hg, pl.ds(pl.multiple_of(128 * a, 128), 128), :] = cot_h[4 * hg + a]
    for r in range(2):
        for t in range(1, 4):
            cy_copy(r, t).start()
        coty[r, pl.ds(pl.multiple_of(128 * y, 128), 128), :] = cot_h[y_head(r, y)]

    def ox_copy(hg):
        cols = pl.ds(pl.multiple_of(128 * a, 128), 128)
        return rcopy(o_buf.at[4 * hg + 1 - a], ox.at[hg, :, cols], ox_s.at[hg], ox_r.at[hg], partner, head)

    def ox_got(hg):
        ref = ox.at[hg, :, pl.ds(pl.multiple_of(128 - 128 * a, 128), 128)]
        return rcopy(ref, ref, ox_s.at[hg], ox_r.at[hg], partner, head)

    def oy_copy(hg, j):
        y2 = 2 * (hg % 2) + j
        cols = pl.ds(pl.multiple_of(128 * y, 128), 128)
        return rcopy(
            o_buf.at[4 * hg + 2 + j], oy.at[hg // 2, :, cols], oy_s.at[hg, j], oy_r.at[hg // 2, y],
            y_index(y2), head,
        )

    def oy_got(r, t):
        y2 = (y + t) % 4
        ref = oy.at[r, :, pl.ds(pl.multiple_of(128 * y2, 128), 128)]
        return rcopy(ref, ref, oy_s.at[2 * r, 0], oy_r.at[r, y2], y_index(y2), head)

    def xy_copy(hg, t):
        y2 = (y + t) % 4
        rows = pl.ds(pl.multiple_of(128 * y2, 128), 128)
        return rcopy(
            xs.at[hg, rows], rxy.at[hg, t - 1], xy_s.at[hg, t - 1], xy_r.at[hg, t - 1], y_index(y2), head
        )

    def yx_copy(r):
        return rcopy(ysb.at[r, 1 - a], ryx.at[r], yx_s.at[r], yx_r.at[r], partner, head)

    def z_copy(r, t):
        z2 = (z + t) % 8
        return rcopy(
            zs.at[r, z2], rz.at[r, t - 1], rz_s.at[r, t - 1], rz_r.at[r, t - 1], y * 16 + z2 * 2 + a, head
        )

    def fx_copy(r):
        return rcopy(fxs.at[r], fxr.at[r], fx_s.at[r], fx_r.at[r], partner, head)

    def fy_copy(r, t):
        y2 = (y + t) % 4
        rows = pl.ds(pl.multiple_of(8 * y2, 8), 8)
        return rcopy(fys.at[r, rows], fyr.at[r, t - 1], fy_s.at[r, t - 1], fy_r.at[r, t - 1], y_index(y2), head)

    def x_second(hg):
        ox_got(hg).wait_recv()
        cx_got(hg).wait_recv()
        total = dot(ox[hg], cotx[hg])
        dxf[hg] = total
        xs[hg] = total.astype(BF16)
        for t in range(1, 4):
            xy_copy(hg, t).start()

    def y_second(r):
        for t in range(1, 4):
            oy_got(r, t).wait_recv()
            cy_got(r, t).wait_recv()
        total = dot(oy[r], coty[r]).reshape(32, 2, 8, 128)
        for half in range(2):
            part = total[:, half].reshape(256, 128)
            ysf[r, half] = part
            ysb[r, half] = part.astype(BF16)
        yx_copy(r).start()

    def third(r):
        for j in range(2):
            hg = 2 * r + j
            for t in range(1, 4):
                xy_copy(hg, t).wait_recv()
            total = dxf[hg, pl.ds(pl.multiple_of(128 * y, 128), 128), :]
            for t in range(3):
                total = total + rxy[hg, t].astype(F32)
            zs[r, :, 16 * j:16 * j + 16, :] = total.reshape(8, 16, 128)
        yx_copy(r).wait_recv()
        total = (ysf[r, a] + ryx[r].astype(F32)).reshape(4, 8, 8, 128)
        for y2 in range(4):
            zs[r, :, 32 + 8 * y2:40 + 8 * y2, :] = total[y2]
        for t in range(1, 8):
            z_copy(r, t).start()

    def fourth(r):
        for t in range(1, 8):
            z_copy(r, t).wait_recv()
        total = zs[r, z]
        for t in range(7):
            total = total + rz[r, t]
        for j in range(2):
            low, high = total[16 * j:16 * j + 8], total[16 * j + 8:16 * j + 16]
            fxs[r, 8 * j:8 * j + 8, :] = jnp.where(a == 0, high, low)
            gv[pl.ds(4 * (2 * r + j) + a, 8, stride=16), :] = jnp.where(a == 0, low, high)
        fys[r] = total[32:]
        fx_copy(r).start()
        for t in range(1, 4):
            fy_copy(r, t).start()

    def fifth(r):
        fx_copy(r).wait_recv()
        for j in range(2):
            gv[pl.ds(4 * (2 * r + j) + 1 - a, 8, stride=16), :] = fxr[r, 8 * j:8 * j + 8, :]
        for t in range(1, 4):
            fy_copy(r, t).wait_recv()
        for t in range(4):
            y2 = (y + 4 - t) % 4
            rows = fys[r, pl.ds(pl.multiple_of(8 * y, 8), 8), :] if t == 0 else fyr[r, t - 1]
            gv[pl.ds(4 * (2 * r + y2 // 2) + 2 + y2 % 2, 8, stride=16), :] = rows

    def folded(x):
        return jnp.sum(jnp.sum(x.reshape(128, 8, 128), axis=0), axis=0, keepdims=True)

    def softmax(hg):
        for h in range(4 * hg, 4 * hg + 4):
            cols = slice(128 * h, 128 * h + 128)
            e = jnp.exp2(s_buf[h] - jnp.max(peak[h], axis=0, keepdims=True))
            s_buf[h] = e
            p_buf[:, cols] = (s_buf[h] * (1.0 / folded(e))).astype(BF16)

    softmax(0)
    for hg in range(4):
        o = dot(k_t[:512, :], p_buf[:, hg * 512:hg * 512 + 512]).astype(BF16)
        for j in range(4):
            o_buf[4 * hg + j] = o[:, j * 128:(j + 1) * 128]
        if hg < 3:
            softmax(hg + 1)
        for j in range(4):
            ao[pl.ds(4 * hg + j, 128, stride=16), :] = dot(vup_t[4 * hg + j], o[:, j * 128:(j + 1) * 128]).T
        ox_copy(hg).start()
        ox[hg, :, pl.ds(pl.multiple_of(128 * a, 128), 128)] = o_buf[4 * hg + a]
        for j in range(2):
            @pl.when(y != 2 * (hg % 2) + j)
            def _():
                oy_copy(hg, j).start()

            @pl.when(y == 2 * (hg % 2) + j)
            def _():
                oy[hg // 2, :, pl.ds(pl.multiple_of(128 * y, 128), 128)] = o_buf[4 * hg + 2 + j]

    def attn16(i, c):
        cot_raw[pl.ds(i * 8, 8)] = ao[pl.ds(i * 128, 128), :].reshape(8, 16, 128).astype(BF16)
        return c

    lax.fori_loop(0, 16, attn16, 0)
    outs = [pltpu.make_async_copy(cot_raw, attn_hbm, out_sem.at[0])]
    outs[0].start()

    def score_grads(hg):
        for j in range(4):
            cols = slice((4 * hg + j) * 128, (4 * hg + j + 1) * 128)
            if j % 2 == 0:
                two = dot(kw[:, :512], do_t[:, hg * 512 + j * 128:hg * 512 + j * 128 + 256]) * SCALE
            dp = two[:, (j % 2) * 128:(j % 2) * 128 + 128]
            dp_buf[:, j * 128:(j + 1) * 128] = dp
            delta = folded(p_buf[:, cols].astype(F32) * dp)
            p = p_buf[:, cols].astype(F32)
            ds_buf[:, cols] = (p * (dp_buf[:, j * 128:(j + 1) * 128] - delta)).astype(BF16)

    def half_rows(cc):
        return pl.ds(pl.multiple_of(288 * cc, 16), 288)

    def quarter_rows(hi2):
        return pl.ds(pl.multiple_of(144 * hi2, 16), 144)

    def dc_copy(g):
        return rcopy(dks.at[pl.ds(2 * g, 2), half_rows(1 - core)], dcore.at[g], dc_s.at[g], dc_r.at[g], ctx, sibling)

    def dx_copy(d, t):
        x2, a2, hi2 = chip_at(t)
        slot = 7 - (2 * d + a - a2) if d < 4 else 0
        return rcopy(
            csb.at[slot, quarter_rows(hi2)], drow.at[d, chip], dx_s.at[d, t], dx_r.at[d, chip],
            row * 2 + a2, hi2 * 2 + core,
        )

    def dx_got(d, t):
        x2, a2, hi2 = chip_at(t)
        return rcopy(
            drow.at[d, x2], drow.at[d, x2], dx_s.at[d, t], dx_r.at[d, x2], row * 2 + a2, hi2 * 2 + core
        )

    def dz_copy(d):
        return rcopy(zsend.at[d], zrecv.at[d], dz_s.at[d], dz_r.at[d], down_row, head)

    def key_grads(g):
        rows = slice(g * 256, g * 256 + 256)
        x = dot_nt(q_t[...], ds_buf[rows, :])
        v = dot_nt(do_t[...], p_buf[rows, :])
        for i in range(2):
            part = slice(128 * i, 128 * i + 128)
            dks[2 * g + i, :512, :] = x[:512, part] + v[:, part]
            dks[2 * g + i, 512:, :] = x[512:, part]
        dc_copy(g).start()

    def chip_sum(g):
        dc_copy(g).wait_recv()
        for i in range(2):
            total = dks[2 * g + i, half_rows(core), :] + dcore[g, i]
            csf[2 * g + i] = total
            csb[2 * g + i] = total.astype(BF16)

        @pl.when(a == 1)
        def _():
            for t in (1, 3, 2):
                dx_copy(3 - g, t).start()

        @pl.when(a == 0)
        def _():
            for t in (1, 3, 2) if g > 0 else (1, 3):
                dx_copy(4 - g, t).start()
            if g == 3:
                dx_copy(0, 2).start()

    def own_part(d):
        return csf[7 - 2 * d, quarter_rows(head // 2), :]

    def row_sum(d):
        total = own_part(d)
        for t in range(1, 4):
            dx_got(d, t).wait_recv()
        for t in range(1, 4):
            total = total + drow[d, (chip + t) % 4].astype(F32)
        if d < 3:
            dz_copy(d + 1).wait_recv()
            total = total + zrecv[d + 1]
        else:
            @pl.when(a == 1)
            def _():
                dz_copy(4).wait_recv()
            total = total + zrecv[4]
        zsend[d] = total
        dz_copy(d).start()

    @pl.when(a == 0)
    def _():
        zrecv[4] = jnp.zeros((144, 128), F32)

    @pl.when(a == 1)
    def _():
        drow[0, 0] = jnp.zeros((144, 128), BF16)
        drow[0, 2] = jnp.zeros((144, 128), BF16)

    def gq_copy(h):
        return pltpu.make_async_copy(gq.at[h], gq_hbm.at[h], gq_sem.at[h])

    def dq(r, c):
        x = dot(k_t[...], ds_buf[:, pl.ds(pl.multiple_of(r * 512, 512), 512)])
        for j in range(4):
            h = r * 4 + j
            part = x[:, j * 128:(j + 1) * 128]
            lower, upper = part[512:544], part[544:576]
            gq[h, :512, :] = part[:512].astype(BF16)
            gq[h, 512:544, :] = (lower * tab[0] + upper * tab[1]).astype(BF16)
            gq[h, 544:576, :] = (upper * tab[0] - lower * tab[1]).astype(BF16)
            gq_copy(h).start()
        return c

    score_grads(0)
    score_grads(1)
    x_second(0)
    score_grads(2)
    x_second(1)
    y_second(0)
    score_grads(3)
    x_second(2)
    key_grads(0)
    key_grads(1)
    chip_sum(0)
    x_second(3)
    y_second(1)
    key_grads(2)
    chip_sum(1)

    @pl.when(a == 1)
    def _():
        for t in (1, 3):
            dx_got(4, t).wait_recv()
        zsend[4] = drow[4, 0].astype(F32) + drow[4, 2].astype(F32)
        dz_copy(4).start()

    third(0)
    key_grads(3)
    chip_sum(2)
    lax.fori_loop(0, 1, dq, 0)
    row_sum(3)
    chip_sum(3)
    lax.fori_loop(1, 2, dq, 0)
    row_sum(2)
    third(1)
    lax.fori_loop(2, 3, dq, 0)
    row_sum(1)
    lax.fori_loop(3, 4, dq, 0)

    total = own_part(0)
    for t in range(1, 4):
        x2, a2, hi2 = chip_at(t)

        @pl.when(a2 >= a)
        def _():
            dx_got(0, t).wait_recv()
    for t in range(1, 4):
        total = total + drow[0, (chip + t) % 4].astype(F32)
    dz_copy(1).wait_recv()
    total = total + zrecv[1]
    quarter = 2 * core + head // 2
    roped = quarter == 3
    cosine = jnp.where(roped, tab[0], 1.0)
    sine = jnp.where(roped, tab[1], 0.0)
    lower, upper = total[80:112], total[112:144]
    own_quarter = glt.at[pl.ds(pl.multiple_of(144 * quarter, 16), 144)]
    own_quarter[...] = jnp.concatenate(
        [total[:80], lower * cosine + upper * sine, upper * cosine - lower * sine], axis=0
    ).astype(BF16)

    def gl_copy(t):
        return rcopy(own_quarter, own_quarter, gl_s.at[t], gl_r.at[head], ctx, (head + t) % 4)

    def gl_got(t):
        h2 = (head + t) % 4
        ref = glt.at[pl.ds(pl.multiple_of(144 * (2 * (h2 % 2) + h2 // 2), 16), 144)]
        return rcopy(ref, ref, gl_s.at[t], gl_r.at[h2], ctx, h2)

    for t in range(1, 4):
        gl_copy(t).start()
    fourth(0)
    fourth(1)
    fifth(0)
    fifth(1)
    outs.append(pltpu.make_async_copy(gv, gv_hbm, out_sem.at[1]))
    outs[-1].start()

    for t in range(1, 4):
        gl_got(t).wait_recv()
    outs.append(pltpu.make_async_copy(glt, gl_hbm, out_sem.at[2]))
    outs[-1].start()

    for d in (1, 2, 3):
        kz(d).wait_send()
        for t in range(4):
            kc(d, t).wait_send()
        for t in range(1, 4):
            kx(d, t).wait_send()
            dx_copy(d, t).wait_send()
        dz_copy(d).wait_send()
    dx_copy(0, 2).wait_send()
    for g in range(4):
        dc_copy(g).wait_send()

    @pl.when(a == 1)
    def _():
        kz(4).wait_send()
        dz_copy(4).wait_send()
        for t in (1, 3):
            kx(4, t).wait_send()
            kc(0, t).wait_send()
            dx_copy(0, t).wait_send()

    @pl.when(a == 0)
    def _():
        for t in (1, 3):
            kx(0, t).wait_send()
            kc(4, t).wait_send()
            dx_copy(4, t).wait_send()

    for t in range(1, 4):
        gl_copy(t).wait_send()

    for hg in range(4):
        cx_copy(hg).wait_send()
        ox_copy(hg).wait_send()
        for t in range(1, 4):
            xy_copy(hg, t).wait_send()
        for j in range(2):
            @pl.when(y != 2 * (hg % 2) + j)
            def _():
                oy_copy(hg, j).wait_send()
    for r in range(2):
        yx_copy(r).wait_send()
        fx_copy(r).wait_send()
        for t in range(1, 4):
            cy_copy(r, t).wait_send()
            fy_copy(r, t).wait_send()
        for t in range(1, 8):
            z_copy(r, t).wait_send()
    for c in outs:
        c.wait()
    for h in range(16):
        gq_copy(h).wait()


def handed_on(attn, gq, gl, gv, attn_out, gq_out, gl_out, gv_out, sem):
    pairs = [(gq, gq_out), (attn, attn_out), (gl, gl_out), (gv, gv_out)]
    copies = [pltpu.make_async_copy(src, dst, sem.at[i]) for i, (src, dst) in enumerate(pairs)]
    for c in copies:
        c.start()
    for c in copies:
        c.wait()


def body(queries, latent_kv, positions, value_up, cotangent):
    anywhere = pl.BlockSpec(memory_space=pl.ANY)
    vmem, dma = pltpu.VMEM, pltpu.SemaphoreType.DMA
    attn, gq, gl, gv = pl.pallas_call(
        kernel,
        out_shape=(
            jax.ShapeDtypeStruct((128, 16, 128), BF16),
            jax.ShapeDtypeStruct((16, 576, 128), BF16),
            jax.ShapeDtypeStruct((576, 128), BF16),
            jax.ShapeDtypeStruct((128, 128), F32),
        ),
        in_specs=[anywhere, anywhere, pl.BlockSpec(memory_space=pltpu.VMEM), anywhere, anywhere],
        out_specs=(anywhere,) * 4,
        scratch_shapes=[
            vmem((576, 128), BF16), vmem((512, 16, 128), BF16), vmem((128, 16, 128), BF16),
            vmem((16, 576, 128), BF16), vmem((2, 32, 128), F32),
            vmem((16, 1024, 128), F32), vmem((1024, 512), F32),
            vmem((576, 2048), BF16), vmem((512, 2048), BF16),
            vmem((16, 512, 128), BF16), vmem((16, 128, 512), BF16), vmem((16, 128, 128), BF16),
            vmem((1024, 2048), BF16), vmem((1024, 2048), BF16), vmem((1024, 128), F32), vmem((16, 8, 128), F32),
            vmem((2048, 128), F32), vmem((1024, 576), BF16), vmem((576, 1024), BF16), vmem((32, 576), BF16),
            vmem((16, 512, 128), BF16), vmem((4, 512, 256), BF16), vmem((2, 512, 512), BF16),
            vmem((4, 256, 128), BF16), vmem((2, 512, 128), BF16), vmem((4, 512, 128), F32), vmem((4, 512, 128), BF16),
            vmem((4, 3, 128, 128), BF16), vmem((2, 2, 256, 128), F32), vmem((2, 2, 256, 128), BF16),
            vmem((2, 256, 128), BF16), vmem((2, 8, 64, 128), F32), vmem((2, 7, 64, 128), F32),
            vmem((2, 16, 128), F32), vmem((2, 16, 128), F32), vmem((2, 32, 128), F32), vmem((2, 3, 8, 128), F32),
            vmem((128, 128), F32),
            vmem((8, 576, 128), F32), vmem((4, 2, 288, 128), F32), vmem((8, 288, 128), F32), vmem((8, 288, 128), BF16),
            vmem((5, 4, 144, 128), BF16), vmem((5, 144, 128), F32),
            vmem((5, 144, 128), F32), vmem((576, 128), BF16),
            dma((3,)), dma((16,)), dma((3,)), dma((16,)), pltpu.SemaphoreType.REGULAR((3,)),
            dma((5,)), dma((5,)), dma((5, 4)), dma((5, 4)), dma((5, 4)), dma((5, 4)),
            dma((4,)), dma((4,)), dma((2, 4)), dma((2, 4)), dma((4,)), dma((4,)), dma((4, 2)), dma((2, 4)),
            dma((4, 3)), dma((4, 3)), dma((2,)), dma((2,)), dma((2, 7)), dma((2, 7)), dma((2,)), dma((2,)),
            dma((2, 3)), dma((2, 3)),
            dma((4,)), dma((4,)), dma((5, 4)), dma((5, 4)), dma((5,)), dma((5,)), dma((4,)), dma((4,)),
        ],
        compiler_params=pltpu.CompilerParams(
            collective_id=0, has_side_effects=True, vmem_limit_bytes=64 * 2**20 - 2**16
        ),
    )(
        jnp.transpose(queries, (1, 2, 0)), latent_kv.T, positions.reshape(1, 128), value_up, cotangent
    )
    attn, gq, gl, gv = pl.pallas_call(
        handed_on,
        out_shape=tuple(jax.ShapeDtypeStruct(x.shape, x.dtype) for x in (attn, gq, gl, gv)),
        in_specs=[pl.BlockSpec(memory_space=pltpu.VMEM)] * 4,
        out_specs=(anywhere,) * 4,
        scratch_shapes=[dma((4,))],
    )(attn, gq, gl, gv)
    return attn, jnp.transpose(gq, (2, 0, 1)), gl.T, gv.reshape(8, 16, 128)


def solution(mesh):
    in_specs = (
        P("ctx", "head", None),
        P("ctx", None),
        P("ctx"),
        P(None, "head", None),
        P("ctx", "head", None),
    )
    out_specs = (
        P("ctx", "head", None),
        P("ctx", "head", None),
        P("ctx", None),
        P("ctx", "head", None),
    )
    return jax.shard_map(body, mesh=mesh, in_specs=in_specs, out_specs=out_specs, check_vma=False)
```

```python
import math

import jax
import jax.numpy as jnp
import numpy as np
from jax import lax
from jax.experimental import pallas as pl
from jax.experimental.pallas import tpu as pltpu
from jax.sharding import PartitionSpec as P

F32, BF16 = jnp.float32, jnp.bfloat16
MESH = pl.DeviceIdType.MESH
SCALE = 1.0 / math.sqrt(192.0)
LOG2E = 1.4426950408889634
FREQUENCY = [
    float(f) for f in np.asarray(10000.0 ** (-2.0 * np.arange(32, dtype=np.float32) / 64), np.float32)
]


def dot(a, b):
    return jnp.dot(a, b, preferred_element_type=F32)


def dot_nt(a, b):
    return lax.dot_general(a, b, (((1,), (1,)), ((), ())), preferred_element_type=F32)


def kernel(
    q_hbm, lat_hbm, pos_ref, vup_hbm, cot_hbm,
    attn_hbm, gq_hbm, gl_hbm, gv_hbm,
    lat_raw, vup_raw, cot_raw, gq, tab, s_buf, dp_buf, q_t, do_t, vup_h, vup_t, cot_h,
    p_buf, ds_buf, bias, peak, ao, kw, k_t, k4,
    o_buf, ox, oy, cotx, coty, dxf, xs, rxy, ysf, ysb, ryx, zs, rz, fxs, fxr, fys, fyr, gv,
    dks, dcore, csf, csb, drow, zsend, zrecv, glt,
    in_sem, q_sem, out_sem, gq_sem, ring_sem, kz_s, kz_r, kx_s, kx_r, kc_s, kc_r,
    cx_s, cx_r, cy_s, cy_r, ox_s, ox_r, oy_s, oy_r, xy_s, xy_r, yx_s, yx_r, rz_s, rz_r, fx_s, fx_r, fy_s, fy_r,
    dc_s, dc_r, dx_s, dx_r, dz_s, dz_r, gl_s, gl_r,
):
    ctx, head = lax.axis_index("ctx"), lax.axis_index("head")
    a, row = ctx % 2, ctx // 2
    y, z = ctx // 16, (ctx // 2) % 8
    partner = ctx + 1 - 2 * a

    def rcopy(src, dst, ss, rs, to_ctx, to_head):
        return pltpu.make_async_remote_copy(
            src_ref=src, dst_ref=dst, send_sem=ss, recv_sem=rs,
            device_id=(to_ctx, to_head), device_id_type=MESH,
        )

    in_copies = [
        pltpu.make_async_copy(src, dst, in_sem.at[i])
        for i, (src, dst) in enumerate(((lat_hbm, lat_raw), (vup_hbm, vup_raw), (cot_hbm, cot_raw)))
    ]
    for c in in_copies:
        c.start()

    def q_copy(h):
        cols = pl.ds(pl.multiple_of(h * 128, 128), 128)
        return pltpu.make_async_copy(q_hbm.at[h], q_t.at[:, cols], q_sem.at[h])

    for h in range(16):
        q_copy(h).start()

    core, chip = head % 2, (head // 2) * 2 + a

    def chip_at(t):
        x2 = (chip + t) % 4
        return x2, x2 % 2, x2 // 2

    def on_chip(t):
        x2, a2, hi2 = chip_at(t)
        return row * 2 + a2, hi2 * 2 + core

    def y_index(y2):
        return (y2 % 4) * 16 + ctx % 16

    def z_index(z2):
        return y * 16 + (z2 % 8) * 2 + a

    sibling = head + 1 - 2 * core
    up_row, down_row = (ctx + 2) % 64, (ctx + 62) % 64
    rings = [(y_index(y + 1), head), (y_index(y + 3), head), (z_index(z + 1), head), (z_index(z + 7), head)]
    partners = [on_chip(t) for t in range(1, 4)] + [(ctx, sibling), (up_row, head), (down_row, head)] + rings
    barrier = pltpu.get_barrier_semaphore()
    for c, h in partners:
        pl.semaphore_signal(barrier, inc=1, device_id=(c, h), device_id_type=MESH)

    lane = lax.broadcasted_iota(jnp.int32, (128, 128), 1)
    sub = lax.broadcasted_iota(jnp.int32, (128, 128), 0)
    frequency = jnp.zeros((32, 128), F32)
    for i in range(32):
        frequency = jnp.where(sub[:32] == i, FREQUENCY[i], frequency)
    angle = pos_ref[...].astype(F32) * frequency
    tab[0] = jnp.cos(angle)
    tab[1] = jnp.sin(angle)

    in_copies[0].wait()
    own = 7 * 128
    k_t[:512, own:own + 128] = lat_raw[:512, :]
    lower, upper = lat_raw[512:544, :].astype(F32), lat_raw[544:576, :].astype(F32)
    k_t[512:544, own:own + 128] = (lower * tab[0] - upper * tab[1]).astype(BF16)
    k_t[544:576, own:own + 128] = (upper * tab[0] + lower * tab[1]).astype(BF16)
    kw[own:own + 128, :] = k_t[:, own:own + 128].T

    pl.semaphore_wait(barrier, len(partners))

    def krows(slot, h):
        return kw.at[pl.ds(pl.multiple_of(slot * 128 + h * 32, 32), 32)]

    def kz(d):
        src = krows(9 - 2 * d, head)
        dst = krows(7 - 2 * d, head) if d < 4 else k4
        return rcopy(src, dst, kz_s.at[d], kz_r.at[d], up_row, head)

    def kz_got(d):
        ref = krows(7 - 2 * d, head) if d < 4 else k4
        return rcopy(ref, ref, kz_s.at[d], kz_r.at[d], down_row, head)

    def kx(d, t):
        x2, a2, hi2 = chip_at(t)
        src = krows(7 - 2 * d, head) if d < 4 else k4
        dst = krows(7 - (2 * d + a2 - a), head) if d < 4 else krows(0, head)
        return rcopy(src, dst, kx_s.at[d, t], kx_r.at[d, chip], row * 2 + a2, hi2 * 2 + core)

    def kpiece(d, x2, cc):
        slot = 7 - (2 * d + a - x2 % 2) if d < 4 else 0
        return krows(slot, (x2 // 2) * 2 + cc)

    def kx_got(d, t):
        x2, a2, hi2 = chip_at(t)
        ref = kpiece(d, x2, core)
        return rcopy(ref, ref, kx_s.at[d, t], kx_r.at[d, x2], row * 2 + a2, hi2 * 2 + core)

    def kc(d, t):
        x2, a2, hi2 = chip_at(t)
        ref = kpiece(d, x2, core)
        return rcopy(ref, ref, kc_s.at[d, x2], kc_r.at[d, x2], ctx, sibling)

    def kc_got(d, t):
        x2, a2, hi2 = chip_at(t)
        ref = kpiece(d, x2, 1 - core)
        return rcopy(ref, ref, kc_s.at[d, x2], kc_r.at[d, x2], ctx, sibling)

    def arrive(d):
        if d < 4:
            kz_got(d).wait_recv()
            if d < 3:
                kz(d + 1).start()
            else:
                @pl.when(a == 1)
                def _():
                    kz(4).start()
            for t in (1, 3, 2):
                kx(d, t).start()
            kc(d, 0).start()
        else:
            @pl.when(a == 1)
            def _():
                kz_got(4).wait_recv()
                for t in (1, 3):
                    kx(4, t).start()

    def pass_on(d):
        if d in (1, 2, 3):
            for t in (1, 3, 2):
                kx_got(d, t).wait_recv()
                kc(d, t).start()
        else:
            @pl.when(a == (1 if d == 0 else 0))
            def _():
                for t in (1, 3):
                    kx_got(d, t).wait_recv()
                    kc(d, t).start()

    def complete(d):
        if d in (1, 2, 3):
            for t in range(4):
                kc_got(d, t).wait_recv()
        else:
            @pl.when(a == (1 if d == 0 else 0))
            def _():
                for t in (1, 3):
                    kc_got(d, t).wait_recv()

    kz(1).start()

    @pl.when(a == 0)
    def _():
        for t in (1, 3):
            kx(0, t).start()

    for c, h in rings:
        pl.semaphore_signal(ring_sem.at[0], inc=1, device_id=(c, h), device_id_type=MESH)

    def vup_in(i, c):
        v = vup_raw[pl.ds(i * 8, 8)].astype(F32).reshape(128, 128)
        s_buf[i // 8, pl.ds((i % 8) * 128, 128), :] = v
        return c

    def cot_in(i, c):
        s_buf[8 + i // 8, pl.ds((i % 8) * 128, 128), :] = cot_raw[pl.ds(i * 8, 8)].astype(F32).reshape(128, 128)
        return c

    def head_up(h, c):
        for cc in range(8):
            vup_h[h, cc * 64:(cc + 1) * 64, :] = s_buf[cc, pl.ds(h, 64, stride=16), :].astype(BF16)
        cot = jnp.concatenate(
            [s_buf[8, pl.ds(h, 64, stride=16), :], s_buf[9, pl.ds(h, 64, stride=16), :]], axis=0
        ).astype(BF16)
        cot_h[h] = cot
        v = vup_h[h]
        vup_t[h] = v.T
        do_t[:, pl.ds(pl.multiple_of(h * 128, 128), 128)] = dot(v, cot.T).astype(BF16)
        return c

    def head_q(h, c):
        q_copy(h).wait()
        cols = pl.ds(pl.multiple_of(h * 128, 128), 128)
        lower, upper = q_t[512:544, cols].astype(F32), q_t[544:576, cols].astype(F32)
        q_t[512:544, cols] = (lower * tab[0] - upper * tab[1]).astype(BF16)
        q_t[544:576, cols] = (upper * tab[0] + lower * tab[1]).astype(BF16)
        return c

    def cx_copy(hg):
        return rcopy(
            cot_h.at[4 * hg + 1 - a], cotx.at[hg, pl.ds(pl.multiple_of(128 * a, 128), 128)],
            cx_s.at[hg], cx_r.at[hg], partner, head,
        )

    def cx_got(hg):
        ref = cotx.at[hg, pl.ds(pl.multiple_of(128 - 128 * a, 128), 128)]
        return rcopy(ref, ref, cx_s.at[hg], cx_r.at[hg], partner, head)

    def y_head(r, y2):
        return 4 * (2 * r + y2 // 2) + 2 + y2 % 2

    def cy_copy(r, t):
        y2 = (y + t) % 4
        return rcopy(
            cot_h.at[y_head(r, y2)], coty.at[r, pl.ds(pl.multiple_of(128 * y, 128), 128)],
            cy_s.at[r, t], cy_r.at[r, y], y2 * 16 + ctx % 16, head,
        )

    def cy_got(r, t):
        y2 = (y + t) % 4
        ref = coty.at[r, pl.ds(pl.multiple_of(128 * y2, 128), 128)]
        return rcopy(ref, ref, cy_s.at[r, t], cy_r.at[r, y2], y2 * 16 + ctx % 16, head)

    def score_group(g):
        rows = slice(g * 256, g * 256 + 256)

        def qk(r, c):
            s = dot(kw[rows, :], q_t[:, r * 512:r * 512 + 512])
            for j in range(4):
                h = r * 4 + j
                x = s[:, j * 128:(j + 1) * 128] * (SCALE * LOG2E) + bias[rows, :]
                s_buf[h, rows, :] = x
                top = jnp.max(x.reshape(32, 8, 128), axis=0)
                peak[h] = top if g == 3 else jnp.maximum(peak[h], top)
            return c

        for r in range(4):
            qk(r, 0)
        for w in (2 * g, 2 * g + 1):
            if w < 7:
                k_t[:, w * 128:(w + 1) * 128] = kw[w * 128:(w + 1) * 128, :].T

    arrive(1)
    in_copies[1].wait()
    lax.fori_loop(0, 32, vup_in, 0)
    arrive(2)
    pass_on(0)
    lax.fori_loop(32, 64, vup_in, 0)
    pass_on(1)
    arrive(3)
    in_copies[2].wait()
    lax.fori_loop(0, 16, cot_in, 0)
    lax.fori_loop(0, 4, head_up, 0)
    pass_on(2)
    arrive(4)
    lax.fori_loop(4, 10, head_up, 0)
    pass_on(3)
    lax.fori_loop(10, 16, head_up, 0)
    pass_on(4)
    lax.fori_loop(0, 16, head_q, 0)
    for w in range(8):
        back = 896 - w * 128 + lane - sub
        bias[w * 128:(w + 1) * 128, :] = jnp.where((back >= 0) & (back <= pos_ref[...]), 0.0, -jnp.inf)
    complete(0)
    complete(1)
    score_group(3)
    complete(2)
    pl.semaphore_wait(ring_sem.at[0], 4)
    for hg in range(4):
        cx_copy(hg).start()
        cotx[hg, pl.ds(pl.multiple_of(128 * a, 128), 128), :] = cot_h[4 * hg + a]
    for r in range(2):
        for t in range(1, 4):
            cy_copy(r, t).start()
        coty[r, pl.ds(pl.multiple_of(128 * y, 128), 128), :] = cot_h[y_head(r, y)]
    for c, h in rings[2:]:
        pl.semaphore_signal(ring_sem.at[1], inc=1, device_id=(c, h), device_id_type=MESH)
    score_group(2)
    complete(3)
    pl.semaphore_wait(ring_sem.at[1], 2)
    for c, h in rings[2:]:
        pl.semaphore_signal(ring_sem.at[2], inc=1, device_id=(c, h), device_id_type=MESH)
    score_group(1)
    complete(4)
    score_group(0)
    pl.semaphore_wait(ring_sem.at[2], 2)

    def ox_copy(hg):
        cols = pl.ds(pl.multiple_of(128 * a, 128), 128)
        return rcopy(o_buf.at[4 * hg + 1 - a], ox.at[hg, :, cols], ox_s.at[hg], ox_r.at[hg], partner, head)

    def ox_got(hg):
        ref = ox.at[hg, :, pl.ds(pl.multiple_of(128 - 128 * a, 128), 128)]
        return rcopy(ref, ref, ox_s.at[hg], ox_r.at[hg], partner, head)

    def oy_copy(hg, j):
        y2 = 2 * (hg % 2) + j
        cols = pl.ds(pl.multiple_of(128 * y, 128), 128)
        return rcopy(
            o_buf.at[4 * hg + 2 + j], oy.at[hg // 2, :, cols], oy_s.at[hg, j], oy_r.at[hg // 2, y],
            y_index(y2), head,
        )

    def oy_got(r, t):
        y2 = (y + t) % 4
        ref = oy.at[r, :, pl.ds(pl.multiple_of(128 * y2, 128), 128)]
        return rcopy(ref, ref, oy_s.at[2 * r, 0], oy_r.at[r, y2], y_index(y2), head)

    def xy_copy(hg, t):
        y2 = (y + t) % 4
        rows = pl.ds(pl.multiple_of(128 * y2, 128), 128)
        return rcopy(
            xs.at[hg, rows], rxy.at[hg, t - 1], xy_s.at[hg, t - 1], xy_r.at[hg, t - 1], y_index(y2), head
        )

    def yx_copy(r):
        return rcopy(ysb.at[r, 1 - a], ryx.at[r], yx_s.at[r], yx_r.at[r], partner, head)

    def z_copy(r, t):
        z2 = (z + t) % 8
        return rcopy(
            zs.at[r, z2], rz.at[r, t - 1], rz_s.at[r, t - 1], rz_r.at[r, t - 1], y * 16 + z2 * 2 + a, head
        )

    def fx_copy(r):
        return rcopy(fxs.at[r], fxr.at[r], fx_s.at[r], fx_r.at[r], partner, head)

    def fy_copy(r, t):
        y2 = (y + t) % 4
        rows = pl.ds(pl.multiple_of(8 * y2, 8), 8)
        return rcopy(fys.at[r, rows], fyr.at[r, t - 1], fy_s.at[r, t - 1], fy_r.at[r, t - 1], y_index(y2), head)

    def x_second(hg):
        ox_got(hg).wait_recv()
        cx_got(hg).wait_recv()
        total = dot(ox[hg], cotx[hg])
        dxf[hg] = total
        xs[hg] = total.astype(BF16)
        for t in range(1, 4):
            xy_copy(hg, t).start()

    def y_second(r):
        for t in range(1, 4):
            oy_got(r, t).wait_recv()
            cy_got(r, t).wait_recv()
        total = dot(oy[r], coty[r]).reshape(32, 2, 8, 128)
        for half in range(2):
            part = total[:, half].reshape(256, 128)
            ysf[r, half] = part
            ysb[r, half] = part.astype(BF16)
        yx_copy(r).start()

    def third(r):
        for j in range(2):
            hg = 2 * r + j
            for t in range(1, 4):
                xy_copy(hg, t).wait_recv()
            total = dxf[hg, pl.ds(pl.multiple_of(128 * y, 128), 128), :]
            for t in range(3):
                total = total + rxy[hg, t].astype(F32)
            zs[r, :, 16 * j:16 * j + 16, :] = total.reshape(8, 16, 128)
        yx_copy(r).wait_recv()
        total = (ysf[r, a] + ryx[r].astype(F32)).reshape(4, 8, 8, 128)
        for y2 in range(4):
            zs[r, :, 32 + 8 * y2:40 + 8 * y2, :] = total[y2]
        for t in range(1, 8):
            z_copy(r, t).start()

    def fourth(r):
        for t in range(1, 8):
            z_copy(r, t).wait_recv()
        total = zs[r, z]
        for t in range(7):
            total = total + rz[r, t]
        for j in range(2):
            low, high = total[16 * j:16 * j + 8], total[16 * j + 8:16 * j + 16]
            fxs[r, 8 * j:8 * j + 8, :] = jnp.where(a == 0, high, low)
            gv[pl.ds(4 * (2 * r + j) + a, 8, stride=16), :] = jnp.where(a == 0, low, high)
        fys[r] = total[32:]
        fx_copy(r).start()
        for t in range(1, 4):
            fy_copy(r, t).start()

    def fifth(r):
        fx_copy(r).wait_recv()
        for j in range(2):
            gv[pl.ds(4 * (2 * r + j) + 1 - a, 8, stride=16), :] = fxr[r, 8 * j:8 * j + 8, :]
        for t in range(1, 4):
            fy_copy(r, t).wait_recv()
        for t in range(4):
            y2 = (y + 4 - t) % 4
            rows = fys[r, pl.ds(pl.multiple_of(8 * y, 8), 8), :] if t == 0 else fyr[r, t - 1]
            gv[pl.ds(4 * (2 * r + y2 // 2) + 2 + y2 % 2, 8, stride=16), :] = rows

    def folded(x):
        return jnp.sum(jnp.sum(x.reshape(128, 8, 128), axis=0), axis=0, keepdims=True)

    def softmax(hg):
        for h in range(4 * hg, 4 * hg + 4):
            cols = slice(128 * h, 128 * h + 128)
            e = jnp.exp2(s_buf[h] - jnp.max(peak[h], axis=0, keepdims=True))
            s_buf[h] = e
            p_buf[:, cols] = (s_buf[h] * (1.0 / folded(e))).astype(BF16)

    softmax(0)
    for hg in range(4):
        o = dot(k_t[:512, :], p_buf[:, hg * 512:hg * 512 + 512]).astype(BF16)
        for j in range(4):
            o_buf[4 * hg + j] = o[:, j * 128:(j + 1) * 128]
        if hg < 3:
            softmax(hg + 1)
        for j in range(4):
            ao[pl.ds(4 * hg + j, 128, stride=16), :] = dot(vup_t[4 * hg + j], o[:, j * 128:(j + 1) * 128]).T
        ox_copy(hg).start()
        ox[hg, :, pl.ds(pl.multiple_of(128 * a, 128), 128)] = o_buf[4 * hg + a]
        for j in range(2):
            @pl.when(y != 2 * (hg % 2) + j)
            def _():
                oy_copy(hg, j).start()

            @pl.when(y == 2 * (hg % 2) + j)
            def _():
                oy[hg // 2, :, pl.ds(pl.multiple_of(128 * y, 128), 128)] = o_buf[4 * hg + 2 + j]

    def attn16(i, c):
        cot_raw[pl.ds(i * 8, 8)] = ao[pl.ds(i * 128, 128), :].reshape(8, 16, 128).astype(BF16)
        return c

    lax.fori_loop(0, 16, attn16, 0)
    outs = [pltpu.make_async_copy(cot_raw, attn_hbm, out_sem.at[0])]
    outs[0].start()

    def score_grads(hg):
        for j in range(4):
            cols = slice((4 * hg + j) * 128, (4 * hg + j + 1) * 128)
            if j % 2 == 0:
                two = dot(kw[:, :512], do_t[:, hg * 512 + j * 128:hg * 512 + j * 128 + 256]) * SCALE
            dp = two[:, (j % 2) * 128:(j % 2) * 128 + 128]
            dp_buf[:, j * 128:(j + 1) * 128] = dp
            delta = folded(p_buf[:, cols].astype(F32) * dp)
            p = p_buf[:, cols].astype(F32)
            ds_buf[:, cols] = (p * (dp_buf[:, j * 128:(j + 1) * 128] - delta)).astype(BF16)

    def half_rows(cc):
        return pl.ds(pl.multiple_of(288 * cc, 16), 288)

    def quarter_rows(hi2):
        return pl.ds(pl.multiple_of(144 * hi2, 16), 144)

    def dc_copy(g):
        return rcopy(dks.at[pl.ds(2 * g, 2), half_rows(1 - core)], dcore.at[g], dc_s.at[g], dc_r.at[g], ctx, sibling)

    def dx_copy(d, t):
        x2, a2, hi2 = chip_at(t)
        slot = 7 - (2 * d + a - a2) if d < 4 else 0
        return rcopy(
            csb.at[slot, quarter_rows(hi2)], drow.at[d, chip], dx_s.at[d, t], dx_r.at[d, chip],
            row * 2 + a2, hi2 * 2 + core,
        )

    def dx_got(d, t):
        x2, a2, hi2 = chip_at(t)
        return rcopy(
            drow.at[d, x2], drow.at[d, x2], dx_s.at[d, t], dx_r.at[d, x2], row * 2 + a2, hi2 * 2 + core
        )

    def dz_copy(d):
        return rcopy(zsend.at[d], zrecv.at[d], dz_s.at[d], dz_r.at[d], down_row, head)

    def key_grads(g):
        rows = slice(g * 256, g * 256 + 256)
        x = dot_nt(q_t[...], ds_buf[rows, :])
        v = dot_nt(do_t[...], p_buf[rows, :])
        for i in range(2):
            part = slice(128 * i, 128 * i + 128)
            dks[2 * g + i, :512, :] = x[:512, part] + v[:, part]
            dks[2 * g + i, 512:, :] = x[512:, part]
        dc_copy(g).start()

    def chip_sum(g):
        dc_copy(g).wait_recv()
        for i in range(2):
            total = dks[2 * g + i, half_rows(core), :] + dcore[g, i]
            csf[2 * g + i] = total
            csb[2 * g + i] = total.astype(BF16)

        @pl.when(a == 1)
        def _():
            for t in (1, 3, 2):
                dx_copy(3 - g, t).start()

        @pl.when(a == 0)
        def _():
            for t in (1, 3, 2) if g > 0 else (1, 3):
                dx_copy(4 - g, t).start()
            if g == 3:
                dx_copy(0, 2).start()

    def own_part(d):
        return csf[7 - 2 * d, quarter_rows(head // 2), :]

    def row_sum(d):
        total = own_part(d)
        for t in range(1, 4):
            dx_got(d, t).wait_recv()
        for t in range(1, 4):
            total = total + drow[d, (chip + t) % 4].astype(F32)
        if d < 3:
            dz_copy(d + 1).wait_recv()
            total = total + zrecv[d + 1]
        else:
            @pl.when(a == 1)
            def _():
                dz_copy(4).wait_recv()
            total = total + zrecv[4]
        zsend[d] = total
        dz_copy(d).start()

    @pl.when(a == 0)
    def _():
        zrecv[4] = jnp.zeros((144, 128), F32)

    @pl.when(a == 1)
    def _():
        drow[0, 0] = jnp.zeros((144, 128), BF16)
        drow[0, 2] = jnp.zeros((144, 128), BF16)

    def gq_copy(h):
        return pltpu.make_async_copy(gq.at[h], gq_hbm.at[h], gq_sem.at[h])

    def dq(r, c):
        x = dot(k_t[...], ds_buf[:, pl.ds(pl.multiple_of(r * 512, 512), 512)])
        for j in range(4):
            h = r * 4 + j
            part = x[:, j * 128:(j + 1) * 128]
            lower, upper = part[512:544], part[544:576]
            gq[h, :512, :] = part[:512].astype(BF16)
            gq[h, 512:544, :] = (lower * tab[0] + upper * tab[1]).astype(BF16)
            gq[h, 544:576, :] = (upper * tab[0] - lower * tab[1]).astype(BF16)
            gq_copy(h).start()
        return c

    score_grads(0)
    score_grads(1)
    x_second(0)
    score_grads(2)
    x_second(1)
    y_second(0)
    score_grads(3)
    x_second(2)
    key_grads(0)
    key_grads(1)
    chip_sum(0)
    key_grads(2)
    chip_sum(1)
    key_grads(3)
    x_second(3)
    chip_sum(2)

    @pl.when(a == 1)
    def _():
        for t in (1, 3):
            dx_got(4, t).wait_recv()
        zsend[4] = drow[4, 0].astype(F32) + drow[4, 2].astype(F32)
        dz_copy(4).start()

    lax.fori_loop(0, 1, dq, 0)
    chip_sum(3)
    row_sum(3)
    y_second(1)
    lax.fori_loop(1, 2, dq, 0)
    third(0)
    row_sum(2)
    lax.fori_loop(2, 3, dq, 0)
    row_sum(1)
    third(1)
    lax.fori_loop(3, 4, dq, 0)

    total = own_part(0)
    for t in range(1, 4):
        x2, a2, hi2 = chip_at(t)

        @pl.when(a2 >= a)
        def _():
            dx_got(0, t).wait_recv()
    for t in range(1, 4):
        total = total + drow[0, (chip + t) % 4].astype(F32)
    dz_copy(1).wait_recv()
    total = total + zrecv[1]
    quarter = 2 * core + head // 2
    roped = quarter == 3
    cosine = jnp.where(roped, tab[0], 1.0)
    sine = jnp.where(roped, tab[1], 0.0)
    lower, upper = total[80:112], total[112:144]
    own_quarter = glt.at[pl.ds(pl.multiple_of(144 * quarter, 16), 144)]
    own_quarter[...] = jnp.concatenate(
        [total[:80], lower * cosine + upper * sine, upper * cosine - lower * sine], axis=0
    ).astype(BF16)

    def gl_copy(t):
        return rcopy(own_quarter, own_quarter, gl_s.at[t], gl_r.at[head], ctx, (head + t) % 4)

    def gl_got(t):
        h2 = (head + t) % 4
        ref = glt.at[pl.ds(pl.multiple_of(144 * (2 * (h2 % 2) + h2 // 2), 16), 144)]
        return rcopy(ref, ref, gl_s.at[t], gl_r.at[h2], ctx, h2)

    for t in range(1, 4):
        gl_copy(t).start()
    fourth(0)
    fourth(1)
    fifth(0)
    fifth(1)
    outs.append(pltpu.make_async_copy(gv, gv_hbm, out_sem.at[1]))
    outs[-1].start()

    for t in range(1, 4):
        gl_got(t).wait_recv()
    outs.append(pltpu.make_async_copy(glt, gl_hbm, out_sem.at[2]))
    outs[-1].start()

    for d in (1, 2, 3):
        kz(d).wait_send()
        for t in range(4):
            kc(d, t).wait_send()
        for t in range(1, 4):
            kx(d, t).wait_send()
            dx_copy(d, t).wait_send()
        dz_copy(d).wait_send()
    dx_copy(0, 2).wait_send()
    for g in range(4):
        dc_copy(g).wait_send()

    @pl.when(a == 1)
    def _():
        kz(4).wait_send()
        dz_copy(4).wait_send()
        for t in (1, 3):
            kx(4, t).wait_send()
            kc(0, t).wait_send()
            dx_copy(0, t).wait_send()

    @pl.when(a == 0)
    def _():
        for t in (1, 3):
            kx(0, t).wait_send()
            kc(4, t).wait_send()
            dx_copy(4, t).wait_send()

    for t in range(1, 4):
        gl_copy(t).wait_send()

    for hg in range(4):
        cx_copy(hg).wait_send()
        ox_copy(hg).wait_send()
        for t in range(1, 4):
            xy_copy(hg, t).wait_send()
        for j in range(2):
            @pl.when(y != 2 * (hg % 2) + j)
            def _():
                oy_copy(hg, j).wait_send()
    for r in range(2):
        yx_copy(r).wait_send()
        fx_copy(r).wait_send()
        for t in range(1, 4):
            cy_copy(r, t).wait_send()
            fy_copy(r, t).wait_send()
        for t in range(1, 8):
            z_copy(r, t).wait_send()
    for c in outs:
        c.wait()
    for h in range(16):
        gq_copy(h).wait()


def handed_on(attn, gq, gl, gv, attn_out, gq_out, gl_out, gv_out, sem):
    pairs = [(gq, gq_out), (attn, attn_out), (gl, gl_out), (gv, gv_out)]
    copies = [pltpu.make_async_copy(src, dst, sem.at[i]) for i, (src, dst) in enumerate(pairs)]
    for c in copies:
        c.start()
    for c in copies:
        c.wait()


def body(queries, latent_kv, positions, value_up, cotangent):
    anywhere = pl.BlockSpec(memory_space=pl.ANY)
    vmem, dma = pltpu.VMEM, pltpu.SemaphoreType.DMA
    attn, gq, gl, gv = pl.pallas_call(
        kernel,
        out_shape=(
            jax.ShapeDtypeStruct((128, 16, 128), BF16),
            jax.ShapeDtypeStruct((16, 576, 128), BF16),
            jax.ShapeDtypeStruct((576, 128), BF16),
            jax.ShapeDtypeStruct((128, 128), F32),
        ),
        in_specs=[anywhere, anywhere, pl.BlockSpec(memory_space=pltpu.VMEM), anywhere, anywhere],
        out_specs=(anywhere,) * 4,
        scratch_shapes=[
            vmem((576, 128), BF16), vmem((512, 16, 128), BF16), vmem((128, 16, 128), BF16),
            vmem((16, 576, 128), BF16), vmem((2, 32, 128), F32),
            vmem((16, 1024, 128), F32), vmem((1024, 512), F32),
            vmem((576, 2048), BF16), vmem((512, 2048), BF16),
            vmem((16, 512, 128), BF16), vmem((16, 128, 512), BF16), vmem((16, 128, 128), BF16),
            vmem((1024, 2048), BF16), vmem((1024, 2048), BF16), vmem((1024, 128), F32), vmem((16, 8, 128), F32),
            vmem((2048, 128), F32), vmem((1024, 576), BF16), vmem((576, 1024), BF16), vmem((32, 576), BF16),
            vmem((16, 512, 128), BF16), vmem((4, 512, 256), BF16), vmem((2, 512, 512), BF16),
            vmem((4, 256, 128), BF16), vmem((2, 512, 128), BF16), vmem((4, 512, 128), F32), vmem((4, 512, 128), BF16),
            vmem((4, 3, 128, 128), BF16), vmem((2, 2, 256, 128), F32), vmem((2, 2, 256, 128), BF16),
            vmem((2, 256, 128), BF16), vmem((2, 8, 64, 128), F32), vmem((2, 7, 64, 128), F32),
            vmem((2, 16, 128), F32), vmem((2, 16, 128), F32), vmem((2, 32, 128), F32), vmem((2, 3, 8, 128), F32),
            vmem((128, 128), F32),
            vmem((8, 576, 128), F32), vmem((4, 2, 288, 128), F32), vmem((8, 288, 128), F32), vmem((8, 288, 128), BF16),
            vmem((5, 4, 144, 128), BF16), vmem((5, 144, 128), F32),
            vmem((5, 144, 128), F32), vmem((576, 128), BF16),
            dma((3,)), dma((16,)), dma((3,)), dma((16,)), pltpu.SemaphoreType.REGULAR((3,)),
            dma((5,)), dma((5,)), dma((5, 4)), dma((5, 4)), dma((5, 4)), dma((5, 4)),
            dma((4,)), dma((4,)), dma((2, 4)), dma((2, 4)), dma((4,)), dma((4,)), dma((4, 2)), dma((2, 4)),
            dma((4, 3)), dma((4, 3)), dma((2,)), dma((2,)), dma((2, 7)), dma((2, 7)), dma((2,)), dma((2,)),
            dma((2, 3)), dma((2, 3)),
            dma((4,)), dma((4,)), dma((5, 4)), dma((5, 4)), dma((5,)), dma((5,)), dma((4,)), dma((4,)),
        ],
        compiler_params=pltpu.CompilerParams(
            collective_id=0, has_side_effects=True, vmem_limit_bytes=64 * 2**20 - 2**16
        ),
    )(
        jnp.transpose(queries, (1, 2, 0)), latent_kv.T, positions.reshape(1, 128), value_up, cotangent
    )
    attn, gq, gl, gv = pl.pallas_call(
        handed_on,
        out_shape=tuple(jax.ShapeDtypeStruct(x.shape, x.dtype) for x in (attn, gq, gl, gv)),
        in_specs=[pl.BlockSpec(memory_space=pltpu.VMEM)] * 4,
        out_specs=(anywhere,) * 4,
        scratch_shapes=[dma((4,))],
    )(attn, gq, gl, gv)
    return attn, jnp.transpose(gq, (2, 0, 1)), gl.T, gv.reshape(8, 16, 128)


def solution(mesh):
    in_specs = (
        P("ctx", "head", None),
        P("ctx", None),
        P("ctx"),
        P(None, "head", None),
        P("ctx", "head", None),
    )
    out_specs = (
        P("ctx", "head", None),
        P("ctx", "head", None),
        P("ctx", None),
        P("ctx", "head", None),
    )
    return jax.shard_map(body, mesh=mesh, in_specs=in_specs, out_specs=out_specs, check_vma=False)
```

```python
import math

import jax
import jax.numpy as jnp
import numpy as np
from jax import lax
from jax.experimental import pallas as pl
from jax.experimental.pallas import tpu as pltpu
from jax.sharding import PartitionSpec as P

F32, BF16 = jnp.float32, jnp.bfloat16
MESH = pl.DeviceIdType.MESH
SCALE = 1.0 / math.sqrt(192.0)
LOG2E = 1.4426950408889634
FREQUENCY = [
    float(f) for f in np.asarray(10000.0 ** (-2.0 * np.arange(32, dtype=np.float32) / 64), np.float32)
]


def dot(a, b):
    return jnp.dot(a, b, preferred_element_type=F32)


def dot_nt(a, b):
    return lax.dot_general(a, b, (((1,), (1,)), ((), ())), preferred_element_type=F32)


def kernel(
    q_hbm, lat_hbm, pos_ref, vup_hbm, cot_hbm,
    attn_hbm, gq_hbm, gl_hbm, gv_hbm,
    lat_raw, vup_raw, cot_raw, gq, tab, s_buf, dp_buf, q_t, do_t, vup_h, vup_t, cot_h,
    p_buf, ds_buf, bias, peak, ao, kw, k_t, k4,
    o_buf, ox, oy, cotx, coty, dxf, xs, rxy, ysf, ysb, ryx, zs, rz, fxs, fxr, fys, fyr, gv,
    dks, dcore, csf, csb, drow, zsend, zrecv, glt,
    in_sem, q_sem, out_sem, gq_sem, ring_sem, kz_s, kz_r, kx_s, kx_r, kc_s, kc_r,
    cx_s, cx_r, cy_s, cy_r, ox_s, ox_r, oy_s, oy_r, xy_s, xy_r, yx_s, yx_r, rz_s, rz_r, fx_s, fx_r, fy_s, fy_r,
    dc_s, dc_r, dx_s, dx_r, dz_s, dz_r, gl_s, gl_r,
):
    ctx, head = lax.axis_index("ctx"), lax.axis_index("head")
    a, row = ctx % 2, ctx // 2
    y, z = ctx // 16, (ctx // 2) % 8
    partner = ctx + 1 - 2 * a

    def rcopy(src, dst, ss, rs, to_ctx, to_head):
        return pltpu.make_async_remote_copy(
            src_ref=src, dst_ref=dst, send_sem=ss, recv_sem=rs,
            device_id=(to_ctx, to_head), device_id_type=MESH,
        )

    in_copies = [
        pltpu.make_async_copy(src, dst, in_sem.at[i])
        for i, (src, dst) in enumerate(((lat_hbm, lat_raw), (vup_hbm, vup_raw), (cot_hbm, cot_raw)))
    ]
    for c in in_copies:
        c.start()

    def q_copy(h):
        cols = pl.ds(pl.multiple_of(h * 128, 128), 128)
        return pltpu.make_async_copy(q_hbm.at[h], q_t.at[:, cols], q_sem.at[h])

    for h in range(16):
        q_copy(h).start()

    core, chip = head % 2, (head // 2) * 2 + a

    def chip_at(t):
        x2 = (chip + t) % 4
        return x2, x2 % 2, x2 // 2

    def on_chip(t):
        x2, a2, hi2 = chip_at(t)
        return row * 2 + a2, hi2 * 2 + core

    def y_index(y2):
        return (y2 % 4) * 16 + ctx % 16

    def z_index(z2):
        return y * 16 + (z2 % 8) * 2 + a

    sibling = head + 1 - 2 * core
    up_row, down_row = (ctx + 2) % 64, (ctx + 62) % 64
    rings = [(y_index(y + 1), head), (y_index(y + 3), head), (z_index(z + 1), head), (z_index(z + 7), head)]
    partners = [on_chip(t) for t in range(1, 4)] + [(ctx, sibling), (up_row, head), (down_row, head)] + rings
    barrier = pltpu.get_barrier_semaphore()
    for c, h in partners:
        pl.semaphore_signal(barrier, inc=1, device_id=(c, h), device_id_type=MESH)

    lane = lax.broadcasted_iota(jnp.int32, (128, 128), 1)
    sub = lax.broadcasted_iota(jnp.int32, (128, 128), 0)
    frequency = jnp.zeros((32, 128), F32)
    for i in range(32):
        frequency = jnp.where(sub[:32] == i, FREQUENCY[i], frequency)
    angle = pos_ref[...].astype(F32) * frequency
    tab[0] = jnp.cos(angle)
    tab[1] = jnp.sin(angle)

    in_copies[0].wait()
    own = 7 * 128
    k_t[:512, own:own + 128] = lat_raw[:512, :]
    lower, upper = lat_raw[512:544, :].astype(F32), lat_raw[544:576, :].astype(F32)
    k_t[512:544, own:own + 128] = (lower * tab[0] - upper * tab[1]).astype(BF16)
    k_t[544:576, own:own + 128] = (upper * tab[0] + lower * tab[1]).astype(BF16)
    kw[own:own + 128, :] = k_t[:, own:own + 128].T

    pl.semaphore_wait(barrier, len(partners))

    def krows(slot, h):
        return kw.at[pl.ds(pl.multiple_of(slot * 128 + h * 32, 32), 32)]

    def kz(d):
        src = krows(9 - 2 * d, head)
        dst = krows(7 - 2 * d, head) if d < 4 else k4
        return rcopy(src, dst, kz_s.at[d], kz_r.at[d], up_row, head)

    def kz_got(d):
        ref = krows(7 - 2 * d, head) if d < 4 else k4
        return rcopy(ref, ref, kz_s.at[d], kz_r.at[d], down_row, head)

    def kx(d, t):
        x2, a2, hi2 = chip_at(t)
        src = krows(7 - 2 * d, head) if d < 4 else k4
        dst = krows(7 - (2 * d + a2 - a), head) if d < 4 else krows(0, head)
        return rcopy(src, dst, kx_s.at[d, t], kx_r.at[d, chip], row * 2 + a2, hi2 * 2 + core)

    def kpiece(d, x2, cc):
        slot = 7 - (2 * d + a - x2 % 2) if d < 4 else 0
        return krows(slot, (x2 // 2) * 2 + cc)

    def kx_got(d, t):
        x2, a2, hi2 = chip_at(t)
        ref = kpiece(d, x2, core)
        return rcopy(ref, ref, kx_s.at[d, t], kx_r.at[d, x2], row * 2 + a2, hi2 * 2 + core)

    def kc(d, t):
        x2, a2, hi2 = chip_at(t)
        ref = kpiece(d, x2, core)
        return rcopy(ref, ref, kc_s.at[d, x2], kc_r.at[d, x2], ctx, sibling)

    def kc_got(d, t):
        x2, a2, hi2 = chip_at(t)
        ref = kpiece(d, x2, 1 - core)
        return rcopy(ref, ref, kc_s.at[d, x2], kc_r.at[d, x2], ctx, sibling)

    def arrive(d):
        if d < 4:
            kz_got(d).wait_recv()
            if d < 3:
                kz(d + 1).start()
            else:
                @pl.when(a == 1)
                def _():
                    kz(4).start()
            for t in (1, 3, 2):
                kx(d, t).start()
            kc(d, 0).start()
        else:
            @pl.when(a == 1)
            def _():
                kz_got(4).wait_recv()
                for t in (1, 3):
                    kx(4, t).start()

    def pass_on(d):
        if d in (1, 2, 3):
            for t in (1, 3, 2):
                kx_got(d, t).wait_recv()
                kc(d, t).start()
        else:
            @pl.when(a == (1 if d == 0 else 0))
            def _():
                for t in (1, 3):
                    kx_got(d, t).wait_recv()
                    kc(d, t).start()

    def complete(d):
        if d in (1, 2, 3):
            for t in range(4):
                kc_got(d, t).wait_recv()
        else:
            @pl.when(a == (1 if d == 0 else 0))
            def _():
                for t in (1, 3):
                    kc_got(d, t).wait_recv()

    kz(1).start()

    @pl.when(a == 0)
    def _():
        for t in (1, 3):
            kx(0, t).start()

    for c, h in rings:
        pl.semaphore_signal(ring_sem.at[0], inc=1, device_id=(c, h), device_id_type=MESH)

    def vup_in(i, c):
        v = vup_raw[pl.ds(i * 8, 8)].astype(F32).reshape(128, 128)
        s_buf[i // 8, pl.ds((i % 8) * 128, 128), :] = v
        return c

    def cot_in(i, c):
        s_buf[8 + i // 8, pl.ds((i % 8) * 128, 128), :] = cot_raw[pl.ds(i * 8, 8)].astype(F32).reshape(128, 128)
        return c

    def head_up(h, c):
        for cc in range(8):
            vup_h[h, cc * 64:(cc + 1) * 64, :] = s_buf[cc, pl.ds(h, 64, stride=16), :].astype(BF16)
        cot = jnp.concatenate(
            [s_buf[8, pl.ds(h, 64, stride=16), :], s_buf[9, pl.ds(h, 64, stride=16), :]], axis=0
        ).astype(BF16)
        cot_h[h] = cot
        v = vup_h[h]
        vup_t[h] = v.T
        do_t[:, pl.ds(pl.multiple_of(h * 128, 128), 128)] = dot(v, cot.T).astype(BF16)
        return c

    def head_q(h, c):
        q_copy(h).wait()
        cols = pl.ds(pl.multiple_of(h * 128, 128), 128)
        lower, upper = q_t[512:544, cols].astype(F32), q_t[544:576, cols].astype(F32)
        q_t[512:544, cols] = (lower * tab[0] - upper * tab[1]).astype(BF16)
        q_t[544:576, cols] = (upper * tab[0] + lower * tab[1]).astype(BF16)
        return c

    def cx_copy(hg):
        return rcopy(
            cot_h.at[4 * hg + 1 - a], cotx.at[hg, pl.ds(pl.multiple_of(128 * a, 128), 128)],
            cx_s.at[hg], cx_r.at[hg], partner, head,
        )

    def cx_got(hg):
        ref = cotx.at[hg, pl.ds(pl.multiple_of(128 - 128 * a, 128), 128)]
        return rcopy(ref, ref, cx_s.at[hg], cx_r.at[hg], partner, head)

    def y_head(r, y2):
        return 4 * (2 * r + y2 // 2) + 2 + y2 % 2

    def cy_copy(r, t):
        y2 = (y + t) % 4
        return rcopy(
            cot_h.at[y_head(r, y2)], coty.at[r, pl.ds(pl.multiple_of(128 * y, 128), 128)],
            cy_s.at[r, t], cy_r.at[r, y], y2 * 16 + ctx % 16, head,
        )

    def cy_got(r, t):
        y2 = (y + t) % 4
        ref = coty.at[r, pl.ds(pl.multiple_of(128 * y2, 128), 128)]
        return rcopy(ref, ref, cy_s.at[r, t], cy_r.at[r, y2], y2 * 16 + ctx % 16, head)

    def score_group(g):
        rows = slice(g * 256, g * 256 + 256)

        def qk(r, c):
            s = dot(kw[rows, :], q_t[:, r * 512:r * 512 + 512])
            for j in range(4):
                h = r * 4 + j
                x = s[:, j * 128:(j + 1) * 128] * (SCALE * LOG2E) + bias[rows, :]
                s_buf[h, rows, :] = x
                top = jnp.max(x.reshape(32, 8, 128), axis=0)
                peak[h] = top if g == 3 else jnp.maximum(peak[h], top)
            return c

        for r in range(4):
            qk(r, 0)
        for w in (2 * g, 2 * g + 1):
            if w < 7:
                k_t[:, w * 128:(w + 1) * 128] = kw[w * 128:(w + 1) * 128, :].T

    arrive(1)
    in_copies[1].wait()
    lax.fori_loop(0, 32, vup_in, 0)
    arrive(2)
    pass_on(0)
    lax.fori_loop(32, 64, vup_in, 0)
    pass_on(1)
    arrive(3)
    in_copies[2].wait()
    lax.fori_loop(0, 16, cot_in, 0)
    lax.fori_loop(0, 4, head_up, 0)
    pass_on(2)
    arrive(4)
    lax.fori_loop(4, 10, head_up, 0)
    lax.fori_loop(10, 16, head_up, 0)
    lax.fori_loop(0, 16, head_q, 0)
    for w in range(8):
        back = 896 - w * 128 + lane - sub
        bias[w * 128:(w + 1) * 128, :] = jnp.where((back >= 0) & (back <= pos_ref[...]), 0.0, -jnp.inf)
    complete(0)
    complete(1)
    pass_on(3)
    score_group(3)
    pass_on(4)
    complete(2)
    pl.semaphore_wait(ring_sem.at[0], 4)
    for c, h in rings[2:]:
        pl.semaphore_signal(ring_sem.at[1], inc=1, device_id=(c, h), device_id_type=MESH)
    score_group(2)
    complete(3)
    pl.semaphore_wait(ring_sem.at[1], 2)
    for c, h in rings[2:]:
        pl.semaphore_signal(ring_sem.at[2], inc=1, device_id=(c, h), device_id_type=MESH)
    score_group(1)
    complete(4)
    score_group(0)
    pl.semaphore_wait(ring_sem.at[2], 2)
    for hg in range(4):
        cx_copy(hg).start()
        cotx[hg, pl.ds(pl.multiple_of(128 * a, 128), 128), :] = cot_h[4 * hg + a]
    for r in range(2):
        for t in range(1, 4):
            cy_copy(r, t).start()
        coty[r, pl.ds(pl.multiple_of(128 * y, 128), 128), :] = cot_h[y_head(r, y)]

    def ox_copy(hg):
        cols = pl.ds(pl.multiple_of(128 * a, 128), 128)
        return rcopy(o_buf.at[4 * hg + 1 - a], ox.at[hg, :, cols], ox_s.at[hg], ox_r.at[hg], partner, head)

    def ox_got(hg):
        ref = ox.at[hg, :, pl.ds(pl.multiple_of(128 - 128 * a, 128), 128)]
        return rcopy(ref, ref, ox_s.at[hg], ox_r.at[hg], partner, head)

    def oy_copy(hg, j):
        y2 = 2 * (hg % 2) + j
        cols = pl.ds(pl.multiple_of(128 * y, 128), 128)
        return rcopy(
            o_buf.at[4 * hg + 2 + j], oy.at[hg // 2, :, cols], oy_s.at[hg, j], oy_r.at[hg // 2, y],
            y_index(y2), head,
        )

    def oy_got(r, t):
        y2 = (y + t) % 4
        ref = oy.at[r, :, pl.ds(pl.multiple_of(128 * y2, 128), 128)]
        return rcopy(ref, ref, oy_s.at[2 * r, 0], oy_r.at[r, y2], y_index(y2), head)

    def xy_copy(hg, t):
        y2 = (y + t) % 4
        rows = pl.ds(pl.multiple_of(128 * y2, 128), 128)
        return rcopy(
            xs.at[hg, rows], rxy.at[hg, t - 1], xy_s.at[hg, t - 1], xy_r.at[hg, t - 1], y_index(y2), head
        )

    def yx_copy(r):
        return rcopy(ysb.at[r, 1 - a], ryx.at[r], yx_s.at[r], yx_r.at[r], partner, head)

    def z_copy(r, t):
        z2 = (z + t) % 8
        return rcopy(
            zs.at[r, z2], rz.at[r, t - 1], rz_s.at[r, t - 1], rz_r.at[r, t - 1], y * 16 + z2 * 2 + a, head
        )

    def fx_copy(r):
        return rcopy(fxs.at[r], fxr.at[r], fx_s.at[r], fx_r.at[r], partner, head)

    def fy_copy(r, t):
        y2 = (y + t) % 4
        rows = pl.ds(pl.multiple_of(8 * y2, 8), 8)
        return rcopy(fys.at[r, rows], fyr.at[r, t - 1], fy_s.at[r, t - 1], fy_r.at[r, t - 1], y_index(y2), head)

    def x_second(hg):
        ox_got(hg).wait_recv()
        cx_got(hg).wait_recv()
        total = dot(ox[hg], cotx[hg])
        dxf[hg] = total
        xs[hg] = total.astype(BF16)
        for t in range(1, 4):
            xy_copy(hg, t).start()

    def y_second(r):
        for t in range(1, 4):
            oy_got(r, t).wait_recv()
            cy_got(r, t).wait_recv()
        total = dot(oy[r], coty[r]).reshape(32, 2, 8, 128)
        for half in range(2):
            part = total[:, half].reshape(256, 128)
            ysf[r, half] = part
            ysb[r, half] = part.astype(BF16)
        yx_copy(r).start()

    def third(r):
        for j in range(2):
            hg = 2 * r + j
            for t in range(1, 4):
                xy_copy(hg, t).wait_recv()
            total = dxf[hg, pl.ds(pl.multiple_of(128 * y, 128), 128), :]
            for t in range(3):
                total = total + rxy[hg, t].astype(F32)
            zs[r, :, 16 * j:16 * j + 16, :] = total.reshape(8, 16, 128)
        yx_copy(r).wait_recv()
        total = (ysf[r, a] + ryx[r].astype(F32)).reshape(4, 8, 8, 128)
        for y2 in range(4):
            zs[r, :, 32 + 8 * y2:40 + 8 * y2, :] = total[y2]
        for t in range(1, 8):
            z_copy(r, t).start()

    def fourth(r):
        for t in range(1, 8):
            z_copy(r, t).wait_recv()
        total = zs[r, z]
        for t in range(7):
            total = total + rz[r, t]
        for j in range(2):
            low, high = total[16 * j:16 * j + 8], total[16 * j + 8:16 * j + 16]
            fxs[r, 8 * j:8 * j + 8, :] = jnp.where(a == 0, high, low)
            gv[pl.ds(4 * (2 * r + j) + a, 8, stride=16), :] = jnp.where(a == 0, low, high)
        fys[r] = total[32:]
        fx_copy(r).start()
        for t in range(1, 4):
            fy_copy(r, t).start()

    def fifth(r):
        fx_copy(r).wait_recv()
        for j in range(2):
            gv[pl.ds(4 * (2 * r + j) + 1 - a, 8, stride=16), :] = fxr[r, 8 * j:8 * j + 8, :]
        for t in range(1, 4):
            fy_copy(r, t).wait_recv()
        for t in range(4):
            y2 = (y + 4 - t) % 4
            rows = fys[r, pl.ds(pl.multiple_of(8 * y, 8), 8), :] if t == 0 else fyr[r, t - 1]
            gv[pl.ds(4 * (2 * r + y2 // 2) + 2 + y2 % 2, 8, stride=16), :] = rows

    def folded(x):
        return jnp.sum(jnp.sum(x.reshape(128, 8, 128), axis=0), axis=0, keepdims=True)

    def softmax(hg):
        for h in range(4 * hg, 4 * hg + 4):
            cols = slice(128 * h, 128 * h + 128)
            e = jnp.exp2(s_buf[h] - jnp.max(peak[h], axis=0, keepdims=True))
            s_buf[h] = e
            p_buf[:, cols] = (s_buf[h] * (1.0 / folded(e))).astype(BF16)

    softmax(0)
    for hg in range(4):
        o = dot(k_t[:512, :], p_buf[:, hg * 512:hg * 512 + 512]).astype(BF16)
        for j in range(4):
            o_buf[4 * hg + j] = o[:, j * 128:(j + 1) * 128]
        if hg < 3:
            softmax(hg + 1)
        for j in range(4):
            ao[pl.ds(4 * hg + j, 128, stride=16), :] = dot(vup_t[4 * hg + j], o[:, j * 128:(j + 1) * 128]).T
        ox_copy(hg).start()
        ox[hg, :, pl.ds(pl.multiple_of(128 * a, 128), 128)] = o_buf[4 * hg + a]
        for j in range(2):
            @pl.when(y != 2 * (hg % 2) + j)
            def _():
                oy_copy(hg, j).start()

            @pl.when(y == 2 * (hg % 2) + j)
            def _():
                oy[hg // 2, :, pl.ds(pl.multiple_of(128 * y, 128), 128)] = o_buf[4 * hg + 2 + j]

    def attn16(i, c):
        cot_raw[pl.ds(i * 8, 8)] = ao[pl.ds(i * 128, 128), :].reshape(8, 16, 128).astype(BF16)
        return c

    lax.fori_loop(0, 16, attn16, 0)
    outs = [pltpu.make_async_copy(cot_raw, attn_hbm, out_sem.at[0])]
    outs[0].start()

    def score_grads(hg):
        for j in range(4):
            cols = slice((4 * hg + j) * 128, (4 * hg + j + 1) * 128)
            if j % 2 == 0:
                two = dot(kw[:, :512], do_t[:, hg * 512 + j * 128:hg * 512 + j * 128 + 256]) * SCALE
            dp = two[:, (j % 2) * 128:(j % 2) * 128 + 128]
            dp_buf[:, j * 128:(j + 1) * 128] = dp
            delta = folded(p_buf[:, cols].astype(F32) * dp)
            p = p_buf[:, cols].astype(F32)
            ds_buf[:, cols] = (p * (dp_buf[:, j * 128:(j + 1) * 128] - delta)).astype(BF16)

    def half_rows(cc):
        return pl.ds(pl.multiple_of(288 * cc, 16), 288)

    def quarter_rows(hi2):
        return pl.ds(pl.multiple_of(144 * hi2, 16), 144)

    def dc_copy(g):
        return rcopy(dks.at[pl.ds(2 * g, 2), half_rows(1 - core)], dcore.at[g], dc_s.at[g], dc_r.at[g], ctx, sibling)

    def dx_copy(d, t):
        x2, a2, hi2 = chip_at(t)
        slot = 7 - (2 * d + a - a2) if d < 4 else 0
        return rcopy(
            csb.at[slot, quarter_rows(hi2)], drow.at[d, chip], dx_s.at[d, t], dx_r.at[d, chip],
            row * 2 + a2, hi2 * 2 + core,
        )

    def dx_got(d, t):
        x2, a2, hi2 = chip_at(t)
        return rcopy(
            drow.at[d, x2], drow.at[d, x2], dx_s.at[d, t], dx_r.at[d, x2], row * 2 + a2, hi2 * 2 + core
        )

    def dz_copy(d):
        return rcopy(zsend.at[d], zrecv.at[d], dz_s.at[d], dz_r.at[d], down_row, head)

    def key_grads(g):
        rows = slice(g * 256, g * 256 + 256)
        x = dot_nt(q_t[...], ds_buf[rows, :])
        v = dot_nt(do_t[...], p_buf[rows, :])
        for i in range(2):
            part = slice(128 * i, 128 * i + 128)
            dks[2 * g + i, :512, :] = x[:512, part] + v[:, part]
            dks[2 * g + i, 512:, :] = x[512:, part]
        dc_copy(g).start()

    def chip_sum(g):
        dc_copy(g).wait_recv()
        for i in range(2):
            total = dks[2 * g + i, half_rows(core), :] + dcore[g, i]
            csf[2 * g + i] = total
            csb[2 * g + i] = total.astype(BF16)

        @pl.when(a == 1)
        def _():
            for t in (1, 3, 2):
                dx_copy(3 - g, t).start()

        @pl.when(a == 0)
        def _():
            for t in (1, 3, 2) if g > 0 else (1, 3):
                dx_copy(4 - g, t).start()
            if g == 3:
                dx_copy(0, 2).start()

    def own_part(d):
        return csf[7 - 2 * d, quarter_rows(head // 2), :]

    def row_sum(d):
        total = own_part(d)
        for t in range(1, 4):
            dx_got(d, t).wait_recv()
        for t in range(1, 4):
            total = total + drow[d, (chip + t) % 4].astype(F32)
        if d < 3:
            dz_copy(d + 1).wait_recv()
            total = total + zrecv[d + 1]
        else:
            @pl.when(a == 1)
            def _():
                dz_copy(4).wait_recv()
            total = total + zrecv[4]
        zsend[d] = total
        dz_copy(d).start()

    @pl.when(a == 0)
    def _():
        zrecv[4] = jnp.zeros((144, 128), F32)

    @pl.when(a == 1)
    def _():
        drow[0, 0] = jnp.zeros((144, 128), BF16)
        drow[0, 2] = jnp.zeros((144, 128), BF16)

    def gq_copy(h):
        return pltpu.make_async_copy(gq.at[h], gq_hbm.at[h], gq_sem.at[h])

    def dq(r, c):
        x = dot(k_t[...], ds_buf[:, pl.ds(pl.multiple_of(r * 512, 512), 512)])
        for j in range(4):
            h = r * 4 + j
            part = x[:, j * 128:(j + 1) * 128]
            lower, upper = part[512:544], part[544:576]
            gq[h, :512, :] = part[:512].astype(BF16)
            gq[h, 512:544, :] = (lower * tab[0] + upper * tab[1]).astype(BF16)
            gq[h, 544:576, :] = (upper * tab[0] - lower * tab[1]).astype(BF16)
            gq_copy(h).start()
        return c

    score_grads(0)
    score_grads(1)
    x_second(0)
    score_grads(2)
    x_second(1)
    y_second(0)
    score_grads(3)
    x_second(2)
    key_grads(0)
    key_grads(1)
    chip_sum(0)
    key_grads(2)
    chip_sum(1)
    key_grads(3)
    x_second(3)
    chip_sum(2)

    @pl.when(a == 1)
    def _():
        for t in (1, 3):
            dx_got(4, t).wait_recv()
        zsend[4] = drow[4, 0].astype(F32) + drow[4, 2].astype(F32)
        dz_copy(4).start()

    lax.fori_loop(0, 1, dq, 0)
    chip_sum(3)
    row_sum(3)
    y_second(1)
    lax.fori_loop(1, 2, dq, 0)
    third(0)
    row_sum(2)
    lax.fori_loop(2, 3, dq, 0)
    row_sum(1)
    third(1)
    lax.fori_loop(3, 4, dq, 0)

    total = own_part(0)
    for t in range(1, 4):
        x2, a2, hi2 = chip_at(t)

        @pl.when(a2 >= a)
        def _():
            dx_got(0, t).wait_recv()
    for t in range(1, 4):
        total = total + drow[0, (chip + t) % 4].astype(F32)
    dz_copy(1).wait_recv()
    total = total + zrecv[1]
    quarter = 2 * core + head // 2
    roped = quarter == 3
    cosine = jnp.where(roped, tab[0], 1.0)
    sine = jnp.where(roped, tab[1], 0.0)
    lower, upper = total[80:112], total[112:144]
    own_quarter = glt.at[pl.ds(pl.multiple_of(144 * quarter, 16), 144)]
    own_quarter[...] = jnp.concatenate(
        [total[:80], lower * cosine + upper * sine, upper * cosine - lower * sine], axis=0
    ).astype(BF16)

    def gl_copy(t):
        return rcopy(own_quarter, own_quarter, gl_s.at[t], gl_r.at[head], ctx, (head + t) % 4)

    def gl_got(t):
        h2 = (head + t) % 4
        ref = glt.at[pl.ds(pl.multiple_of(144 * (2 * (h2 % 2) + h2 // 2), 16), 144)]
        return rcopy(ref, ref, gl_s.at[t], gl_r.at[h2], ctx, h2)

    for t in range(1, 4):
        gl_copy(t).start()
    fourth(0)
    fourth(1)
    fifth(0)
    fifth(1)
    outs.append(pltpu.make_async_copy(gv, gv_hbm, out_sem.at[1]))
    outs[-1].start()

    for t in range(1, 4):
        gl_got(t).wait_recv()
    outs.append(pltpu.make_async_copy(glt, gl_hbm, out_sem.at[2]))
    outs[-1].start()

    for d in (1, 2, 3):
        kz(d).wait_send()
        for t in range(4):
            kc(d, t).wait_send()
        for t in range(1, 4):
            kx(d, t).wait_send()
            dx_copy(d, t).wait_send()
        dz_copy(d).wait_send()
    dx_copy(0, 2).wait_send()
    for g in range(4):
        dc_copy(g).wait_send()

    @pl.when(a == 1)
    def _():
        kz(4).wait_send()
        dz_copy(4).wait_send()
        for t in (1, 3):
            kx(4, t).wait_send()
            kc(0, t).wait_send()
            dx_copy(0, t).wait_send()

    @pl.when(a == 0)
    def _():
        for t in (1, 3):
            kx(0, t).wait_send()
            kc(4, t).wait_send()
            dx_copy(4, t).wait_send()

    for t in range(1, 4):
        gl_copy(t).wait_send()

    for hg in range(4):
        cx_copy(hg).wait_send()
        ox_copy(hg).wait_send()
        for t in range(1, 4):
            xy_copy(hg, t).wait_send()
        for j in range(2):
            @pl.when(y != 2 * (hg % 2) + j)
            def _():
                oy_copy(hg, j).wait_send()
    for r in range(2):
        yx_copy(r).wait_send()
        fx_copy(r).wait_send()
        for t in range(1, 4):
            cy_copy(r, t).wait_send()
            fy_copy(r, t).wait_send()
        for t in range(1, 8):
            z_copy(r, t).wait_send()
    for c in outs:
        c.wait()
    for h in range(16):
        gq_copy(h).wait()


def handed_on(attn, gq, gl, gv, attn_out, gq_out, gl_out, gv_out, sem):
    pairs = [(gq, gq_out), (attn, attn_out), (gl, gl_out), (gv, gv_out)]
    copies = [pltpu.make_async_copy(src, dst, sem.at[i]) for i, (src, dst) in enumerate(pairs)]
    for c in copies:
        c.start()
    for c in copies:
        c.wait()


def body(queries, latent_kv, positions, value_up, cotangent):
    anywhere = pl.BlockSpec(memory_space=pl.ANY)
    vmem, dma = pltpu.VMEM, pltpu.SemaphoreType.DMA
    attn, gq, gl, gv = pl.pallas_call(
        kernel,
        out_shape=(
            jax.ShapeDtypeStruct((128, 16, 128), BF16),
            jax.ShapeDtypeStruct((16, 576, 128), BF16),
            jax.ShapeDtypeStruct((576, 128), BF16),
            jax.ShapeDtypeStruct((128, 128), F32),
        ),
        in_specs=[anywhere, anywhere, pl.BlockSpec(memory_space=pltpu.VMEM), anywhere, anywhere],
        out_specs=(anywhere,) * 4,
        scratch_shapes=[
            vmem((576, 128), BF16), vmem((512, 16, 128), BF16), vmem((128, 16, 128), BF16),
            vmem((16, 576, 128), BF16), vmem((2, 32, 128), F32),
            vmem((16, 1024, 128), F32), vmem((1024, 512), F32),
            vmem((576, 2048), BF16), vmem((512, 2048), BF16),
            vmem((16, 512, 128), BF16), vmem((16, 128, 512), BF16), vmem((16, 128, 128), BF16),
            vmem((1024, 2048), BF16), vmem((1024, 2048), BF16), vmem((1024, 128), F32), vmem((16, 8, 128), F32),
            vmem((2048, 128), F32), vmem((1024, 576), BF16), vmem((576, 1024), BF16), vmem((32, 576), BF16),
            vmem((16, 512, 128), BF16), vmem((4, 512, 256), BF16), vmem((2, 512, 512), BF16),
            vmem((4, 256, 128), BF16), vmem((2, 512, 128), BF16), vmem((4, 512, 128), F32), vmem((4, 512, 128), BF16),
            vmem((4, 3, 128, 128), BF16), vmem((2, 2, 256, 128), F32), vmem((2, 2, 256, 128), BF16),
            vmem((2, 256, 128), BF16), vmem((2, 8, 64, 128), F32), vmem((2, 7, 64, 128), F32),
            vmem((2, 16, 128), F32), vmem((2, 16, 128), F32), vmem((2, 32, 128), F32), vmem((2, 3, 8, 128), F32),
            vmem((128, 128), F32),
            vmem((8, 576, 128), F32), vmem((4, 2, 288, 128), F32), vmem((8, 288, 128), F32), vmem((8, 288, 128), BF16),
            vmem((5, 4, 144, 128), BF16), vmem((5, 144, 128), F32),
            vmem((5, 144, 128), F32), vmem((576, 128), BF16),
            dma((3,)), dma((16,)), dma((3,)), dma((16,)), pltpu.SemaphoreType.REGULAR((3,)),
            dma((5,)), dma((5,)), dma((5, 4)), dma((5, 4)), dma((5, 4)), dma((5, 4)),
            dma((4,)), dma((4,)), dma((2, 4)), dma((2, 4)), dma((4,)), dma((4,)), dma((4, 2)), dma((2, 4)),
            dma((4, 3)), dma((4, 3)), dma((2,)), dma((2,)), dma((2, 7)), dma((2, 7)), dma((2,)), dma((2,)),
            dma((2, 3)), dma((2, 3)),
            dma((4,)), dma((4,)), dma((5, 4)), dma((5, 4)), dma((5,)), dma((5,)), dma((4,)), dma((4,)),
        ],
        compiler_params=pltpu.CompilerParams(
            collective_id=0, has_side_effects=True, vmem_limit_bytes=64 * 2**20 - 2**16
        ),
    )(
        jnp.transpose(queries, (1, 2, 0)), latent_kv.T, positions.reshape(1, 128), value_up, cotangent
    )
    attn, gq, gl, gv = pl.pallas_call(
        handed_on,
        out_shape=tuple(jax.ShapeDtypeStruct(x.shape, x.dtype) for x in (attn, gq, gl, gv)),
        in_specs=[pl.BlockSpec(memory_space=pltpu.VMEM)] * 4,
        out_specs=(anywhere,) * 4,
        scratch_shapes=[dma((4,))],
    )(attn, gq, gl, gv)
    return attn, jnp.transpose(gq, (2, 0, 1)), gl.T, gv.reshape(8, 16, 128)


def solution(mesh):
    in_specs = (
        P("ctx", "head", None),
        P("ctx", None),
        P("ctx"),
        P(None, "head", None),
        P("ctx", "head", None),
    )
    out_specs = (
        P("ctx", "head", None),
        P("ctx", "head", None),
        P("ctx", None),
        P("ctx", "head", None),
    )
    return jax.shard_map(body, mesh=mesh, in_specs=in_specs, out_specs=out_specs, check_vma=False)
```
